32 devices in a mesh: dp: 8 (over z, y), group: 4 (over x, core).
Axes of the slice: x: 2, y: 2, z: 4, core: 2. Of those that a mesh axis runs over, the one named last changes fastest.
Arguments:
- frames: bfloat16 [4, 4608, 2048], P('group', 'dp'), may hold values from -6 to 6
- lengths: int32 [4, 24], P('group', 'dp'), may hold values from 24 to 192, as said below
- destination: int32 [4, 24], P('group', 'dp'), may hold values from 0 to 7, as said below
- offsets: int32 [4, 24], P('group', 'dp'), may hold values from 0 to 360, as said below
- norm_gain: bfloat16 [2048], P(('dp', 'group')), may hold values from 0.099609375 to 1.8984375
- weight_in: bfloat16 [2048, 4096], P(('dp', 'group')), may hold values from -0.125 to 0.125
- depth_kernel: bfloat16 [2048, 32], P(('dp', 'group')), may hold values from -1 to 1
- post_gain: bfloat16 [2048], P(('dp', 'group')), may hold values from 0.099609375 to 1.8984375
- weight_out: bfloat16 [2048, 2048], P(('dp', 'group')), may hold values from -0.125 to 0.125
Outputs:
- mixed: bfloat16 [4, 3072, 2048], P('group', 'dp')
The draws below stay inside these ranges and needn't reach their ends.
Inputs may be any that keep to these rules, and one draw needn't show every extreme that they name: `destination`: every device of a group sends exactly one utterance to itself, one to dp index + 1 and one to dp index - 1, both taken modulo 8, within its own group index. `lengths`: every device receives utterances with 384 frames in all; one utterance of each device's receipts has exactly 192 frames; in every group some device's slots are full. `offsets`: the utterances that one device receives lie back to back without gaps or intersection over its 384 rows.
All inputs are finite; a program needn't handle non-finite values.
Results may differ from the reference program's by a relative error of at most 0.0085.
Values may be sent and summed in bfloat16 or wider, within the bound.
No kernel may reach another device: no remote copies, remote signals or barrier semaphores. Data moves between devices by JAX's collectives and lax.ppermute only.
A program may use at most 128 MiB of HBM per device.

```python
import jax
import jax.numpy as jnp
from jax import lax

D = 2048
KERNEL = 32
MAXLEN = 192
UTT_DEV = 3
LMIN = 24
RCV_DEV = 384
FR_DEV = 576
RCV_ALL = 3072
FR_ALL = 4608
UTT_ALL = 24
N_DP = 8
N_GROUP = 4


def layout(key):
    base = jax.random.fold_in(key, 17)
    key_full, key_split, key_long, key_order, key_slot = jax.random.split(base, 5)
    full_device = jax.random.randint(key_full, (N_GROUP, 1), 0, N_DP)
    first_len = jax.random.randint(key_split, (N_GROUP, N_DP), LMIN, MAXLEN - LMIN + 1)
    second_len = MAXLEN - first_len
    long_rel = jax.random.randint(key_long, (N_GROUP, N_DP), 0, 3)
    receiver = jnp.arange(N_DP, dtype=jnp.int32)[None, :]
    distance = (receiver - full_device) % N_DP
    forced = jnp.where(distance == 0, 1, jnp.where(distance == 1, 2, jnp.where(distance == N_DP - 1, 0, long_rel)))
    rel_index = jnp.arange(3, dtype=jnp.int32)[None, None, :]
    other_rank = (rel_index - forced[..., None]) % 3
    per_dest_len = jnp.where(other_rank == 0, MAXLEN, jnp.where(other_rank == 1, first_len[..., None], second_len[..., None]))
    rotate = jax.random.randint(key_order, (N_GROUP, N_DP, 1), 0, 3)
    placed = (rel_index + rotate) % 3
    earlier = (placed[..., None, :] < placed[..., :, None]).astype(jnp.int32)
    per_dest_off = jnp.sum(per_dest_len[..., None, :] * earlier, axis=-1)
    src_len = jnp.stack([jnp.roll(per_dest_len[:, :, index], -(index - 1), axis=1) for index in range(3)], axis=2)
    src_off = jnp.stack([jnp.roll(per_dest_off[:, :, index], -(index - 1), axis=1) for index in range(3)], axis=2)
    sources = jnp.arange(N_DP, dtype=jnp.int32)[None, :, None]
    src_dest = jnp.broadcast_to((sources + rel_index - 1) % N_DP, (N_GROUP, N_DP, 3))
    slot_turn = jax.random.randint(key_slot, (N_GROUP, N_DP, 1), 0, 3)
    order = (jnp.arange(3, dtype=jnp.int32)[None, None, :] + slot_turn) % 3
    lengths_out = jnp.take_along_axis(src_len, order, axis=2).reshape(N_GROUP, N_DP * 3)
    dest_out = jnp.take_along_axis(src_dest, order, axis=2).reshape(N_GROUP, N_DP * 3)
    offsets_out = jnp.take_along_axis(src_off, order, axis=2).reshape(N_GROUP, N_DP * 3)
    return (lengths_out.astype(jnp.int32), dest_out.astype(jnp.int32), offsets_out.astype(jnp.int32))


def draw_lengths(key, part):
    return layout(key)[0]


def draw_destination(key, part):
    return layout(key)[1]


def draw_offsets(key, part):
    return layout(key)[2]


def block_scale(rng, dims, shards, least, top_value):
    def one(dim, shards_of):
        heights = jax.random.uniform(jax.random.fold_in(jax.random.fold_in(rng, 6), dim), (shards_of,), jnp.float32, least / len(shards), top_value / len(shards))
        return jnp.repeat(jnp.exp(heights), dims[dim] // shards_of).reshape((-1,) + (1,) * (len(dims) - dim - 1))

    gain = one(*shards[0])
    for cut in shards[1:]:
        gain = gain * one(*cut)
    return gain


def noise(key, shape, scale, limit, cuts=(), held_as=jnp.bfloat16):
    entries = jax.random.normal(key, shape, jnp.float32) * scale
    if len(cuts) > 0:
        entries = block_scale(key, shape, cuts, -0.22, 0.18) * entries
    return jnp.clip(entries, min=-limit, max=limit).astype(held_as)


def setup_inputs(seed: int = 0) -> dict:
    keys = jax.random.split(jax.random.key(seed), 10)
    frames = noise(keys[0], (N_GROUP, FR_ALL, D), 1.0, 6.0, ((0, 4), (1, 8)))
    lengths = draw_lengths(jax.random.fold_in(keys[9], 71), 0)
    destination = draw_destination(jax.random.fold_in(keys[9], 71), 0)
    offsets = draw_offsets(jax.random.fold_in(keys[9], 71), 0)
    norm_gain = jnp.clip(1.0 + 0.18 * jax.random.normal(keys[4], (D,), jnp.float32), 0.099609375, 1.8984375).astype(jnp.bfloat16)
    weight_in = noise(keys[5], (D, 2 * D), D ** -0.5, 0.125, ((0, 32),))
    depth_kernel = noise(keys[6], (D, KERNEL), KERNEL ** -0.5, 1.0, ((0, 32),))
    post_gain = jnp.clip(1.0 + 0.18 * jax.random.normal(keys[7], (D,), jnp.float32), 0.099609375, 1.8984375).astype(jnp.bfloat16)
    weight_out = noise(keys[8], (D, D), D ** -0.5, 0.125, ((0, 32),))
    return {"frames": frames, "lengths": lengths, "destination": destination, "offsets": offsets, "norm_gain": norm_gain, "weight_in": weight_in, "depth_kernel": depth_kernel, "post_gain": post_gain, "weight_out": weight_out}


epsilon = 1e-05

def layer_norm(values, scale_gain):
    center = values - lax.optimization_barrier(jnp.mean(values, axis=-1, keepdims=True))
    spread = lax.optimization_barrier(jnp.mean(center * center, axis=-1, keepdims=True))
    return center * lax.rsqrt(spread + epsilon) * scale_gain.astype(jnp.float32)

def conv_module(inputs, segment, norm_gain, weight_in, depth_kernel, post_gain, weight_out):
    row_count = inputs.shape[0]
    widths = inputs.shape[1]
    source = inputs.astype(jnp.float32)
    normed = layer_norm(source, norm_gain).astype(jnp.bfloat16)
    projected = jnp.dot(normed, weight_in, preferred_element_type=jnp.float32)
    gated_rows = projected[:, :widths] * jax.nn.sigmoid(projected[:, widths:])
    margin = KERNEL // 2
    padded = jnp.pad(gated_rows, ((margin, margin), (0, 0)))
    labels = jnp.pad(segment, (margin, margin), constant_values=-1)
    kernel_rows = depth_kernel.astype(jnp.float32)
    depthwise = jnp.zeros_like(gated_rows)
    for column in range(KERNEL):
        inside = (labels[column:column + row_count] == segment)[:, None]
        depthwise = depthwise + jnp.where(inside, padded[column:column + row_count], 0.0) * kernel_rows[:, column]
    normed_post = layer_norm(depthwise, post_gain)
    active = (normed_post * jax.nn.sigmoid(normed_post)).astype(jnp.bfloat16)
    return (source + jnp.dot(active, weight_out, preferred_element_type=jnp.float32)).astype(jnp.bfloat16)

def rebalance_map(lengths, destination, offsets):
    lengths = lengths.astype(jnp.int32)
    destination = destination.astype(jnp.int32)
    offsets = offsets.astype(jnp.int32)
    per_source = lengths.reshape(-1, UTT_DEV)
    starts = (jnp.cumsum(per_source, axis=1).astype(jnp.int32) - per_source).reshape(-1)
    sender = jnp.arange(UTT_ALL, dtype=jnp.int32) // UTT_DEV
    frame_step = jnp.arange(MAXLEN, dtype=jnp.int32)
    valid_rows = frame_step[None, :] < lengths[:, None]
    target = jnp.where(valid_rows, destination[:, None] * RCV_DEV + offsets[:, None] + frame_step[None, :], RCV_ALL)
    anchor = sender[:, None] * FR_DEV + starts[:, None] + frame_step[None, :]
    names = jnp.broadcast_to(jnp.arange(UTT_ALL, dtype=jnp.int32)[:, None] + 1, target.shape)
    pick_rows = jnp.zeros((RCV_ALL,), jnp.int32).at[target.reshape(-1)].set(anchor.reshape(-1).astype(jnp.int32), mode='drop')
    labels = jnp.zeros((RCV_ALL,), jnp.int32).at[target.reshape(-1)].set(names.reshape(-1), mode='drop')
    return (pick_rows, labels)

def reference(frames, lengths, destination, offsets, norm_gain, weight_in, depth_kernel, post_gain, weight_out):

    def one_group(items):
        group_frames, group_lengths, group_dest, group_offsets = items
        pick_rows, labels = rebalance_map(group_lengths, group_dest, group_offsets)
        balanced = group_frames[pick_rows]
        return conv_module(balanced, labels, norm_gain, weight_in, depth_kernel, post_gain, weight_out)
    return lax.map(one_group, (frames, lengths, destination, offsets))
```

```python
import functools

import jax
import jax.numpy as jnp
from jax import lax
from jax.experimental import pallas as pl
from jax.experimental.pallas import tpu as pltpu
from jax.sharding import PartitionSpec as P

D = 2048
KERNEL = 32
MAXLEN = 192
RCV_DEV = 384


epsilon = 1e-05


def shifted(array, axis, by):
    peers = lax.axis_size(axis)
    return lax.ppermute(array, axis, [(i, (i + by) % peers) for i in range(peers)])


def layer_norm(values, scale_gain):
    center = values - jnp.mean(values, axis=-1, keepdims=True)
    spread = jnp.mean(center * center, axis=-1, keepdims=True)
    return center * lax.rsqrt(spread + epsilon) * scale_gain.astype(jnp.float32)


def depth_pass(gated_rows, segment, depth_kernel):
    row_count = gated_rows.shape[0]
    margin = KERNEL // 2
    padded = jnp.pad(gated_rows, ((margin, margin), (0, 0)))
    labels = jnp.pad(segment, (margin, margin), constant_values=-1)
    kernel_rows = depth_kernel.astype(jnp.float32)
    depthwise = jnp.zeros_like(gated_rows)
    for column in range(KERNEL):
        inside = (labels[column : column + row_count] == segment)[:, None]
        depthwise = (
            depthwise
            + jnp.where(inside, padded[column : column + row_count], 0.0) * kernel_rows[:, column]
        )
    return depthwise


def conv_module(inputs, segment, params):
    norm_gain, weight_in, depth_kernel, post_gain, weight_out = params
    widths = inputs.shape[1]
    source = inputs.astype(jnp.float32)
    normed = layer_norm(source, norm_gain).astype(jnp.bfloat16)
    projected = jnp.dot(normed, weight_in, preferred_element_type=jnp.float32)
    gated_rows = projected[:, :widths] * jax.nn.sigmoid(projected[:, widths:])
    depthwise = depth_pass(gated_rows, segment, depth_kernel)
    normed_post = layer_norm(depthwise, post_gain)
    active = (normed_post * jax.nn.sigmoid(normed_post)).astype(jnp.bfloat16)
    return (source + jnp.dot(active, weight_out, preferred_element_type=jnp.float32)).astype(
        jnp.bfloat16
    )


def relocate(own_part, next_part, prev_part):
    from_prev = shifted((next_part[0], next_part[1]), "dp", 1)
    from_next = shifted((prev_part[0], prev_part[1]), "dp", -1)
    received = jnp.zeros((RCV_DEV + MAXLEN, D), jnp.bfloat16)
    segment = jnp.zeros((RCV_DEV,), jnp.int32)
    position = jnp.arange(RCV_DEV, dtype=jnp.int32)
    arrivals = (own_part, from_prev, from_next)
    for label_id in range(3):
        frame_rows, meta_data = arrivals[label_id]
        current = lax.dynamic_slice_in_dim(received, meta_data[1], MAXLEN, 0)
        received = lax.dynamic_update_slice_in_dim(received, current + frame_rows, meta_data[1], 0)
        inside = (position >= meta_data[1]) & (position < meta_data[1] + meta_data[0])
        segment = jnp.where(inside, label_id + 1, segment)
    return (received[:RCV_DEV], segment)


def shards(
    frames, lengths, destination, offsets, norm_gain, weight_in, depth_kernel, post_gain, weight_out
):
    dp_count = lax.axis_size("dp")
    params = (
        lax.all_gather(norm_gain, ("dp", "group"), axis=0, tiled=True),
        lax.all_gather(weight_in, ("dp", "group"), axis=0, tiled=True),
        lax.all_gather(depth_kernel, ("dp", "group"), axis=0, tiled=True),
        lax.all_gather(post_gain, ("dp", "group"), axis=0, tiled=True),
        lax.all_gather(weight_out, ("dp", "group"), axis=0, tiled=True),
    )
    my_index = lax.axis_index("dp")
    local_frames = frames[0]
    lengths_here = lengths[0]
    dest_here = destination[0]
    offsets_here = offsets[0]
    starts = jnp.cumsum(lengths_here) - lengths_here
    relative = (dest_here - my_index) % dp_count
    slot_ids = jnp.arange(3, dtype=jnp.int32)

    def pick_entry(values, which):
        return jnp.sum(jnp.where(slot_ids == which, values, 0))

    def slot_of(code):
        return jnp.sum(jnp.where(relative == code, slot_ids, 0))

    chosen = (slot_of(0), slot_of(1), slot_of(dp_count - 1))

    def cut_utterance(source_rows, which):
        start_row = pick_entry(starts, which)
        live_count = pick_entry(lengths_here, which)
        frame_rows = lax.dynamic_slice_in_dim(source_rows, start_row, MAXLEN, 0)
        keep_rows = jnp.arange(MAXLEN, dtype=jnp.int32) < live_count
        kept = jnp.where(keep_rows[:, None], frame_rows, jnp.zeros_like(frame_rows))
        return (kept, jnp.stack([live_count, pick_entry(offsets_here, which)]))

    received, segment = relocate(
        cut_utterance(local_frames, chosen[0]),
        cut_utterance(local_frames, chosen[1]),
        cut_utterance(local_frames, chosen[2]),
    )
    mixed = conv_module(received, segment, params)
    return mixed[None]


SWAP = ((0, 1), (1, 0))
HOPS = {
    "c": ("core", SWAP),
    "x": ("x", SWAP),
    "y": ("y", SWAP),
    "z1": ("z", tuple((i, i ^ 1) for i in range(4))),
    "z2": ("z", tuple((i, i ^ 2) for i in range(4))),
}
GAP = KERNEL // 2
PAD = RCV_DEV + 4 * GAP
PAIR = 2 * PAD
LANE = 128
BLOCKS = D // LANE
HALF = D // 2
CHUNK = 256
SMALL = 48
META = 16
ROWS = 224
TILE = 64


def hop(array, name):
    axis, pairs = HOPS[name]
    return lax.ppermute(array, axis, pairs)


def turn(array, by):
    return lax.ppermute(array, ("z", "y"), [(i, (i + by) % 8) for i in range(8)])


def stack(first, second):
    return jnp.concatenate([first, second], 0)


def beside(*parts):
    return jnp.concatenate(parts, 1)


def tie(*arrays):
    return list(lax.optimization_barrier(arrays))


def lanes(index):
    return pl.ds(pl.multiple_of(index * LANE, LANE), LANE)


def prep_kernel(where, rows_ref, small_ref, first_ref, second_ref):
    def one(step, carry):
        at = pl.ds(pl.multiple_of(step * LANE, LANE), LANE)
        values = rows_ref[at, :].astype(jnp.float32)
        center = values - jnp.mean(values, axis=-1, keepdims=True)
        spread = jnp.mean(center * center, axis=-1, keepdims=True)
        scaled = center * lax.rsqrt(spread + epsilon)
        for block in range(BLOCKS):
            gain = small_ref[KERNEL : KERNEL + 1, lanes(where[0, block])]
            part = scaled[:, block * LANE : (block + 1) * LANE] * gain
            part = part.astype(jnp.bfloat16)
            first_ref[at, lanes(where[0, block])] = part
            second_ref[at, lanes(where[1, block])] = part
        return carry

    lax.fori_loop(0, PAIR // LANE, one, 0)


def prep(where, rows, small):
    out = jax.ShapeDtypeStruct((PAIR, D), jnp.bfloat16)
    vmem = pl.BlockSpec(memory_space=pltpu.VMEM)
    return pl.pallas_call(
        prep_kernel,
        out_shape=(out, out),
        in_specs=[pl.BlockSpec(memory_space=pltpu.SMEM), vmem, vmem],
        out_specs=(vmem, vmem),
        compiler_params=pltpu.CompilerParams(vmem_limit_bytes=32 * 2**20),
        cost_estimate=pl.CostEstimate(
            flops=20 * PAIR * D, bytes_accessed=6 * PAIR * D, transcendentals=PAIR
        ),
        name="prep",
    )(where, rows, small)


def conv_kernel(sub, where, rows_ref, near_ref, far_ref, small_ref, own_ref, other_ref, gated, taps):
    tiles = CHUNK // LANE
    half = where[4, 0]
    for tile in range(tiles):
        gated[tile, 0:GAP, :] = jnp.zeros((GAP, LANE), jnp.float32)
        gated[tile, GAP + PAIR : 2 * GAP + PAIR, :] = jnp.zeros((GAP, LANE), jnp.float32)
        taps[tile] = small_ref[0:KERNEL, lanes(where[0, half * (BLOCKS // 2) + sub + tile])]

    def project(step, carry):
        at = pl.ds(pl.multiple_of(step * ROWS, ROWS), ROWS)
        near, far = rows_ref[at, 0:HALF], rows_ref[at, HALF:D]

        def columns(low):
            span = slice(low, low + CHUNK)
            return jnp.dot(
                near, near_ref[:, span], preferred_element_type=jnp.float32
            ) + jnp.dot(far, far_ref[:, span], preferred_element_type=jnp.float32)

        mixed = columns(0) * jax.nn.sigmoid(columns(CHUNK))
        at = pl.ds(pl.multiple_of(step * ROWS + GAP, GAP), ROWS)
        for tile in range(tiles):
            gated[tile, at, :] = mixed[:, tile * LANE : (tile + 1) * LANE]
        return carry

    lax.fori_loop(0, PAIR // ROWS, project, 0)

    def slide(out_ref, base):
        def one(step, carry):
            for tile in range(tiles):
                total = jnp.zeros((TILE, LANE), jnp.float32)
                for tap in range(KERNEL):
                    window = gated[tile, pl.ds(base + step * TILE + tap, TILE), :]
                    total = total + window * taps[tile, tap : tap + 1, :]
                at = pl.ds(pl.multiple_of(step * TILE, TILE), TILE)
                out_ref[at, tile * LANE : (tile + 1) * LANE] = total.astype(jnp.bfloat16)
            return carry

        lax.fori_loop(0, PAD // TILE, one, 0)

    slide(own_ref, 0)
    slide(other_ref, PAD)


def conv(sub, where, rows, near, far, small):
    out = jax.ShapeDtypeStruct((PAD, CHUNK), jnp.bfloat16)
    vmem = pl.BlockSpec(memory_space=pltpu.VMEM)
    return pl.pallas_call(
        functools.partial(conv_kernel, sub),
        out_shape=(out, out),
        in_specs=[pl.BlockSpec(memory_space=pltpu.SMEM)] + [vmem] * 4,
        out_specs=(vmem, vmem),
        scratch_shapes=[
            pltpu.VMEM((CHUNK // LANE, PAIR + 2 * GAP, LANE), jnp.float32),
            pltpu.VMEM((CHUNK // LANE, KERNEL, LANE), jnp.float32),
        ],
        compiler_params=pltpu.CompilerParams(vmem_limit_bytes=32 * 2**20),
        cost_estimate=pl.CostEstimate(
            flops=4 * PAIR * D * CHUNK, bytes_accessed=8 * 2**20, transcendentals=PAIR * CHUNK
        ),
        name="conv",
    )(where, rows, near, far, small)


def finish_kernel(
    where, m0, m1, m2, m3, o0, o1, o2, o3, small_ref, pick_ref, base_ref,
    e8, er, d8, dr, f8, fr, g8, gr, out_ref, first, second,
):
    half = where[4, 0]
    count = KERNEL + 1
    pieces = [(half, (m0, m1, m2, m3)), (1 - half, (o0, o1, o2, o3))]
    refs = [ref for _, group in pieces for ref in group]
    total = jnp.zeros((PAD, 1), jnp.float32)
    for ref in refs:
        total = total + jnp.sum(ref[...].astype(jnp.float32), axis=-1, keepdims=True)
    mean = total / D
    total = jnp.zeros((PAD, 1), jnp.float32)
    for ref in refs:
        center = ref[...].astype(jnp.float32) - mean
        total = total + jnp.sum(center * center, axis=-1, keepdims=True)
    scale = lax.rsqrt(total / D + epsilon)
    for side, group in pieces:
        for place, ref in enumerate(group):
            parts = []
            for tile in range(CHUNK // LANE):
                block = side * (BLOCKS // 2) + place * (CHUNK // LANE) + tile
                gain = small_ref[count : count + 1, lanes(where[0, block])]
                values = ref[:, tile * LANE : (tile + 1) * LANE].astype(jnp.float32)
                post = (values - mean) * scale * gain
                parts.append((post * jax.nn.sigmoid(post)).astype(jnp.bfloat16))
            kept = jnp.dot(
                pick_ref[...], beside(*parts), preferred_element_type=jnp.float32
            ).astype(jnp.bfloat16)
            for tile in range(CHUNK // LANE):
                block = side * (BLOCKS // 2) + place * (CHUNK // LANE) + tile
                part = kept[:, tile * LANE : (tile + 1) * LANE]
                first[:, lanes(where[2, block])] = part
                second[:, lanes(where[3, block])] = part
    width = HALF // 2
    for side, active, near, far, low in (
        (half, first, e8, er, 0),
        (half, second, d8, dr, width),
        (1 - half, first, f8, fr, 0),
        (1 - half, second, g8, gr, width),
    ):
        at = pl.ds(pl.multiple_of(side * HALF + low, width), width)
        result = (
            jnp.dot(active[:, 0:HALF], near[...], preferred_element_type=jnp.float32)
            + jnp.dot(active[:, HALF:D], far[...], preferred_element_type=jnp.float32)
            + base_ref[:, at].astype(jnp.float32)
        )
        out_ref[:, at] = result.astype(jnp.bfloat16)


def finish(where, mine, others, small, pick, base, weights):
    vmem = pl.BlockSpec(memory_space=pltpu.VMEM)
    return pl.pallas_call(
        finish_kernel,
        out_shape=jax.ShapeDtypeStruct((RCV_DEV, D), jnp.bfloat16),
        in_specs=[pl.BlockSpec(memory_space=pltpu.SMEM)] + [vmem] * 19,
        out_specs=vmem,
        scratch_shapes=[pltpu.VMEM((RCV_DEV, D), jnp.bfloat16)] * 2,
        compiler_params=pltpu.CompilerParams(vmem_limit_bytes=48 * 2**20),
        cost_estimate=pl.CostEstimate(
            flops=2 * RCV_DEV * D * D, bytes_accessed=16 * 2**20, transcendentals=PAD * D
        ),
        name="finish",
    )(where, *mine, *others, small, pick, base, *weights)


def hot(condition):
    return condition.astype(jnp.bfloat16)


def take(picker, rows):
    return jnp.dot(picker, rows, preferred_element_type=jnp.float32)


def hyper_shards(
    frames, lengths, destination, offsets, norm_gain, weight_in, depth_kernel, post_gain, weight_out
):
    core, x, y, z = (lax.axis_index(name) for name in ("core", "x", "y", "z"))
    low = core == 0
    per = weight_in.shape[0]

    small = jnp.concatenate(
        [depth_kernel, norm_gain[:, None], post_gain[:, None], jnp.zeros((per, LANE - KERNEL - 2), jnp.bfloat16)], 1
    )
    left = [weight_in[:, 0:HALF], weight_in[:, D : D + HALF], weight_out[:, 0:HALF]]
    right = [weight_in[:, HALF:D], weight_in[:, D + HALF :], weight_out[:, HALF:]]
    left, right = beside(*left), beside(*right)
    kept = beside(jnp.where(low, left, right), small)
    given = beside(jnp.where(low, right, left), small)
    got = hop(given, "c")
    chip = jnp.where(low, stack(kept, got), stack(got, kept))

    def value_gate(start):
        return [chip[:, start : start + CHUNK], chip[:, HALF + start : HALF + start + CHUNK]]

    a = beside(*value_gate(0), *value_gate(CHUNK), chip[:, 3 * HALF :])
    b = beside(*value_gate(2 * CHUNK), *value_gate(3 * CHUNK))
    o = chip[:, 2 * HALF : 3 * HALF]

    rows, lens, dest, offs = frames[0], lengths[0], destination[0], offsets[0]
    starts = jnp.cumsum(lens) - lens
    relative = (dest - (z * 2 + y)) % 8

    def entry(values, code):
        return jnp.sum(jnp.where(relative == code, values, 0))

    def sent(code):
        count, offset, start = entry(lens, code), entry(offs, code), entry(starts, code)
        spot = jnp.arange(MAXLEN + META, dtype=jnp.int32)[:, None]
        slot = jnp.arange(rows.shape[0], dtype=jnp.int32)[None, :]
        picker = hot((slot == start + spot) & (spot < count))
        note = jnp.where(spot == MAXLEN, count, 0) + jnp.where(spot == MAXLEN + 1, offset // 2, 0)
        note = note + jnp.where(spot == MAXLEN + 2, offset % 2, 0)
        first = take(picker, rows[:, 0:HALF]) + note.astype(jnp.float32)
        second = take(picker[0:MAXLEN], rows[:, HALF:D])
        return first.astype(jnp.bfloat16), second.astype(jnp.bfloat16)

    up, down = sent(1), sent(7)
    prev_first, next_first = turn(up[0], 1), turn(down[0], -1)
    arrived = [hop(a, "z2"), hop(b, "z1"), hop(o, "x")]
    a, b, o, prev_first, next_first, up_second, down_second = tie(
        stack(a, arrived[0]), stack(b, arrived[1]), stack(o, arrived[2]),
        prev_first, next_first, up[1], down[1],
    )
    prev_second, next_second = turn(up_second, 1), turn(down_second, -1)
    arrived = [hop(a, "z1"), hop(b, "z2"), hop(o, "y")]
    a, b, o, prev_second, next_second = tie(
        stack(a, arrived[0]), stack(b, arrived[1]), stack(o, arrived[2]), prev_second, next_second
    )
    e, d = o[:, 0 : HALF // 2], o[:, HALF // 2 :]
    small = a[:, 4 * CHUNK :].T[0:SMALL]
    a = a[:, 0 : 4 * CHUNK]
    small = beside(small, hop(small, "y"))
    arrived = [hop(a, "y"), hop(b, "x"), hop(e, "z1"), hop(d, "z2")]
    a, b, e, d, small = tie(
        stack(a, arrived[0]), stack(b, arrived[1]), stack(e, arrived[2]), stack(d, arrived[3]), small
    )
    small = beside(small, hop(small, "x")).astype(jnp.float32)
    e_far, d_far = hop(e, "z2"), hop(d, "z1")
    cut = 2 * CHUNK
    a1, a2, b1, b2 = a[:, 0:cut], a[:, cut:], b[:, 0:cut], b[:, cut:]
    a1_far, b1_far = hop(a1, "x"), hop(b1, "y")
    a1_far, b1_far, a2, b2 = tie(a1_far, b1_far, a2, b2)
    a2_far, b2_far = hop(a2, "x"), hop(b2, "y")

    def noted(first):
        head = first[MAXLEN : MAXLEN + 3, 0].astype(jnp.int32)
        return head[0], head[1] * 2 + head[2]

    own = (entry(lens, 0), entry(offs, 0))
    parts = [own, noted(prev_first), noted(next_first)]
    order = [sum((other[1] < part[1]).astype(jnp.int32) for other in parts) for part in parts]
    padded = jnp.arange(PAD, dtype=jnp.int32)[:, None]

    def placer(part, rank, width, start):
        source = jnp.arange(width, dtype=jnp.int32)[None, :] - start
        inside = (source >= 0) & (source < part[0])
        return hot((padded == GAP + part[1] + GAP * rank + source) & inside)

    place_own = placer(parts[0], order[0], rows.shape[0], entry(starts, 0))
    place_prev = placer(parts[1], order[1], MAXLEN + META, 0)
    place_next = placer(parts[2], order[2], MAXLEN + META, 0)
    first = take(place_own, rows[:, 0:HALF]) + take(place_prev, prev_first) + take(place_next, next_first)
    second = (
        take(place_own, rows[:, HALF:D])
        + take(place_prev[:, 0:MAXLEN], prev_second)
        + take(place_next[:, 0:MAXLEN], next_second)
    )
    spread_rows = beside(first, second).astype(jnp.bfloat16)
    flat = jnp.arange(RCV_DEV, dtype=jnp.int32)[:, None]
    rank = sum((part[1] <= flat).astype(jnp.int32) for part in parts)
    pick = hot(jnp.arange(PAD, dtype=jnp.int32)[None, :] == flat + GAP * rank)
    base = take(pick, spread_rows).astype(jnp.bfloat16)

    block = jnp.arange(BLOCKS, dtype=jnp.int32)
    zb2, zb1 = (block >> 3) ^ (z >> 1), ((block >> 2) & 1) ^ (z & 1)
    yb, xb = ((block >> 1) & 1) ^ y, (block & 1) ^ x
    where = jnp.stack(
        [
            xb * 8 + yb * 4 + zb1 * 2 + zb2,
            yb * 8 + xb * 4 + zb2 * 2 + zb1,
            zb2 * 8 + zb1 * 4 + yb * 2 + xb,
            zb1 * 8 + zb2 * 4 + yb * 2 + xb,
            jnp.full_like(block, core),
        ]
    )

    both = stack(spread_rows, hop(spread_rows, "c"))
    for_a, for_b = prep(where, both, small)
    mine, others = [], []

    def run(sub, rows_in, near, far):
        kept_part, given_part = conv(sub, where, rows_in, near, far, small)
        mine.append(kept_part)
        others.append(hop(given_part, "c"))

    run(0, for_a, a1, a1_far)
    run(4, for_b, b1, b1_far)
    e, d, e_far, d_far, a2_far, b2_far = tie(e, d, e_far, d_far, a2_far, b2_far)
    weights = [e, e_far, d, d_far]
    weights = weights + [hop(array, "c") for array in weights]
    run(2, for_a, a2, a2_far)
    run(6, for_b, b2, b2_far)
    order = (0, 2, 1, 3)
    mixed = finish(
        where, [mine[i] for i in order], [others[i] for i in order], small, pick, base, weights
    )
    return mixed[None]


def solution(mesh):
    if dict(mesh.shape) == {"dp": 8, "group": 4}:
        grid = jax.sharding.Mesh(mesh.devices.reshape(4, 2, 2, 2), ("z", "y", "x", "core"))
        dp, group, body = ("z", "y"), ("x", "core"), hyper_shards
    else:
        grid, dp, group, body = mesh, ("dp",), ("group",), shards
    every = dp + group
    placed = (
        P(group, dp, None),
        P(group, dp),
        P(group, dp),
        P(group, dp),
        P(every),
        P(every, None),
        P(every, None),
        P(every),
        P(every, None),
    )
    return jax.shard_map(
        body, mesh=grid, in_specs=placed, out_specs=P(group, dp, None), check_vma=False
    )
```

```python
import functools

import jax
import jax.numpy as jnp
from jax import lax
from jax.experimental import pallas as pl
from jax.experimental.pallas import tpu as pltpu
from jax.sharding import PartitionSpec as P

D = 2048
KERNEL = 32
MAXLEN = 192
RCV_DEV = 384


epsilon = 1e-05


def shifted(array, axis, by):
    peers = lax.axis_size(axis)
    return lax.ppermute(array, axis, [(i, (i + by) % peers) for i in range(peers)])


def layer_norm(values, scale_gain):
    center = values - jnp.mean(values, axis=-1, keepdims=True)
    spread = jnp.mean(center * center, axis=-1, keepdims=True)
    return center * lax.rsqrt(spread + epsilon) * scale_gain.astype(jnp.float32)


def depth_pass(gated_rows, segment, depth_kernel):
    row_count = gated_rows.shape[0]
    margin = KERNEL // 2
    padded = jnp.pad(gated_rows, ((margin, margin), (0, 0)))
    labels = jnp.pad(segment, (margin, margin), constant_values=-1)
    kernel_rows = depth_kernel.astype(jnp.float32)
    depthwise = jnp.zeros_like(gated_rows)
    for column in range(KERNEL):
        inside = (labels[column : column + row_count] == segment)[:, None]
        depthwise = (
            depthwise
            + jnp.where(inside, padded[column : column + row_count], 0.0) * kernel_rows[:, column]
        )
    return depthwise


def conv_module(inputs, segment, params):
    norm_gain, weight_in, depth_kernel, post_gain, weight_out = params
    widths = inputs.shape[1]
    source = inputs.astype(jnp.float32)
    normed = layer_norm(source, norm_gain).astype(jnp.bfloat16)
    projected = jnp.dot(normed, weight_in, preferred_element_type=jnp.float32)
    gated_rows = projected[:, :widths] * jax.nn.sigmoid(projected[:, widths:])
    depthwise = depth_pass(gated_rows, segment, depth_kernel)
    normed_post = layer_norm(depthwise, post_gain)
    active = (normed_post * jax.nn.sigmoid(normed_post)).astype(jnp.bfloat16)
    return (source + jnp.dot(active, weight_out, preferred_element_type=jnp.float32)).astype(
        jnp.bfloat16
    )


def relocate(own_part, next_part, prev_part):
    from_prev = shifted((next_part[0], next_part[1]), "dp", 1)
    from_next = shifted((prev_part[0], prev_part[1]), "dp", -1)
    received = jnp.zeros((RCV_DEV + MAXLEN, D), jnp.bfloat16)
    segment = jnp.zeros((RCV_DEV,), jnp.int32)
    position = jnp.arange(RCV_DEV, dtype=jnp.int32)
    arrivals = (own_part, from_prev, from_next)
    for label_id in range(3):
        frame_rows, meta_data = arrivals[label_id]
        current = lax.dynamic_slice_in_dim(received, meta_data[1], MAXLEN, 0)
        received = lax.dynamic_update_slice_in_dim(received, current + frame_rows, meta_data[1], 0)
        inside = (position >= meta_data[1]) & (position < meta_data[1] + meta_data[0])
        segment = jnp.where(inside, label_id + 1, segment)
    return (received[:RCV_DEV], segment)


def shards(
    frames, lengths, destination, offsets, norm_gain, weight_in, depth_kernel, post_gain, weight_out
):
    dp_count = lax.axis_size("dp")
    params = (
        lax.all_gather(norm_gain, ("dp", "group"), axis=0, tiled=True),
        lax.all_gather(weight_in, ("dp", "group"), axis=0, tiled=True),
        lax.all_gather(depth_kernel, ("dp", "group"), axis=0, tiled=True),
        lax.all_gather(post_gain, ("dp", "group"), axis=0, tiled=True),
        lax.all_gather(weight_out, ("dp", "group"), axis=0, tiled=True),
    )
    my_index = lax.axis_index("dp")
    local_frames = frames[0]
    lengths_here = lengths[0]
    dest_here = destination[0]
    offsets_here = offsets[0]
    starts = jnp.cumsum(lengths_here) - lengths_here
    relative = (dest_here - my_index) % dp_count
    slot_ids = jnp.arange(3, dtype=jnp.int32)

    def pick_entry(values, which):
        return jnp.sum(jnp.where(slot_ids == which, values, 0))

    def slot_of(code):
        return jnp.sum(jnp.where(relative == code, slot_ids, 0))

    chosen = (slot_of(0), slot_of(1), slot_of(dp_count - 1))

    def cut_utterance(source_rows, which):
        start_row = pick_entry(starts, which)
        live_count = pick_entry(lengths_here, which)
        frame_rows = lax.dynamic_slice_in_dim(source_rows, start_row, MAXLEN, 0)
        keep_rows = jnp.arange(MAXLEN, dtype=jnp.int32) < live_count
        kept = jnp.where(keep_rows[:, None], frame_rows, jnp.zeros_like(frame_rows))
        return (kept, jnp.stack([live_count, pick_entry(offsets_here, which)]))

    received, segment = relocate(
        cut_utterance(local_frames, chosen[0]),
        cut_utterance(local_frames, chosen[1]),
        cut_utterance(local_frames, chosen[2]),
    )
    mixed = conv_module(received, segment, params)
    return mixed[None]


SWAP = ((0, 1), (1, 0))
HOPS = {
    "c": ("core", SWAP),
    "x": ("x", SWAP),
    "y": ("y", SWAP),
    "z1": ("z", tuple((i, i ^ 1) for i in range(4))),
    "z2": ("z", tuple((i, i ^ 2) for i in range(4))),
}
GAP = KERNEL // 2
PAD = RCV_DEV + 4 * GAP
PAIR = 2 * PAD
LANE = 128
BLOCKS = D // LANE
HALF = D // 2
CHUNK = 256
SMALL = 48
META = 16
ROWS = 224
TILE = 64


def hop(array, name):
    axis, pairs = HOPS[name]
    return lax.ppermute(array, axis, pairs)


def turn(array, by):
    return lax.ppermute(array, ("z", "y"), [(i, (i + by) % 8) for i in range(8)])


def stack(first, second):
    return jnp.concatenate([first, second], 0)


def beside(*parts):
    return jnp.concatenate(parts, 1)


def tie(*arrays):
    return list(lax.optimization_barrier(arrays))


def lanes(index):
    return pl.ds(pl.multiple_of(index * LANE, LANE), LANE)


def local(lens, dest, offs, where, code):
    count, offset, start, before = 0, 0, 0, 0
    for slot in range(3):
        match = (dest[0, slot] - where[4, 3] + 8) % 8 == code
        count = jnp.where(match, lens[0, slot], count)
        offset = jnp.where(match, offs[0, slot], offset)
        start = jnp.where(match, before, start)
        before = before + lens[0, slot]
    return count, offset, start


def hot(condition):
    return jnp.where(condition, 1.0, 0.0).astype(jnp.bfloat16)


def take(picker, rows):
    return jnp.dot(picker, rows, preferred_element_type=jnp.float32)


def grid_of(rows, columns):
    shape = (rows, columns)
    return lax.broadcasted_iota(jnp.int32, shape, 0), lax.broadcasted_iota(jnp.int32, shape, 1)


def cut_kernel(where, lens, dest, offs, rows_ref, up0, up1, down0, down1):
    for code, first_ref, second_ref in ((1, up0, up1), (7, down0, down1)):
        count, offset, start = local(lens, dest, offs, where, code)
        spot, slot = grid_of(MAXLEN + META, rows_ref.shape[0])
        picker = hot((slot == start + spot) & (spot < count))
        spot, _ = grid_of(MAXLEN + META, HALF)
        note = jnp.where(spot == MAXLEN, count, 0) + jnp.where(spot == MAXLEN + 1, offset // 2, 0)
        note = note + jnp.where(spot == MAXLEN + 2, offset % 2, 0)
        first = take(picker, rows_ref[:, 0:HALF]) + note.astype(jnp.float32)
        first_ref[...] = first.astype(jnp.bfloat16)
        second_ref[...] = take(picker[0:MAXLEN], rows_ref[:, HALF:D]).astype(jnp.bfloat16)


def smem(count):
    return [pl.BlockSpec(memory_space=pltpu.SMEM)] * count


def vmem(count):
    return [pl.BlockSpec(memory_space=pltpu.VMEM)] * count


def shape(rows, columns, dtype=jnp.bfloat16):
    return jax.ShapeDtypeStruct((rows, columns), dtype)


def limits(mebibytes):
    return pltpu.CompilerParams(vmem_limit_bytes=mebibytes * 2**20)


def cut(where, lens, dest, offs, rows):
    first, second = shape(MAXLEN + META, HALF), shape(MAXLEN, HALF)
    return pl.pallas_call(
        cut_kernel,
        out_shape=(first, second, first, second),
        in_specs=smem(4) + vmem(1),
        out_specs=tuple(vmem(4)),
        compiler_params=limits(16),
        cost_estimate=pl.CostEstimate(
            flops=4 * (MAXLEN + META) * rows.shape[0] * D, bytes_accessed=5 * 2**20, transcendentals=0
        ),
        name="cut",
    )(where, lens, dest, offs, rows)


def place_kernel(where, lens, dest, offs, rows_ref, p0, p1, n0, n1, spread_ref, base_ref, pick_ref):
    count, offset, start = local(lens, dest, offs, where, 0)
    ones = jnp.ones((1, 1), jnp.int32)

    def noted(ref):
        head = ref[MAXLEN : MAXLEN + META, 0:LANE].astype(jnp.float32).astype(jnp.int32)
        return head[0:1, 0:1], head[1:2, 0:1] * 2 + head[2:3, 0:1]

    parts = [(count * ones, offset * ones), noted(p0), noted(n0)]

    def placer(which, width, first):
        mine = parts[which]
        rank = sum((other[1] < mine[1]).astype(jnp.int32) for other in parts)
        spot, slot = grid_of(PAD, width)
        source = slot - first
        inside = (source >= 0) & (source < mine[0])
        return hot((spot == GAP + mine[1] + GAP * rank + source) & inside)

    from_own = placer(0, rows_ref.shape[0], start)
    from_prev = placer(1, MAXLEN + META, 0)
    from_next = placer(2, MAXLEN + META, 0)
    first = take(from_own, rows_ref[:, 0:HALF]) + take(from_prev, p0[...]) + take(from_next, n0[...])
    spread_ref[:, 0:HALF] = first.astype(jnp.bfloat16)
    second = (
        take(from_own, rows_ref[:, HALF:D])
        + take(from_prev[:, 0:MAXLEN], p1[...])
        + take(from_next[:, 0:MAXLEN], n1[...])
    )
    spread_ref[:, HALF:D] = second.astype(jnp.bfloat16)
    flat, spot = grid_of(RCV_DEV, PAD)
    rank = sum((part[1] <= flat).astype(jnp.int32) for part in parts)
    pick = hot(spot == flat + GAP * rank)
    pick_ref[...] = pick
    base_ref[...] = take(pick, spread_ref[...]).astype(jnp.bfloat16)


def place(where, lens, dest, offs, rows, arrived):
    return pl.pallas_call(
        place_kernel,
        out_shape=(shape(PAD, D), shape(RCV_DEV, D), shape(RCV_DEV, PAD)),
        in_specs=smem(4) + vmem(5),
        out_specs=tuple(vmem(3)),
        compiler_params=limits(24),
        cost_estimate=pl.CostEstimate(flops=4 * 2**30, bytes_accessed=10 * 2**20, transcendentals=0),
        name="place",
    )(where, lens, dest, offs, rows, *arrived)


def prep_kernel(where, mine_ref, other_ref, notes_ref, first_ref, second_ref, small_ref):
    for block in range(BLOCKS):
        at = pl.ds(pl.multiple_of(where[5, block] * META, META), META)
        for part in range(SMALL // META):
            tile = notes_ref[at, lanes(where[6, block] * (SMALL // META) + part)]
            small_ref[part * META : (part + 1) * META, block * LANE : (block + 1) * LANE] = tile.astype(
                jnp.float32
            )
    for base, rows_ref in ((0, mine_ref), (PAD, other_ref)):

        def one(step, carry):
            values = rows_ref[pl.ds(pl.multiple_of(step * TILE, TILE), TILE), :].astype(jnp.float32)
            center = values - jnp.mean(values, axis=-1, keepdims=True)
            spread = jnp.mean(center * center, axis=-1, keepdims=True)
            scaled = center * lax.rsqrt(spread + epsilon) * small_ref[KERNEL : KERNEL + 1, :]
            scaled = scaled.astype(jnp.bfloat16)
            at = pl.ds(pl.multiple_of(base + step * TILE, TILE), TILE)
            for block in range(BLOCKS):
                part = scaled[:, block * LANE : (block + 1) * LANE]
                first_ref[at, lanes(where[0, block])] = part
                second_ref[at, lanes(where[1, block])] = part
            return carry

        lax.fori_loop(0, PAD // TILE, one, 0)


def prep(where, mine, other, notes):
    return pl.pallas_call(
        prep_kernel,
        out_shape=(shape(PAIR, D), shape(PAIR, D), shape(SMALL, D, jnp.float32)),
        in_specs=smem(1) + vmem(3),
        out_specs=tuple(vmem(3)),
        compiler_params=limits(20),
        cost_estimate=pl.CostEstimate(
            flops=20 * PAIR * D, bytes_accessed=6 * PAIR * D, transcendentals=PAIR
        ),
        name="prep",
    )(where, mine, other, notes)


def conv_kernel(sub, where, rows_ref, near_ref, far_ref, small_ref, own_ref, other_ref, gated, taps):
    tiles = CHUNK // LANE
    half = where[4, 0]
    for tile in range(tiles):
        gated[tile, 0:GAP, :] = jnp.zeros((GAP, LANE), jnp.float32)
        gated[tile, GAP + PAIR : 2 * GAP + PAIR, :] = jnp.zeros((GAP, LANE), jnp.float32)
        taps[tile] = small_ref[0:KERNEL, lanes(half * (BLOCKS // 2) + sub + tile)]

    def project(step, carry):
        at = pl.ds(pl.multiple_of(step * ROWS, ROWS), ROWS)
        near, far = rows_ref[at, 0:HALF], rows_ref[at, HALF:D]

        def columns(low):
            span = slice(low, low + CHUNK)
            return jnp.dot(
                near, near_ref[:, span], preferred_element_type=jnp.float32
            ) + jnp.dot(far, far_ref[:, span], preferred_element_type=jnp.float32)

        mixed = columns(0) * jax.nn.sigmoid(columns(CHUNK))
        at = pl.ds(pl.multiple_of(step * ROWS + GAP, GAP), ROWS)
        for tile in range(tiles):
            gated[tile, at, :] = mixed[:, tile * LANE : (tile + 1) * LANE]
        return carry

    lax.fori_loop(0, PAIR // ROWS, project, 0)

    def slide(out_ref, base):
        def one(step, carry):
            for tile in range(tiles):
                total = jnp.zeros((TILE, LANE), jnp.float32)
                for tap in range(KERNEL):
                    window = gated[tile, pl.ds(base + step * TILE + tap, TILE), :]
                    total = total + window * taps[tile, tap : tap + 1, :]
                at = pl.ds(pl.multiple_of(step * TILE, TILE), TILE)
                out_ref[at, tile * LANE : (tile + 1) * LANE] = total.astype(jnp.bfloat16)
            return carry

        lax.fori_loop(0, PAD // TILE, one, 0)

    slide(own_ref, 0)
    slide(other_ref, PAD)


def conv(sub, where, rows, near, far, small):
    out = shape(PAD, CHUNK)
    return pl.pallas_call(
        functools.partial(conv_kernel, sub),
        out_shape=(out, out),
        in_specs=smem(1) + vmem(4),
        out_specs=tuple(vmem(2)),
        scratch_shapes=[
            pltpu.VMEM((CHUNK // LANE, PAIR + 2 * GAP, LANE), jnp.float32),
            pltpu.VMEM((CHUNK // LANE, KERNEL, LANE), jnp.float32),
        ],
        compiler_params=limits(16),
        cost_estimate=pl.CostEstimate(
            flops=4 * PAIR * D * CHUNK, bytes_accessed=8 * 2**20, transcendentals=PAIR * CHUNK
        ),
        name="conv",
    )(where, rows, near, far, small)


def finish_kernel(
    where, m0, m1, m2, m3, o0, o1, o2, o3, small_ref, pick_ref, base_ref,
    e8, er, d8, dr, f8, fr, g8, gr, out_ref, first, second,
):
    half = where[4, 0]
    count = KERNEL + 1
    pieces = [(half, (m0, m1, m2, m3)), (1 - half, (o0, o1, o2, o3))]
    refs = [ref for _, group in pieces for ref in group]
    total = jnp.zeros((PAD, 1), jnp.float32)
    for ref in refs:
        total = total + jnp.sum(ref[...].astype(jnp.float32), axis=-1, keepdims=True)
    mean = total / D
    total = jnp.zeros((PAD, 1), jnp.float32)
    for ref in refs:
        center = ref[...].astype(jnp.float32) - mean
        total = total + jnp.sum(center * center, axis=-1, keepdims=True)
    scale = lax.rsqrt(total / D + epsilon)
    for side, group in pieces:
        for place, ref in enumerate(group):
            parts = []
            for tile in range(CHUNK // LANE):
                block = side * (BLOCKS // 2) + place * (CHUNK // LANE) + tile
                gain = small_ref[count : count + 1, lanes(block)]
                values = ref[:, tile * LANE : (tile + 1) * LANE].astype(jnp.float32)
                post = (values - mean) * scale * gain
                parts.append((post * jax.nn.sigmoid(post)).astype(jnp.bfloat16))
            kept = jnp.dot(
                pick_ref[...], beside(*parts), preferred_element_type=jnp.float32
            ).astype(jnp.bfloat16)
            for tile in range(CHUNK // LANE):
                block = side * (BLOCKS // 2) + place * (CHUNK // LANE) + tile
                part = kept[:, tile * LANE : (tile + 1) * LANE]
                first[:, lanes(where[2, block])] = part
                second[:, lanes(where[3, block])] = part
    width = HALF // 2
    for side, active, near, far, low in (
        (half, first, e8, er, 0),
        (half, second, d8, dr, width),
        (1 - half, first, f8, fr, 0),
        (1 - half, second, g8, gr, width),
    ):
        at = pl.ds(pl.multiple_of(side * HALF + low, width), width)
        result = (
            jnp.dot(active[:, 0:HALF], near[...], preferred_element_type=jnp.float32)
            + jnp.dot(active[:, HALF:D], far[...], preferred_element_type=jnp.float32)
            + base_ref[:, at].astype(jnp.float32)
        )
        out_ref[:, at] = result.astype(jnp.bfloat16)


def finish(where, mine, others, small, pick, base, weights):
    return pl.pallas_call(
        finish_kernel,
        out_shape=shape(RCV_DEV, D),
        in_specs=smem(1) + vmem(19),
        out_specs=vmem(1)[0],
        scratch_shapes=[pltpu.VMEM((RCV_DEV, D), jnp.bfloat16)] * 2,
        compiler_params=limits(28),
        cost_estimate=pl.CostEstimate(
            flops=2 * RCV_DEV * D * D, bytes_accessed=16 * 2**20, transcendentals=PAD * D
        ),
        name="finish",
    )(where, *mine, *others, small, pick, base, *weights)


def hyper_shards(
    frames, lengths, destination, offsets, norm_gain, weight_in, depth_kernel, post_gain, weight_out
):
    core, x, y, z = (lax.axis_index(name) for name in ("core", "x", "y", "z"))
    low = core == 0
    per = weight_in.shape[0]

    block = jnp.arange(BLOCKS, dtype=jnp.int32)
    zb2, zb1 = (block >> 3) ^ (z >> 1), ((block >> 2) & 1) ^ (z & 1)
    yb, xb = ((block >> 1) & 1) ^ y, (block & 1) ^ x
    info = jnp.where(block == 3, z * 2 + y, core)
    where = jnp.stack(
        [
            xb * 8 + yb * 4 + zb1 * 2 + zb2,
            yb * 8 + xb * 4 + zb2 * 2 + zb1,
            zb2 * 8 + zb1 * 4 + yb * 2 + xb,
            zb1 * 8 + zb2 * 4 + yb * 2 + xb,
            info,
            yb * 4 + zb1 * 2 + zb2,
            xb,
        ]
    )

    left = beside(weight_in[:, 0:HALF], weight_in[:, D : D + HALF], weight_out[:, 0:HALF])
    right = beside(weight_in[:, HALF:D], weight_in[:, D + HALF :], weight_out[:, HALF:])
    kept, given = jnp.where(low, left, right), jnp.where(low, right, left)
    got = hop(given, "c")
    chip = jnp.where(low, stack(kept, got), stack(got, kept))

    notes = jnp.concatenate(
        [depth_kernel.T, norm_gain[None], post_gain[None], jnp.zeros((SMALL - KERNEL - 2, per), jnp.bfloat16)], 0
    )
    blank = jnp.zeros_like(notes)
    notes = jnp.where(low, beside(notes, blank), beside(blank, notes))
    notes = notes + hop(notes, "c")
    pair = [notes, hop(notes, "x")]
    tiles = [one[low_row : low_row + META] for one in pair for low_row in range(0, SMALL, META)]
    notes = beside(*tiles, jnp.zeros((META, 4 * CHUNK - 2 * LANE * SMALL // META), jnp.bfloat16))

    def value_gate(start):
        return [chip[:, start : start + CHUNK], chip[:, HALF + start : HALF + start + CHUNK]]

    a = beside(*value_gate(0), *value_gate(CHUNK))
    b = beside(*value_gate(2 * CHUNK), *value_gate(3 * CHUNK))
    o = chip[:, 2 * HALF : 3 * HALF]

    def grow(array, extra, name):
        size = array.shape[0]
        arrived = hop(stack(array, extra), name)
        return stack(array, arrived[0:size]), stack(extra, arrived[size:])

    rows = frames[0]
    up0, up1, down0, down1 = cut(where, lengths, destination, offsets, rows)
    prev0, next0 = turn(up0, 1), turn(down0, -1)
    (a, notes), b_far, o_far = grow(a, notes, "z2"), hop(b, "z1"), hop(o, "x")
    a, notes, b, o, prev0, next0, up1, down1 = tie(
        a, notes, stack(b, b_far), stack(o, o_far), prev0, next0, up1, down1
    )
    prev1, next1 = turn(up1, 1), turn(down1, -1)
    (a, notes), b_far, o_far = grow(a, notes, "z1"), hop(b, "z2"), hop(o, "y")
    a, notes, b, o, prev1, next1 = tie(a, notes, stack(b, b_far), stack(o, o_far), prev1, next1)
    e, d = o[:, 0 : HALF // 2], o[:, HALF // 2 :]
    spread, base, pick = place(
        where, lengths, destination, offsets, rows, (prev0, prev1, next0, next1)
    )
    spread_other = hop(spread, "c")
    (a, notes), b_far, e_far, d_far = grow(a, notes, "y"), hop(b, "x"), hop(e, "z1"), hop(d, "z2")
    a, notes, b, e, d, spread, spread_other, base, pick = tie(
        a, notes, stack(b, b_far), stack(e, e_far), stack(d, d_far), spread, spread_other, base, pick
    )
    e_far, d_far = hop(e, "z2"), hop(d, "z1")
    cut_at = 2 * CHUNK
    a1, a2, b1, b2 = a[:, 0:cut_at], a[:, cut_at:], b[:, 0:cut_at], b[:, cut_at:]
    a1_far, b1_far = hop(a1, "x"), hop(b1, "y")
    a1_far, b1_far, a2, b2 = tie(a1_far, b1_far, a2, b2)
    a2_far, b2_far = hop(a2, "x"), hop(b2, "y")

    for_a, for_b, small = prep(where, spread, spread_other, notes)

    def run(sub, rows_in, near, far):
        mine, given_part = conv(sub, where, rows_in, near, far, small)
        return mine, hop(given_part, "c")

    m0, o0 = run(0, for_a, a1, a1_far)
    m2, o2 = run(4, for_b, b1, b1_far)
    e, d, e_far, d_far, a2_far, b2_far, m0, m2 = tie(e, d, e_far, d_far, a2_far, b2_far, m0, m2)
    weights = [e, e_far, d, d_far]
    weights = weights + [hop(array, "c") for array in weights]
    m1, o1 = run(2, for_a, a2, a2_far)
    m3, o3 = run(6, for_b, b2, b2_far)
    mixed = finish(where, (m0, m1, m2, m3), (o0, o1, o2, o3), small, pick, base, weights)
    return mixed[None]


def solution(mesh):
    if dict(mesh.shape) == {"dp": 8, "group": 4}:
        grid = jax.sharding.Mesh(mesh.devices.reshape(4, 2, 2, 2), ("z", "y", "x", "core"))
        dp, group, body = ("z", "y"), ("x", "core"), hyper_shards
    else:
        grid, dp, group, body = mesh, ("dp",), ("group",), shards
    every = dp + group
    placed = (
        P(group, dp, None),
        P(group, dp),
        P(group, dp),
        P(group, dp),
        P(every),
        P(every, None),
        P(every, None),
        P(every),
        P(every, None),
    )
    return jax.shard_map(
        body, mesh=grid, in_specs=placed, out_specs=P(group, dp, None), check_vma=False
    )
```

```python
import functools

import jax
import jax.numpy as jnp
from jax import lax
from jax.experimental import pallas as pl
from jax.experimental.pallas import tpu as pltpu
from jax.sharding import PartitionSpec as P

D = 2048
KERNEL = 32
MAXLEN = 192
RCV_DEV = 384


epsilon = 1e-05


def shifted(array, axis, by):
    peers = lax.axis_size(axis)
    return lax.ppermute(array, axis, [(i, (i + by) % peers) for i in range(peers)])


def layer_norm(values, scale_gain):
    center = values - jnp.mean(values, axis=-1, keepdims=True)
    spread = jnp.mean(center * center, axis=-1, keepdims=True)
    return center * lax.rsqrt(spread + epsilon) * scale_gain.astype(jnp.float32)


def depth_pass(gated_rows, segment, depth_kernel):
    row_count = gated_rows.shape[0]
    margin = KERNEL // 2
    padded = jnp.pad(gated_rows, ((margin, margin), (0, 0)))
    labels = jnp.pad(segment, (margin, margin), constant_values=-1)
    kernel_rows = depth_kernel.astype(jnp.float32)
    depthwise = jnp.zeros_like(gated_rows)
    for column in range(KERNEL):
        inside = (labels[column : column + row_count] == segment)[:, None]
        depthwise = (
            depthwise
            + jnp.where(inside, padded[column : column + row_count], 0.0) * kernel_rows[:, column]
        )
    return depthwise


def conv_module(inputs, segment, params):
    norm_gain, weight_in, depth_kernel, post_gain, weight_out = params
    widths = inputs.shape[1]
    source = inputs.astype(jnp.float32)
    normed = layer_norm(source, norm_gain).astype(jnp.bfloat16)
    projected = jnp.dot(normed, weight_in, preferred_element_type=jnp.float32)
    gated_rows = projected[:, :widths] * jax.nn.sigmoid(projected[:, widths:])
    depthwise = depth_pass(gated_rows, segment, depth_kernel)
    normed_post = layer_norm(depthwise, post_gain)
    active = (normed_post * jax.nn.sigmoid(normed_post)).astype(jnp.bfloat16)
    return (source + jnp.dot(active, weight_out, preferred_element_type=jnp.float32)).astype(
        jnp.bfloat16
    )


def relocate(own_part, next_part, prev_part):
    from_prev = shifted((next_part[0], next_part[1]), "dp", 1)
    from_next = shifted((prev_part[0], prev_part[1]), "dp", -1)
    received = jnp.zeros((RCV_DEV + MAXLEN, D), jnp.bfloat16)
    segment = jnp.zeros((RCV_DEV,), jnp.int32)
    position = jnp.arange(RCV_DEV, dtype=jnp.int32)
    arrivals = (own_part, from_prev, from_next)
    for label_id in range(3):
        frame_rows, meta_data = arrivals[label_id]
        current = lax.dynamic_slice_in_dim(received, meta_data[1], MAXLEN, 0)
        received = lax.dynamic_update_slice_in_dim(received, current + frame_rows, meta_data[1], 0)
        inside = (position >= meta_data[1]) & (position < meta_data[1] + meta_data[0])
        segment = jnp.where(inside, label_id + 1, segment)
    return (received[:RCV_DEV], segment)


def shards(
    frames, lengths, destination, offsets, norm_gain, weight_in, depth_kernel, post_gain, weight_out
):
    dp_count = lax.axis_size("dp")
    params = (
        lax.all_gather(norm_gain, ("dp", "group"), axis=0, tiled=True),
        lax.all_gather(weight_in, ("dp", "group"), axis=0, tiled=True),
        lax.all_gather(depth_kernel, ("dp", "group"), axis=0, tiled=True),
        lax.all_gather(post_gain, ("dp", "group"), axis=0, tiled=True),
        lax.all_gather(weight_out, ("dp", "group"), axis=0, tiled=True),
    )
    my_index = lax.axis_index("dp")
    local_frames = frames[0]
    lengths_here = lengths[0]
    dest_here = destination[0]
    offsets_here = offsets[0]
    starts = jnp.cumsum(lengths_here) - lengths_here
    relative = (dest_here - my_index) % dp_count
    slot_ids = jnp.arange(3, dtype=jnp.int32)

    def pick_entry(values, which):
        return jnp.sum(jnp.where(slot_ids == which, values, 0))

    def slot_of(code):
        return jnp.sum(jnp.where(relative == code, slot_ids, 0))

    chosen = (slot_of(0), slot_of(1), slot_of(dp_count - 1))

    def cut_utterance(source_rows, which):
        start_row = pick_entry(starts, which)
        live_count = pick_entry(lengths_here, which)
        frame_rows = lax.dynamic_slice_in_dim(source_rows, start_row, MAXLEN, 0)
        keep_rows = jnp.arange(MAXLEN, dtype=jnp.int32) < live_count
        kept = jnp.where(keep_rows[:, None], frame_rows, jnp.zeros_like(frame_rows))
        return (kept, jnp.stack([live_count, pick_entry(offsets_here, which)]))

    received, segment = relocate(
        cut_utterance(local_frames, chosen[0]),
        cut_utterance(local_frames, chosen[1]),
        cut_utterance(local_frames, chosen[2]),
    )
    mixed = conv_module(received, segment, params)
    return mixed[None]


SWAP = ((0, 1), (1, 0))
HOPS = {
    "c": ("core", SWAP),
    "x": ("x", SWAP),
    "y": ("y", SWAP),
    "z1": ("z", tuple((i, i ^ 1) for i in range(4))),
    "z2": ("z", tuple((i, i ^ 2) for i in range(4))),
}
GAP = KERNEL // 2
PAD = RCV_DEV + 4 * GAP
PAIR = 2 * PAD
LANE = 128
BLOCKS = D // LANE
HALF = D // 2
FIRST = 384
SMALL = 48
META = 16
ROWS = PAIR
TILE = 64


def hop(array, name):
    axis, pairs = HOPS[name]
    return lax.ppermute(array, axis, pairs)


def turn(array, by):
    return lax.ppermute(array, ("z", "y"), [(i, (i + by) % 8) for i in range(8)])


def stack(first, second):
    return jnp.concatenate([first, second], 0)


def beside(*parts):
    return jnp.concatenate(parts, 1)


def tie(*arrays):
    return list(lax.optimization_barrier(arrays))


def coordinates():
    return [lax.axis_index(name) for name in ("z", "y", "x", "core")]


def bits(block):
    z, y, x, _ = coordinates()
    return (block >> 3) ^ (z >> 1), ((block >> 2) & 1) ^ (z & 1), ((block >> 1) & 1) ^ y, (block & 1) ^ x


def spot_a(block):
    z2, z1, y, x = bits(block)
    return x * 8 + y * 4 + z1 * 2 + z2


def spot_b(block):
    z2, z1, y, x = bits(block)
    return y * 8 + x * 4 + z2 * 2 + z1


def spot_e(block):
    z2, z1, y, x = bits(block)
    return z2 * 8 + z1 * 4 + y * 2 + x


def spot_d(block):
    z2, z1, y, x = bits(block)
    return z1 * 8 + z2 * 4 + y * 2 + x


def lanes(index):
    return pl.ds(pl.multiple_of(index * LANE, LANE), LANE)


COST = pl.CostEstimate(flops=2**20, bytes_accessed=2**16, transcendentals=0)


def local(lens, dest, offs, code):
    z, y, _, _ = coordinates()
    count, offset, start, before = 0, 0, 0, 0
    for slot in range(3):
        match = (dest[0, slot] - (z * 2 + y) + 8) % 8 == code
        count = jnp.where(match, lens[0, slot], count)
        offset = jnp.where(match, offs[0, slot], offset)
        start = jnp.where(match, before, start)
        before = before + lens[0, slot]
    return count, offset, start


def hot(condition):
    return jnp.where(condition, 1.0, 0.0).astype(jnp.bfloat16)


def take(picker, rows):
    return jnp.dot(picker, rows, preferred_element_type=jnp.float32)


def grid_of(rows, columns):
    shape = (rows, columns)
    return lax.broadcasted_iota(jnp.int32, shape, 0), lax.broadcasted_iota(jnp.int32, shape, 1)


def cut_kernel(lens, dest, offs, rows_ref, up0, up1, down0, down1):
    for code, first_ref, second_ref in ((1, up0, up1), (7, down0, down1)):
        count, offset, start = local(lens, dest, offs, code)
        spot, slot = grid_of(MAXLEN + META, rows_ref.shape[0])
        picker = hot((slot == start + spot) & (spot < count))
        spot, _ = grid_of(MAXLEN + META, HALF)
        note = jnp.where(spot == MAXLEN, count, 0) + jnp.where(spot == MAXLEN + 1, offset // 2, 0)
        note = note + jnp.where(spot == MAXLEN + 2, offset % 2, 0)
        first = take(picker, rows_ref[:, 0:HALF]) + note.astype(jnp.float32)
        first_ref[...] = first.astype(jnp.bfloat16)
        second_ref[...] = take(picker[0:MAXLEN], rows_ref[:, HALF:D]).astype(jnp.bfloat16)


def smem(count):
    return [pl.BlockSpec(memory_space=pltpu.SMEM)] * count


def vmem(count):
    return [pl.BlockSpec(memory_space=pltpu.VMEM)] * count


def shape(rows, columns, dtype=jnp.bfloat16):
    return jax.ShapeDtypeStruct((rows, columns), dtype)


def limits(mebibytes):
    return pltpu.CompilerParams(vmem_limit_bytes=mebibytes * 2**20)


def cut(lens, dest, offs, rows):
    first, second = shape(MAXLEN + META, HALF), shape(MAXLEN, HALF)
    return pl.pallas_call(
        cut_kernel,
        out_shape=(first, second, first, second),
        in_specs=smem(3) + vmem(1),
        out_specs=tuple(vmem(4)),
        compiler_params=limits(16),
        cost_estimate=COST,
        name="cut",
    )(lens, dest, offs, rows)


def place_kernel(lens, dest, offs, rows_ref, p0, p1, n0, n1, spread_ref, base_ref, pick_ref):
    count, offset, start = local(lens, dest, offs, 0)
    ones = jnp.ones((1, 1), jnp.int32)

    def noted(ref):
        head = ref[MAXLEN : MAXLEN + META, 0:LANE].astype(jnp.float32).astype(jnp.int32)
        return head[0:1, 0:1], head[1:2, 0:1] * 2 + head[2:3, 0:1]

    parts = [(count * ones, offset * ones), noted(p0), noted(n0)]

    def placer(which, width, first):
        mine = parts[which]
        rank = sum((other[1] < mine[1]).astype(jnp.int32) for other in parts)
        spot, slot = grid_of(PAD, width)
        source = slot - first
        inside = (source >= 0) & (source < mine[0])
        return hot((spot == GAP + mine[1] + GAP * rank + source) & inside)

    from_own = placer(0, rows_ref.shape[0], start)
    from_prev = placer(1, MAXLEN + META, 0)
    from_next = placer(2, MAXLEN + META, 0)
    first = take(from_own, rows_ref[:, 0:HALF]) + take(from_prev, p0[...]) + take(from_next, n0[...])
    spread_ref[:, 0:HALF] = first.astype(jnp.bfloat16)
    second = (
        take(from_own, rows_ref[:, HALF:D])
        + take(from_prev[:, 0:MAXLEN], p1[...])
        + take(from_next[:, 0:MAXLEN], n1[...])
    )
    spread_ref[:, HALF:D] = second.astype(jnp.bfloat16)
    flat, spot = grid_of(RCV_DEV, PAD)
    rank = sum((part[1] <= flat).astype(jnp.int32) for part in parts)
    pick = hot(spot == flat + GAP * rank)
    pick_ref[...] = pick
    base_ref[...] = take(pick, spread_ref[...]).astype(jnp.bfloat16)


def place(lens, dest, offs, rows, arrived):
    return pl.pallas_call(
        place_kernel,
        out_shape=(shape(PAD, D), shape(RCV_DEV, D), shape(RCV_DEV, PAD)),
        in_specs=smem(3) + vmem(5),
        out_specs=tuple(vmem(3)),
        compiler_params=limits(24),
        cost_estimate=COST,
        name="place",
    )(lens, dest, offs, rows, *arrived)


def prep_kernel(mine_ref, other_ref, notes_ref, first_ref, second_ref, small_ref):
    for block in range(BLOCKS):
        spot = spot_a(block)
        at = pl.ds(pl.multiple_of((spot & 7) * META, META), META)
        for part in range(SMALL // META):
            tile = notes_ref[at, lanes((spot >> 3) * (SMALL // META) + part)]
            small_ref[part * META : (part + 1) * META, block * LANE : (block + 1) * LANE] = tile.astype(
                jnp.float32
            )
    for base, rows_ref in ((0, mine_ref), (PAD, other_ref)):

        def one(step, carry):
            values = rows_ref[pl.ds(pl.multiple_of(step * TILE, TILE), TILE), :].astype(jnp.float32)
            center = values - jnp.mean(values, axis=-1, keepdims=True)
            spread = jnp.mean(center * center, axis=-1, keepdims=True)
            scaled = center * lax.rsqrt(spread + epsilon) * small_ref[KERNEL : KERNEL + 1, :]
            scaled = scaled.astype(jnp.bfloat16)
            at = pl.ds(pl.multiple_of(base + step * TILE, TILE), TILE)
            for block in range(BLOCKS):
                part = scaled[:, block * LANE : (block + 1) * LANE]
                first_ref[at, lanes(spot_a(block))] = part
                second_ref[at, lanes(spot_b(block))] = part
            return carry

        lax.fori_loop(0, PAD // TILE, one, 0)


def prep(mine, other, notes):
    return pl.pallas_call(
        prep_kernel,
        out_shape=(shape(PAIR, D), shape(PAIR, D), shape(SMALL, D, jnp.float32)),
        in_specs=vmem(3),
        out_specs=tuple(vmem(3)),
        compiler_params=limits(20),
        cost_estimate=COST,
        name="prep",
    )(mine, other, notes)


def conv_kernel(sub, rows_hbm, near_hbm, far_hbm, small_ref, own_ref, other_ref, gated, taps, rows_ref, near_ref, far_ref, done):
    width = own_ref.shape[1]
    tiles = width // LANE
    steps = PAIR // ROWS
    spans = [pl.ds(step * ROWS, ROWS) for step in range(steps)]
    loads = [
        pltpu.make_async_copy(near_hbm, near_ref, done.at[0]),
        pltpu.make_async_copy(far_hbm, far_ref, done.at[1]),
    ]
    for step, span in enumerate(spans):
        loads.append(pltpu.make_async_copy(rows_hbm.at[span, :], rows_ref.at[span, :], done.at[2 + step]))
    for load in loads:
        load.start()
    half = lax.axis_index("core")
    for tile in range(tiles):
        gated[tile, 0:GAP, :] = jnp.zeros((GAP, LANE), jnp.float32)
        gated[tile, GAP + PAIR : 2 * GAP + PAIR, :] = jnp.zeros((GAP, LANE), jnp.float32)
        taps[tile] = small_ref[0:KERNEL, lanes(half * (BLOCKS // 2) + sub + tile)]
    loads[0].wait()
    loads[1].wait()
    for step, span in enumerate(spans):
        loads[2 + step].wait()
        both = take(rows_ref[span, 0:HALF], near_ref[...]) + take(rows_ref[span, HALF:D], far_ref[...])
        mixed = both[:, 0:width] * jax.nn.sigmoid(both[:, width:])
        for tile in range(tiles):
            gated[tile, pl.ds(GAP + step * ROWS, ROWS), :] = mixed[:, tile * LANE : (tile + 1) * LANE]

    def slide(out_ref, base):
        def one(step, carry):
            for tile in range(tiles):
                total = jnp.zeros((TILE, LANE), jnp.float32)
                for tap in range(KERNEL):
                    window = gated[tile, pl.ds(base + step * TILE + tap, TILE), :]
                    total = total + window * taps[tile, tap : tap + 1, :]
                at = pl.ds(pl.multiple_of(step * TILE, TILE), TILE)
                out_ref[at, tile * LANE : (tile + 1) * LANE] = total.astype(jnp.bfloat16)
            return carry

        lax.fori_loop(0, PAD // TILE, one, 0)

    slide(own_ref, 0)
    slide(other_ref, PAD)


def anywhere(count):
    return [pl.BlockSpec(memory_space=pl.ANY)] * count


def conv(sub, rows, near, far, small):
    width = near.shape[1] // 2
    out = shape(PAD, width)
    weight = pltpu.VMEM(near.shape, near.dtype)
    return pl.pallas_call(
        functools.partial(conv_kernel, sub),
        out_shape=(out, out),
        in_specs=anywhere(3) + vmem(1),
        out_specs=tuple(vmem(2)),
        scratch_shapes=[
            pltpu.VMEM((width // LANE, PAIR + 2 * GAP, LANE), jnp.float32),
            pltpu.VMEM((width // LANE, KERNEL, LANE), jnp.float32),
            pltpu.VMEM((PAIR, D), jnp.bfloat16),
            weight,
            weight,
            pltpu.SemaphoreType.DMA((2 + PAIR // ROWS,)),
        ],
        compiler_params=limits(16),
        cost_estimate=COST,
        name="conv",
    )(rows, near, far, small)


def finish_kernel(
    m0, m1, m2, m3, o0, o1, o2, o3, small_ref, pick_ref, base_ref,
    e8, er, d8, dr, f8, fr, g8, gr, out_ref, first, second, weights, done,
):
    sources = (e8, er, d8, dr, f8, fr, g8, gr)
    loads = [
        pltpu.make_async_copy(source, weights.at[index], done.at[index])
        for index, source in enumerate(sources)
    ]
    for load in loads:
        load.start()
    half = lax.axis_index("core")
    count = KERNEL + 1
    pieces = [(half, (m0, m1, m2, m3)), (1 - half, (o0, o1, o2, o3))]
    refs = [ref for _, group in pieces for ref in group]
    total = jnp.zeros((PAD, 1), jnp.float32)
    for ref in refs:
        total = total + jnp.sum(ref[...].astype(jnp.float32), axis=-1, keepdims=True)
    mean = total / D
    total = jnp.zeros((PAD, 1), jnp.float32)
    for ref in refs:
        center = ref[...].astype(jnp.float32) - mean
        total = total + jnp.sum(center * center, axis=-1, keepdims=True)
    scale = lax.rsqrt(total / D + epsilon)
    for side, group in pieces:
        place = side * (BLOCKS // 2)
        for ref in group:
            blocks = [place + tile for tile in range(ref.shape[1] // LANE)]
            place = place + len(blocks)
            parts = []
            for tile, block in enumerate(blocks):
                gain = small_ref[count : count + 1, lanes(block)]
                values = ref[:, tile * LANE : (tile + 1) * LANE].astype(jnp.float32)
                post = (values - mean) * scale * gain
                parts.append((post * jax.nn.sigmoid(post)).astype(jnp.bfloat16))
            kept = take(pick_ref[...], beside(*parts) if len(parts) > 1 else parts[0])
            kept = kept.astype(jnp.bfloat16)
            for tile, block in enumerate(blocks):
                part = kept[:, tile * LANE : (tile + 1) * LANE]
                first[:, lanes(spot_e(block))] = part
                second[:, lanes(spot_d(block))] = part
    width = HALF // 2
    for turn_index, (side, active, edge) in enumerate(
        ((half, first, 0), (half, second, width), (1 - half, first, 0), (1 - half, second, width))
    ):
        at = pl.ds(pl.multiple_of(side * HALF + edge, width), width)
        loads[2 * turn_index].wait()
        loads[2 * turn_index + 1].wait()
        result = (
            take(active[:, 0:HALF], weights[2 * turn_index])
            + take(active[:, HALF:D], weights[2 * turn_index + 1])
            + base_ref[:, at].astype(jnp.float32)
        )
        out_ref[:, at] = result.astype(jnp.bfloat16)


def finish(mine, others, small, pick, base, weights):
    return pl.pallas_call(
        finish_kernel,
        out_shape=shape(RCV_DEV, D),
        in_specs=vmem(11) + anywhere(8),
        out_specs=vmem(1)[0],
        scratch_shapes=[pltpu.VMEM((RCV_DEV, D), jnp.bfloat16)] * 2
        + [pltpu.VMEM((8, HALF, HALF // 2), jnp.bfloat16), pltpu.SemaphoreType.DMA((8,))],
        compiler_params=limits(28),
        cost_estimate=COST,
        name="finish",
    )(*mine, *others, small, pick, base, *weights)


def hyper_shards(
    frames, lengths, destination, offsets, norm_gain, weight_in, depth_kernel, post_gain, weight_out
):
    low = lax.axis_index("core") == 0
    per = weight_in.shape[0]

    left = beside(weight_in[:, 0:HALF], weight_in[:, D : D + HALF], weight_out[:, 0:HALF])
    right = beside(weight_in[:, HALF:D], weight_in[:, D + HALF :], weight_out[:, HALF:])
    kept, given = jnp.where(low, left, right), jnp.where(low, right, left)
    got = hop(given, "c")
    rows = frames[0]
    up0, up1, down0, down1 = cut(lengths, destination, offsets, rows)
    chip = jnp.where(low, stack(kept, got), stack(got, kept))
    chip, up1, down1 = tie(chip, up1, down1)

    notes = jnp.concatenate(
        [depth_kernel.T, norm_gain[None], post_gain[None], jnp.zeros((SMALL - KERNEL - 2, per), jnp.bfloat16)], 0
    )
    blank = jnp.zeros_like(notes)
    pair = [jnp.where(low, beside(one, blank), beside(blank, one)) for one in (notes, hop(notes, "x"))]
    pair = stack(*pair)
    pair = pair + hop(pair, "c")
    tiles = [pair[low_row : low_row + META] for low_row in range(0, 2 * SMALL, META)]
    notes = beside(*tiles, jnp.zeros((META, HALF - 2 * LANE * SMALL // META), jnp.bfloat16))

    def stream(start):
        edges = (start, start + FIRST, start + HALF // 2)
        spans = [(low_edge + gate, high_edge + gate) for low_edge, high_edge in zip(edges, edges[1:]) for gate in (0, HALF)]
        return beside(*[chip[:, low_edge:high_edge] for low_edge, high_edge in spans])

    a, b = stream(0), stream(HALF // 2)
    o = chip[:, 2 * HALF : 3 * HALF]

    def grow(array, extra, name):
        size = array.shape[0]
        arrived = hop(stack(array, extra), name)
        return stack(array, arrived[0:size]), stack(extra, arrived[size:])

    prev0, next0 = turn(up0, 1), turn(down0, -1)
    (a, notes), b_far, o_far = grow(a, notes, "z2"), hop(b, "z1"), hop(o, "x")
    prev0, next0, a, notes, b, o, up1, down1 = tie(
        prev0, next0, a, notes, stack(b, b_far), stack(o, o_far), up1, down1
    )
    prev1, next1 = turn(up1, 1), turn(down1, -1)
    (a, notes), b_far, o_far = grow(a, notes, "z1"), hop(b, "z2"), hop(o, "y")
    prev1, next1, a, notes, b, o = tie(prev1, next1, a, notes, stack(b, b_far), stack(o, o_far))
    e, d = o[:, 0 : HALF // 2], o[:, HALF // 2 :]
    spread, base, pick = place(lengths, destination, offsets, rows, (prev0, prev1, next0, next1))
    (a, notes), b_far, e_far, d_far = grow(a, notes, "y"), hop(b, "x"), hop(e, "z1"), hop(d, "z2")
    a, notes, b, e, d, spread, base, pick = tie(
        a, notes, stack(b, b_far), stack(e, e_far), stack(d, d_far), spread, base, pick
    )
    e_far, d_far = hop(e, "z2"), hop(d, "z1")
    cut_at = 2 * FIRST
    a1, a2, b1, b2 = a[:, 0:cut_at], a[:, cut_at:], b[:, 0:cut_at], b[:, cut_at:]
    a1_far, b1_far = hop(a1, "x"), hop(b1, "y")
    for_a, for_b, small = prep(spread, hop(spread, "c"), notes)
    a1_far, b1_far, a2, b2, small = tie(a1_far, b1_far, a2, b2, small)
    a2_far, b2_far = hop(a2, "x"), hop(b2, "y")

    def run(sub, rows_in, near, far):
        mine, given_part = conv(sub, rows_in, near, far, small)
        return mine, hop(given_part, "c")

    m0, o0 = run(0, for_a, a1, a1_far)
    m2, o2 = run(BLOCKS // 4, for_b, b1, b1_far)
    e, d, e_far, d_far, a2_far, b2_far, m0, o0, m2, o2 = tie(
        e, d, e_far, d_far, a2_far, b2_far, m0, o0, m2, o2
    )
    weights = [e, e_far, d, d_far]
    weights = weights + [hop(array, "c") for array in weights]
    m1, o1 = run(FIRST // LANE, for_a, a2, a2_far)
    m3, o3 = run(BLOCKS // 4 + FIRST // LANE, for_b, b2, b2_far)
    mixed = finish((m0, m1, m2, m3), (o0, o1, o2, o3), small, pick, base, weights)
    return mixed[None]


def solution(mesh):
    if dict(mesh.shape) == {"dp": 8, "group": 4}:
        grid = jax.sharding.Mesh(mesh.devices.reshape(4, 2, 2, 2), ("z", "y", "x", "core"))
        dp, group, body = ("z", "y"), ("x", "core"), hyper_shards
    else:
        grid, dp, group, body = mesh, ("dp",), ("group",), shards
    every = dp + group
    placed = (
        P(group, dp, None),
        P(group, dp),
        P(group, dp),
        P(group, dp),
        P(every),
        P(every, None),
        P(every, None),
        P(every),
        P(every, None),
    )
    return jax.shard_map(
        body, mesh=grid, in_specs=placed, out_specs=P(group, dp, None), check_vma=False
    )
```

```python
import functools

import jax
import jax.numpy as jnp
from jax import lax
from jax.experimental import pallas as pl
from jax.experimental.pallas import tpu as pltpu
from jax.sharding import PartitionSpec as P

D = 2048
KERNEL = 32
MAXLEN = 192
RCV_DEV = 384


epsilon = 1e-05


def shifted(array, axis, by):
    peers = lax.axis_size(axis)
    return lax.ppermute(array, axis, [(i, (i + by) % peers) for i in range(peers)])


def layer_norm(values, scale_gain):
    center = values - jnp.mean(values, axis=-1, keepdims=True)
    spread = jnp.mean(center * center, axis=-1, keepdims=True)
    return center * lax.rsqrt(spread + epsilon) * scale_gain.astype(jnp.float32)


def depth_pass(gated_rows, segment, depth_kernel):
    row_count = gated_rows.shape[0]
    margin = KERNEL // 2
    padded = jnp.pad(gated_rows, ((margin, margin), (0, 0)))
    labels = jnp.pad(segment, (margin, margin), constant_values=-1)
    kernel_rows = depth_kernel.astype(jnp.float32)
    depthwise = jnp.zeros_like(gated_rows)
    for column in range(KERNEL):
        inside = (labels[column : column + row_count] == segment)[:, None]
        depthwise = (
            depthwise
            + jnp.where(inside, padded[column : column + row_count], 0.0) * kernel_rows[:, column]
        )
    return depthwise


def conv_module(inputs, segment, params):
    norm_gain, weight_in, depth_kernel, post_gain, weight_out = params
    widths = inputs.shape[1]
    source = inputs.astype(jnp.float32)
    normed = layer_norm(source, norm_gain).astype(jnp.bfloat16)
    projected = jnp.dot(normed, weight_in, preferred_element_type=jnp.float32)
    gated_rows = projected[:, :widths] * jax.nn.sigmoid(projected[:, widths:])
    depthwise = depth_pass(gated_rows, segment, depth_kernel)
    normed_post = layer_norm(depthwise, post_gain)
    active = (normed_post * jax.nn.sigmoid(normed_post)).astype(jnp.bfloat16)
    return (source + jnp.dot(active, weight_out, preferred_element_type=jnp.float32)).astype(
        jnp.bfloat16
    )


def relocate(own_part, next_part, prev_part):
    from_prev = shifted((next_part[0], next_part[1]), "dp", 1)
    from_next = shifted((prev_part[0], prev_part[1]), "dp", -1)
    received = jnp.zeros((RCV_DEV + MAXLEN, D), jnp.bfloat16)
    segment = jnp.zeros((RCV_DEV,), jnp.int32)
    position = jnp.arange(RCV_DEV, dtype=jnp.int32)
    arrivals = (own_part, from_prev, from_next)
    for label_id in range(3):
        frame_rows, meta_data = arrivals[label_id]
        current = lax.dynamic_slice_in_dim(received, meta_data[1], MAXLEN, 0)
        received = lax.dynamic_update_slice_in_dim(received, current + frame_rows, meta_data[1], 0)
        inside = (position >= meta_data[1]) & (position < meta_data[1] + meta_data[0])
        segment = jnp.where(inside, label_id + 1, segment)
    return (received[:RCV_DEV], segment)


def shards(
    frames, lengths, destination, offsets, norm_gain, weight_in, depth_kernel, post_gain, weight_out
):
    dp_count = lax.axis_size("dp")
    params = (
        lax.all_gather(norm_gain, ("dp", "group"), axis=0, tiled=True),
        lax.all_gather(weight_in, ("dp", "group"), axis=0, tiled=True),
        lax.all_gather(depth_kernel, ("dp", "group"), axis=0, tiled=True),
        lax.all_gather(post_gain, ("dp", "group"), axis=0, tiled=True),
        lax.all_gather(weight_out, ("dp", "group"), axis=0, tiled=True),
    )
    my_index = lax.axis_index("dp")
    local_frames = frames[0]
    lengths_here = lengths[0]
    dest_here = destination[0]
    offsets_here = offsets[0]
    starts = jnp.cumsum(lengths_here) - lengths_here
    relative = (dest_here - my_index) % dp_count
    slot_ids = jnp.arange(3, dtype=jnp.int32)

    def pick_entry(values, which):
        return jnp.sum(jnp.where(slot_ids == which, values, 0))

    def slot_of(code):
        return jnp.sum(jnp.where(relative == code, slot_ids, 0))

    chosen = (slot_of(0), slot_of(1), slot_of(dp_count - 1))

    def cut_utterance(source_rows, which):
        start_row = pick_entry(starts, which)
        live_count = pick_entry(lengths_here, which)
        frame_rows = lax.dynamic_slice_in_dim(source_rows, start_row, MAXLEN, 0)
        keep_rows = jnp.arange(MAXLEN, dtype=jnp.int32) < live_count
        kept = jnp.where(keep_rows[:, None], frame_rows, jnp.zeros_like(frame_rows))
        return (kept, jnp.stack([live_count, pick_entry(offsets_here, which)]))

    received, segment = relocate(
        cut_utterance(local_frames, chosen[0]),
        cut_utterance(local_frames, chosen[1]),
        cut_utterance(local_frames, chosen[2]),
    )
    mixed = conv_module(received, segment, params)
    return mixed[None]


SWAP = ((0, 1), (1, 0))
HOPS = {
    "c": ("core", SWAP),
    "x": ("x", SWAP),
    "y": ("y", SWAP),
    "z1": ("z", tuple((i, i ^ 1) for i in range(4))),
    "z2": ("z", tuple((i, i ^ 2) for i in range(4))),
}
GAP = KERNEL // 2
PAD = RCV_DEV + 4 * GAP
PAIR = 2 * PAD
LANE = 128
BLOCKS = D // LANE
HALF = D // 2
PART = 256
IN1, IN2 = ("z1", "y", "z2", "x"), ("z2", "z1", "y", "x")
IN3, IN4 = ("z1", "z2", "x", "y"), ("z2", "x", "z1", "y")
OUT1, OUT2 = ("z2", "x", "y", "z1"), ("z1", "y", "x", "z2")
NOTES = ("x", "z1", "z2", "y")
SMALL = 48
META = 16
TILE = 64


def hop(array, name):
    axis, pairs = HOPS[name]
    return lax.ppermute(array, axis, pairs)


def turn(array, by):
    return lax.ppermute(array, ("z", "y"), [(i, (i + by) % 8) for i in range(8)])


def stack(first, second):
    return jnp.concatenate([first, second], 0)


def beside(*parts):
    return jnp.concatenate(parts, 1)


def tie(*arrays):
    return list(lax.optimization_barrier(arrays))


def coordinates():
    return [lax.axis_index(name) for name in ("z", "y", "x", "core")]


def spot(order, block):
    z, y, x, _ = coordinates()
    bit = {"z2": (block >> 3) ^ (z >> 1), "z1": ((block >> 2) & 1) ^ (z & 1), "y": ((block >> 1) & 1) ^ y, "x": (block & 1) ^ x}
    return sum(bit[name] << place for place, name in enumerate(order))


def lanes(index):
    return pl.ds(pl.multiple_of(index * LANE, LANE), LANE)


COST = pl.CostEstimate(flops=2**20, bytes_accessed=2**16, transcendentals=0)


def local(lens, dest, offs, code):
    z, y, _, _ = coordinates()
    count, offset, start, before = 0, 0, 0, 0
    for slot in range(3):
        match = (dest[0, slot] - (z * 2 + y) + 8) % 8 == code
        count = jnp.where(match, lens[0, slot], count)
        offset = jnp.where(match, offs[0, slot], offset)
        start = jnp.where(match, before, start)
        before = before + lens[0, slot]
    return count, offset, start


def hot(condition):
    return jnp.where(condition, 1.0, 0.0).astype(jnp.bfloat16)


def take(picker, rows):
    return jnp.dot(picker, rows, preferred_element_type=jnp.float32)


def grid_of(rows, columns):
    shape = (rows, columns)
    return lax.broadcasted_iota(jnp.int32, shape, 0), lax.broadcasted_iota(jnp.int32, shape, 1)


def cut_kernel(lens, dest, offs, rows_ref, up_ref, down_ref):
    for code, out_ref in ((1, up_ref), (7, down_ref)):
        count, offset, start = local(lens, dest, offs, code)
        spot, slot = grid_of(MAXLEN + META, rows_ref.shape[0])
        picker = hot((slot == start + spot) & (spot < count))
        spot, _ = grid_of(MAXLEN + META, D)
        note = jnp.where(spot == MAXLEN, count, 0) + jnp.where(spot == MAXLEN + 1, offset // 2, 0)
        note = note + jnp.where(spot == MAXLEN + 2, offset % 2, 0)
        out_ref[...] = (take(picker, rows_ref[...]) + note.astype(jnp.float32)).astype(jnp.bfloat16)


def smem(count):
    return [pl.BlockSpec(memory_space=pltpu.SMEM)] * count


def vmem(count):
    return [pl.BlockSpec(memory_space=pltpu.VMEM)] * count


def anywhere(count):
    return [pl.BlockSpec(memory_space=pl.ANY)] * count


def shape(rows, columns, dtype=jnp.bfloat16):
    return jax.ShapeDtypeStruct((rows, columns), dtype)


def limits(mebibytes):
    return pltpu.CompilerParams(vmem_limit_bytes=mebibytes * 2**20)


def cut(lens, dest, offs, rows):
    sent = shape(MAXLEN + META, D)
    return pl.pallas_call(
        cut_kernel,
        out_shape=(sent, sent),
        in_specs=smem(3) + vmem(1),
        out_specs=tuple(vmem(2)),
        compiler_params=limits(16),
        cost_estimate=COST,
        name="cut",
    )(lens, dest, offs, rows)


def place_kernel(lens, dest, offs, rows_ref, prev_ref, next_ref, spread_ref, base_ref, pick_ref):
    count, offset, start = local(lens, dest, offs, 0)
    ones = jnp.ones((1, 1), jnp.int32)

    def noted(ref):
        head = ref[MAXLEN : MAXLEN + META, 0:LANE].astype(jnp.float32).astype(jnp.int32)
        return head[0:1, 0:1], head[1:2, 0:1] * 2 + head[2:3, 0:1]

    parts = [(count * ones, offset * ones), noted(prev_ref), noted(next_ref)]

    def placer(which, width, first):
        mine = parts[which]
        rank = sum((other[1] < mine[1]).astype(jnp.int32) for other in parts)
        spot, slot = grid_of(PAD, width)
        source = slot - first
        inside = (source >= 0) & (source < mine[0])
        return hot((spot == GAP + mine[1] + GAP * rank + source) & inside)

    from_own = placer(0, rows_ref.shape[0], start)
    from_prev = placer(1, MAXLEN + META, 0)
    from_next = placer(2, MAXLEN + META, 0)
    found = take(from_own, rows_ref[...]) + take(from_prev, prev_ref[...]) + take(from_next, next_ref[...])
    spread_ref[...] = found.astype(jnp.bfloat16)
    flat, spot = grid_of(RCV_DEV, PAD)
    rank = sum((part[1] <= flat).astype(jnp.int32) for part in parts)
    pick = hot(spot == flat + GAP * rank)
    pick_ref[...] = pick
    base_ref[...] = take(pick, spread_ref[...]).astype(jnp.bfloat16)


def place(lens, dest, offs, rows, arrived):
    return pl.pallas_call(
        place_kernel,
        out_shape=(shape(PAD, D), shape(RCV_DEV, D), shape(RCV_DEV, PAD)),
        in_specs=smem(3) + vmem(3),
        out_specs=tuple(vmem(3)),
        compiler_params=limits(24),
        cost_estimate=COST,
        name="place",
    )(lens, dest, offs, rows, *arrived)


def prep_kernel(mine_ref, other_ref, notes_ref, out1, out2, out3, out4, small_ref):
    for block in range(BLOCKS):
        tile = notes_ref[:, lanes(spot(NOTES, block))]
        small_ref[:, block * LANE : (block + 1) * LANE] = tile.astype(jnp.float32)
    for base, rows_ref in ((0, mine_ref), (PAD, other_ref)):

        def one(step, carry):
            values = rows_ref[pl.ds(pl.multiple_of(step * TILE, TILE), TILE), :].astype(jnp.float32)
            center = values - jnp.mean(values, axis=-1, keepdims=True)
            spread = jnp.mean(center * center, axis=-1, keepdims=True)
            scaled = center * lax.rsqrt(spread + epsilon) * small_ref[KERNEL : KERNEL + 1, :]
            scaled = scaled.astype(jnp.bfloat16)
            at = pl.ds(pl.multiple_of(base + step * TILE, TILE), TILE)
            for block in range(BLOCKS):
                part = scaled[:, block * LANE : (block + 1) * LANE]
                for order, out_ref in ((IN1, out1), (IN2, out2), (IN3, out3), (IN4, out4)):
                    place = spot(order, block)
                    out_ref[place >> 3, at, lanes(place & 7)] = part
            return carry

        lax.fori_loop(0, PAD // TILE, one, 0)


def prep(mine, other, notes):
    return pl.pallas_call(
        prep_kernel,
        out_shape=(jax.ShapeDtypeStruct((2, PAIR, HALF), jnp.bfloat16),) * 4 + (shape(SMALL, D, jnp.float32),),
        in_specs=vmem(3),
        out_specs=tuple(vmem(5)),
        compiler_params=limits(28),
        cost_estimate=COST,
        name="prep",
    )(mine, other, notes)


def early_kernel(rows_hbm, near_ref, out_ref, rows_ref, done):
    load = pltpu.make_async_copy(rows_hbm.at[0], rows_ref, done)
    load.start()
    load.wait()
    out_ref[...] = take(rows_ref[...], near_ref[...])


def early(rows, near):
    return pl.pallas_call(
        early_kernel,
        out_shape=shape(PAIR, near.shape[1], jnp.float32),
        in_specs=anywhere(1) + vmem(1),
        out_specs=vmem(1)[0],
        scratch_shapes=[pltpu.VMEM((PAIR, HALF), jnp.bfloat16), pltpu.SemaphoreType.DMA],
        compiler_params=limits(12),
        cost_estimate=COST,
        name="early",
    )(rows, near)


def conv_kernel(sub, rows_hbm, part_hbm, far_hbm, small_ref, own_ref, other_ref, gated, taps, rows_ref, part_ref, far_ref, done):
    width = own_ref.shape[1]
    tiles = width // LANE
    loads = [
        pltpu.make_async_copy(rows_hbm.at[1], rows_ref, done.at[0]),
        pltpu.make_async_copy(far_hbm, far_ref, done.at[1]),
        pltpu.make_async_copy(part_hbm, part_ref, done.at[2]),
    ]
    for load in loads:
        load.start()
    half = lax.axis_index("core")
    for tile in range(tiles):
        gated[tile, 0:GAP, :] = jnp.zeros((GAP, LANE), jnp.float32)
        gated[tile, GAP + PAIR : 2 * GAP + PAIR, :] = jnp.zeros((GAP, LANE), jnp.float32)
        taps[tile] = small_ref[0:KERNEL, lanes(half * (BLOCKS // 2) + sub + tile)]
    for load in loads:
        load.wait()
    both = part_ref[...] + take(rows_ref[...], far_ref[...])
    mixed = both[:, 0:width] * jax.nn.sigmoid(both[:, width:])
    for tile in range(tiles):
        gated[tile, GAP : GAP + PAIR, :] = mixed[:, tile * LANE : (tile + 1) * LANE]

    def slide(out_ref, base):
        def one(step, carry):
            for tile in range(tiles):
                total = jnp.zeros((TILE, LANE), jnp.float32)
                for tap in range(KERNEL):
                    window = gated[tile, pl.ds(base + step * TILE + tap, TILE), :]
                    total = total + window * taps[tile, tap : tap + 1, :]
                at = pl.ds(pl.multiple_of(step * TILE, TILE), TILE)
                out_ref[at, tile * LANE : (tile + 1) * LANE] = total.astype(jnp.bfloat16)
            return carry

        lax.fori_loop(0, PAD // TILE, one, 0)

    slide(own_ref, 0)
    slide(other_ref, PAD)


def conv(sub, rows, part, far, small):
    width = far.shape[1] // 2
    out = shape(PAD, width)
    return pl.pallas_call(
        functools.partial(conv_kernel, sub),
        out_shape=(out, out),
        in_specs=anywhere(3) + vmem(1),
        out_specs=tuple(vmem(2)),
        scratch_shapes=[
            pltpu.VMEM((width // LANE, PAIR + 2 * GAP, LANE), jnp.float32),
            pltpu.VMEM((width // LANE, KERNEL, LANE), jnp.float32),
            pltpu.VMEM((PAIR, HALF), jnp.bfloat16),
            pltpu.VMEM(part.shape, part.dtype),
            pltpu.VMEM(far.shape, far.dtype),
            pltpu.SemaphoreType.DMA((3,)),
        ],
        compiler_params=limits(16),
        cost_estimate=COST,
        name="conv",
    )(rows, part, far, small)


def finish_kernel(
    m0, m1, m2, m3, o0, o1, o2, o3, small_ref, pick_ref, base_hbm,
    e8, er, d8, dr, f8, fr, g8, gr, out_hbm, first, second, weights, base, result, done, sent,
):
    sources = (e8, er, d8, dr, f8, fr, g8, gr)
    loads = [
        pltpu.make_async_copy(
            source, weights.at[index // 2, pl.ds(index % 2 * HALF, HALF), :], done.at[index]
        )
        for index, source in enumerate(sources)
    ]
    loads.append(pltpu.make_async_copy(base_hbm, base, done.at[len(sources)]))
    for load in loads:
        load.start()
    half = lax.axis_index("core")
    count = KERNEL + 1
    pieces = [(half, (m0, m1, m2, m3)), (1 - half, (o0, o1, o2, o3))]
    refs = [ref for _, group in pieces for ref in group]
    total = jnp.zeros((PAD, 1), jnp.float32)
    for ref in refs:
        total = total + jnp.sum(ref[...].astype(jnp.float32), axis=-1, keepdims=True)
    mean = total / D
    total = jnp.zeros((PAD, 1), jnp.float32)
    for ref in refs:
        center = ref[...].astype(jnp.float32) - mean
        total = total + jnp.sum(center * center, axis=-1, keepdims=True)
    scale = lax.rsqrt(total / D + epsilon)
    for side, group in pieces:
        place = side * (BLOCKS // 2)
        for ref in group:
            blocks = [place + tile for tile in range(ref.shape[1] // LANE)]
            place = place + len(blocks)
            parts = []
            for tile, block in enumerate(blocks):
                gain = small_ref[count : count + 1, lanes(block)]
                values = ref[:, tile * LANE : (tile + 1) * LANE].astype(jnp.float32)
                post = (values - mean) * scale * gain
                parts.append((post * jax.nn.sigmoid(post)).astype(jnp.bfloat16))
            kept = take(pick_ref[...], beside(*parts) if len(parts) > 1 else parts[0])
            kept = kept.astype(jnp.bfloat16)
            for tile, block in enumerate(blocks):
                part = kept[:, tile * LANE : (tile + 1) * LANE]
                first[:, lanes(spot(OUT1, block))] = part
                second[:, lanes(spot(OUT2, block))] = part
    width = HALF // 2
    loads[len(sources)].wait()
    stores = []
    for turn_index, (side, active, edge) in enumerate(
        ((half, first, 0), (half, second, width), (1 - half, first, 0), (1 - half, second, width))
    ):
        at = pl.ds(pl.multiple_of(side * HALF + edge, width), width)
        loads[2 * turn_index].wait()
        loads[2 * turn_index + 1].wait()
        mixed = take(active[...], weights[turn_index]) + base[:, at].astype(jnp.float32)
        result[turn_index] = mixed.astype(jnp.bfloat16)
        stores.append(pltpu.make_async_copy(result.at[turn_index], out_hbm.at[:, at], sent.at[turn_index]))
        stores[-1].start()
    for store in stores:
        store.wait()


def finish(mine, others, small, pick, base, weights):
    return pl.pallas_call(
        finish_kernel,
        out_shape=shape(RCV_DEV, D),
        in_specs=vmem(10) + anywhere(9),
        out_specs=anywhere(1)[0],
        scratch_shapes=[pltpu.VMEM((RCV_DEV, D), jnp.bfloat16)] * 2
        + [
            pltpu.VMEM((4, D, HALF // 2), jnp.bfloat16),
            pltpu.VMEM((RCV_DEV, D), jnp.bfloat16),
            pltpu.VMEM((4, RCV_DEV, HALF // 2), jnp.bfloat16),
            pltpu.SemaphoreType.DMA((9,)),
            pltpu.SemaphoreType.DMA((4,)),
        ],
        compiler_params=limits(28),
        cost_estimate=COST,
        name="finish",
    )(*mine, *others, small, pick, base, *weights)


def hyper_shards(
    frames, lengths, destination, offsets, norm_gain, weight_in, depth_kernel, post_gain, weight_out
):
    low = lax.axis_index("core") == 0
    per = weight_in.shape[0]

    rows = frames[0]
    up, down = cut(lengths, destination, offsets, rows)
    left = beside(weight_in[:, 0:HALF], weight_in[:, D : D + HALF], weight_out[:, 0:HALF])
    right = beside(weight_in[:, HALF:D], weight_in[:, D + HALF :], weight_out[:, HALF:])
    kept, given = jnp.where(low, left, right), jnp.where(low, right, left)
    got = hop(given, "c")
    chip = jnp.where(low, stack(kept, got), stack(got, kept))
    chip, up, down = tie(chip, up, down)

    notes = jnp.concatenate(
        [depth_kernel.T, norm_gain[None], post_gain[None], jnp.zeros((SMALL - KERNEL - 2, per), jnp.bfloat16)], 0
    )
    blank = jnp.zeros_like(notes)
    notes = jnp.where(low, beside(notes, blank), beside(blank, notes))
    notes = notes + hop(notes, "c")

    def span(which):
        if which >= 4:
            return [chip[:, 2 * HALF + (which - 4) * 2 * PART : 2 * HALF + (which - 3) * 2 * PART]]
        return [chip[:, gate + which * PART : gate + (which + 1) * PART] for gate in (0, HALF)]

    def streams(*which):
        return beside(*[piece for one in which for piece in span(one)])

    def wide(notes, name):
        return beside(notes, hop(notes, name))

    size = 2 * PART

    prev, next_ = turn(up, 1), turn(down, -1)
    one, two = streams(0, 5, 2), streams(3, 4, 1)
    one_far, two_far = hop(one, "z1"), hop(two, "z2")
    one, two, notes = tie(stack(one, one_far), stack(two, two_far), wide(notes, NOTES[0]))

    in1_out2, in3, in4_out1, in2 = one[:, 0 : 2 * size], one[:, 2 * size :], two[:, 0 : 2 * size], two[:, 2 * size :]
    far = [hop(in3, "z2"), hop(in4_out1, "x"), hop(in2, "z1")]
    in1_out2, notes, prev, next_ = tie(in1_out2, notes, prev, next_)
    far = [hop(in1_out2, "y")] + far
    in1_out2, in3, in4_out1, in2, notes = tie(
        stack(in1_out2, far[0]), stack(in3, far[1]), stack(in4_out1, far[2]), stack(in2, far[3]), wide(wide(notes, NOTES[1]), NOTES[2])
    )
    spread, base, pick = place(lengths, destination, offsets, rows, (prev, next_))

    in1, in4 = in1_out2[:, 0:size], in4_out1[:, 0:size]
    in3_out2, in2_out1 = beside(in3, in1_out2[:, size:]), beside(in2, in4_out1[:, size:])
    far = hop(in1, "z2"), hop(in3_out2, "x"), hop(in2_out1, "y"), hop(in4, "z1")
    in1, in3_out2, in2_out1, in4, notes, spread, base, pick = tie(
        stack(in1, far[0]), stack(in3_out2, far[1]), stack(in2_out1, far[2]), stack(in4, far[3]), wide(notes, NOTES[3]),
        spread, base, pick,
    )

    in2, out1, in3, out2 = in2_out1[:, 0:size], in2_out1[:, size:], in3_out2[:, 0:size], in3_out2[:, size:]
    out1_far, out2_far = hop(out1, "z1"), hop(out2, "z2")
    in1_far, in3_far = hop(in1, "x"), hop(in3, "y")
    n1, n2, n3, n4, small = prep(spread, hop(spread, "c"), notes)
    part1, part2, part3, part4 = early(n1, in1), early(n2, in2), early(n3, in3), early(n4, in4)
    in2, in4, small, part1, part2, part3, part4 = tie(in2, in4, small, part1, part2, part3, part4)
    in2_far, in4_far = hop(in2, "x"), hop(in4, "y")

    def run(normed, which, part, far):
        mine, given_part = conv(which * PART // LANE, normed, part, far, small)
        return mine, hop(given_part, "c")

    m0, o0 = run(n1, 0, part1, in1_far)
    m2, o2 = run(n3, 2, part3, in3_far)
    out1, out2, out1_far, out2_far, in2_far, in4_far, m0, o0, m2, o2 = tie(
        out1, out2, out1_far, out2_far, in2_far, in4_far, m0, o0, m2, o2
    )
    weights = [out1, out1_far, out2, out2_far]
    weights = weights + [hop(array, "c") for array in weights]
    m1, o1 = run(n2, 1, part2, in2_far)
    m3, o3 = run(n4, 3, part4, in4_far)
    mixed = finish((m0, m1, m2, m3), (o0, o1, o2, o3), small, pick, base, weights)
    return mixed[None]


def solution(mesh):
    if dict(mesh.shape) == {"dp": 8, "group": 4}:
        grid = jax.sharding.Mesh(mesh.devices.reshape(4, 2, 2, 2), ("z", "y", "x", "core"))
        dp, group, body = ("z", "y"), ("x", "core"), hyper_shards
    else:
        grid, dp, group, body = mesh, ("dp",), ("group",), shards
    every = dp + group
    placed = (
        P(group, dp, None),
        P(group, dp),
        P(group, dp),
        P(group, dp),
        P(every),
        P(every, None),
        P(every, None),
        P(every),
        P(every, None),
    )
    return jax.shard_map(
        body, mesh=grid, in_specs=placed, out_specs=P(group, dp, None), check_vma=False
    )
```

```python
import functools

import jax
import jax.numpy as jnp
from jax import lax
from jax.experimental import pallas as pl
from jax.experimental.pallas import tpu as pltpu
from jax.sharding import PartitionSpec as P

D = 2048
KERNEL = 32
MAXLEN = 192
RCV_DEV = 384


epsilon = 1e-05


def shifted(array, axis, by):
    peers = lax.axis_size(axis)
    return lax.ppermute(array, axis, [(i, (i + by) % peers) for i in range(peers)])


def layer_norm(values, scale_gain):
    center = values - jnp.mean(values, axis=-1, keepdims=True)
    spread = jnp.mean(center * center, axis=-1, keepdims=True)
    return center * lax.rsqrt(spread + epsilon) * scale_gain.astype(jnp.float32)


def depth_pass(gated_rows, segment, depth_kernel):
    row_count = gated_rows.shape[0]
    margin = KERNEL // 2
    padded = jnp.pad(gated_rows, ((margin, margin), (0, 0)))
    labels = jnp.pad(segment, (margin, margin), constant_values=-1)
    kernel_rows = depth_kernel.astype(jnp.float32)
    depthwise = jnp.zeros_like(gated_rows)
    for column in range(KERNEL):
        inside = (labels[column : column + row_count] == segment)[:, None]
        depthwise = (
            depthwise
            + jnp.where(inside, padded[column : column + row_count], 0.0) * kernel_rows[:, column]
        )
    return depthwise


def conv_module(inputs, segment, params):
    norm_gain, weight_in, depth_kernel, post_gain, weight_out = params
    widths = inputs.shape[1]
    source = inputs.astype(jnp.float32)
    normed = layer_norm(source, norm_gain).astype(jnp.bfloat16)
    projected = jnp.dot(normed, weight_in, preferred_element_type=jnp.float32)
    gated_rows = projected[:, :widths] * jax.nn.sigmoid(projected[:, widths:])
    depthwise = depth_pass(gated_rows, segment, depth_kernel)
    normed_post = layer_norm(depthwise, post_gain)
    active = (normed_post * jax.nn.sigmoid(normed_post)).astype(jnp.bfloat16)
    return (source + jnp.dot(active, weight_out, preferred_element_type=jnp.float32)).astype(
        jnp.bfloat16
    )


def relocate(own_part, next_part, prev_part):
    from_prev = shifted((next_part[0], next_part[1]), "dp", 1)
    from_next = shifted((prev_part[0], prev_part[1]), "dp", -1)
    received = jnp.zeros((RCV_DEV + MAXLEN, D), jnp.bfloat16)
    segment = jnp.zeros((RCV_DEV,), jnp.int32)
    position = jnp.arange(RCV_DEV, dtype=jnp.int32)
    arrivals = (own_part, from_prev, from_next)
    for label_id in range(3):
        frame_rows, meta_data = arrivals[label_id]
        current = lax.dynamic_slice_in_dim(received, meta_data[1], MAXLEN, 0)
        received = lax.dynamic_update_slice_in_dim(received, current + frame_rows, meta_data[1], 0)
        inside = (position >= meta_data[1]) & (position < meta_data[1] + meta_data[0])
        segment = jnp.where(inside, label_id + 1, segment)
    return (received[:RCV_DEV], segment)


def shards(
    frames, lengths, destination, offsets, norm_gain, weight_in, depth_kernel, post_gain, weight_out
):
    dp_count = lax.axis_size("dp")
    params = (
        lax.all_gather(norm_gain, ("dp", "group"), axis=0, tiled=True),
        lax.all_gather(weight_in, ("dp", "group"), axis=0, tiled=True),
        lax.all_gather(depth_kernel, ("dp", "group"), axis=0, tiled=True),
        lax.all_gather(post_gain, ("dp", "group"), axis=0, tiled=True),
        lax.all_gather(weight_out, ("dp", "group"), axis=0, tiled=True),
    )
    my_index = lax.axis_index("dp")
    local_frames = frames[0]
    lengths_here = lengths[0]
    dest_here = destination[0]
    offsets_here = offsets[0]
    starts = jnp.cumsum(lengths_here) - lengths_here
    relative = (dest_here - my_index) % dp_count
    slot_ids = jnp.arange(3, dtype=jnp.int32)

    def pick_entry(values, which):
        return jnp.sum(jnp.where(slot_ids == which, values, 0))

    def slot_of(code):
        return jnp.sum(jnp.where(relative == code, slot_ids, 0))

    chosen = (slot_of(0), slot_of(1), slot_of(dp_count - 1))

    def cut_utterance(source_rows, which):
        start_row = pick_entry(starts, which)
        live_count = pick_entry(lengths_here, which)
        frame_rows = lax.dynamic_slice_in_dim(source_rows, start_row, MAXLEN, 0)
        keep_rows = jnp.arange(MAXLEN, dtype=jnp.int32) < live_count
        kept = jnp.where(keep_rows[:, None], frame_rows, jnp.zeros_like(frame_rows))
        return (kept, jnp.stack([live_count, pick_entry(offsets_here, which)]))

    received, segment = relocate(
        cut_utterance(local_frames, chosen[0]),
        cut_utterance(local_frames, chosen[1]),
        cut_utterance(local_frames, chosen[2]),
    )
    mixed = conv_module(received, segment, params)
    return mixed[None]


SWAP = ((0, 1), (1, 0))
HOPS = {
    "c": ("core", SWAP),
    "x": ("x", SWAP),
    "y": ("y", SWAP),
    "z1": ("z", tuple((i, i ^ 1) for i in range(4))),
    "z2": ("z", tuple((i, i ^ 2) for i in range(4))),
}
GAP = KERNEL // 2
PAD = RCV_DEV + 4 * GAP
PAIR = 2 * PAD
LANE = 128
BLOCKS = D // LANE
HALF = D // 2
PART = 256
IN1, IN2 = ("z1", "y", "z2", "x"), ("z2", "z1", "y", "x")
IN3, IN4 = ("z1", "z2", "x", "y"), ("z2", "x", "z1", "y")
OUT1, OUT2 = ("z2", "x", "y", "z1"), ("z1", "y", "x", "z2")
NOTES = ("z1", "z2", "y", "x")
SMALL = 48
TILE = 64


def hop(array, name):
    axis, pairs = HOPS[name]
    return lax.ppermute(array, axis, pairs)


def turn(array, by):
    return lax.ppermute(array, ("z", "y"), [(i, (i + by) % 8) for i in range(8)])


def stack(first, second):
    return jnp.concatenate([first, second], 0)


def beside(*parts):
    return jnp.concatenate(parts, 1)


def tie(*arrays):
    return list(lax.optimization_barrier(arrays))


def coordinates():
    return [lax.axis_index(name) for name in ("z", "y", "x", "core")]


def spot(order, block):
    z, y, x, _ = coordinates()
    bit = {"z2": (block >> 3) ^ (z >> 1), "z1": ((block >> 2) & 1) ^ (z & 1), "y": ((block >> 1) & 1) ^ y, "x": (block & 1) ^ x}
    return sum(bit[name] << place for place, name in enumerate(order))


def lanes(index):
    return pl.ds(pl.multiple_of(index * LANE, LANE), LANE)


COST = pl.CostEstimate(flops=2**20, bytes_accessed=2**16, transcendentals=0)


def local(lens, dest, offs, code):
    z, y, _, _ = coordinates()
    count, offset, start, before = 0, 0, 0, 0
    for slot in range(3):
        match = (dest[0, slot] - (z * 2 + y) + 8) % 8 == code
        count = jnp.where(match, lens[0, slot], count)
        offset = jnp.where(match, offs[0, slot], offset)
        start = jnp.where(match, before, start)
        before = before + lens[0, slot]
    return count, offset, start


def hot(condition):
    return jnp.where(condition, 1.0, 0.0).astype(jnp.bfloat16)


def take(picker, rows):
    return jnp.dot(picker, rows, preferred_element_type=jnp.float32)


def grid_of(rows, columns):
    shape = (rows, columns)
    return lax.broadcasted_iota(jnp.int32, shape, 0), lax.broadcasted_iota(jnp.int32, shape, 1)


def cut_kernel(lens, dest, offs, rows_ref, notes_ref, up_ref, down_ref, out_ref):
    row, lane = grid_of(SMALL, LANE)
    slot = lane - lax.axis_index("core") * (LANE // 2)
    notes = notes_ref[...].astype(jnp.float32)
    for which in range(3):
        facts = (lens[0, which], dest[0, which], offs[0, which] // 2, offs[0, which] % 2)
        for place, fact in enumerate(facts):
            here = (slot == which) & (row == KERNEL + 2 + place)
            notes = jnp.where(here, fact.astype(jnp.float32), notes)
    out_ref[...] = notes.astype(jnp.bfloat16)
    for code, sent_ref in ((1, up_ref), (7, down_ref)):
        count, _, start = local(lens, dest, offs, code)
        step, slot = grid_of(MAXLEN, rows_ref.shape[0])
        picker = hot((slot == start + step) & (step < count))
        sent_ref[...] = take(picker, rows_ref[...]).astype(jnp.bfloat16)


def smem(count):
    return [pl.BlockSpec(memory_space=pltpu.SMEM)] * count


def vmem(count):
    return [pl.BlockSpec(memory_space=pltpu.VMEM)] * count


def anywhere(count):
    return [pl.BlockSpec(memory_space=pl.ANY)] * count


def shape(rows, columns, dtype=jnp.bfloat16):
    return jax.ShapeDtypeStruct((rows, columns), dtype)


def limits(mebibytes):
    return pltpu.CompilerParams(vmem_limit_bytes=mebibytes * 2**20)


def cut(lens, dest, offs, rows, notes):
    sent = shape(MAXLEN, D)
    return pl.pallas_call(
        cut_kernel,
        out_shape=(sent, sent, shape(SMALL, LANE)),
        in_specs=smem(3) + vmem(2),
        out_specs=tuple(vmem(3)),
        compiler_params=limits(16),
        cost_estimate=COST,
        name="cut",
    )(lens, dest, offs, rows, notes)


def place_kernel(lens, dest, offs, rows_ref, prev_ref, next_ref, notes_ref, spread_ref, base_ref, pick_ref):
    count, offset, start = local(lens, dest, offs, 0)
    z, y, x, core = coordinates()
    here = z * 2 + y
    ones = jnp.ones((1, 1), jnp.int32)

    def noted(place):
        block = (place >> 1) * 4 + (place & 1) * 2 + x
        note = notes_ref[32:SMALL, lanes(spot(NOTES[0:3], block))].astype(jnp.float32)
        _, lane = grid_of(1, LANE)
        slot = lane - core * (LANE // 2)
        ours = (slot >= 0) & (slot < 3) & (note[3:4].astype(jnp.int32) == here)

        def chosen(row):
            found = jnp.sum(jnp.where(ours, note[row : row + 1], 0.0), axis=-1, keepdims=True)
            return found.astype(jnp.int32)

        return chosen(2), chosen(4) * 2 + chosen(5)

    parts = [(count * ones, offset * ones), noted((here + 7) & 7), noted((here + 1) & 7)]

    def placer(which, width, first):
        mine = parts[which]
        rank = sum((other[1] < mine[1]).astype(jnp.int32) for other in parts)
        step, slot = grid_of(PAD, width)
        source = slot - first
        inside = (source >= 0) & (source < mine[0])
        return hot((step == GAP + mine[1] + GAP * rank + source) & inside)

    from_own = placer(0, rows_ref.shape[0], start)
    from_prev = placer(1, MAXLEN, 0)
    from_next = placer(2, MAXLEN, 0)
    found = take(from_own, rows_ref[...]) + take(from_prev, prev_ref[...]) + take(from_next, next_ref[...])
    spread_ref[...] = found.astype(jnp.bfloat16)
    flat, step = grid_of(RCV_DEV, PAD)
    rank = sum((part[1] <= flat).astype(jnp.int32) for part in parts)
    pick = hot(step == flat + GAP * rank)
    pick_ref[...] = pick
    base_ref[...] = take(pick, spread_ref[...]).astype(jnp.bfloat16)


def place(lens, dest, offs, rows, prev, next_, notes):
    return pl.pallas_call(
        place_kernel,
        out_shape=(shape(PAD, D), shape(RCV_DEV, D), shape(RCV_DEV, PAD)),
        in_specs=smem(3) + vmem(4),
        out_specs=tuple(vmem(3)),
        compiler_params=limits(24),
        cost_estimate=COST,
        name="place",
    )(lens, dest, offs, rows, prev, next_, notes)


def prep_kernel(mine_ref, other_ref, notes_ref, out1, out2, out3, out4, small_ref):
    for block in range(BLOCKS):
        tile = notes_ref[:, lanes(spot(NOTES, block))]
        small_ref[:, block * LANE : (block + 1) * LANE] = tile.astype(jnp.float32)
    for base, rows_ref in ((0, mine_ref), (PAD, other_ref)):

        def one(step, carry):
            values = rows_ref[pl.ds(pl.multiple_of(step * TILE, TILE), TILE), :].astype(jnp.float32)
            center = values - jnp.mean(values, axis=-1, keepdims=True)
            spread = jnp.mean(center * center, axis=-1, keepdims=True)
            scaled = center * lax.rsqrt(spread + epsilon) * small_ref[KERNEL : KERNEL + 1, :]
            scaled = scaled.astype(jnp.bfloat16)
            at = pl.ds(pl.multiple_of(base + step * TILE, TILE), TILE)
            for block in range(BLOCKS):
                part = scaled[:, block * LANE : (block + 1) * LANE]
                for order, out_ref in ((IN1, out1), (IN2, out2), (IN3, out3), (IN4, out4)):
                    place = spot(order, block)
                    out_ref[place >> 3, at, lanes(place & 7)] = part
            return carry

        lax.fori_loop(0, PAD // TILE, one, 0)


def prep(mine, other, notes):
    return pl.pallas_call(
        prep_kernel,
        out_shape=(jax.ShapeDtypeStruct((2, PAIR, HALF), jnp.bfloat16),) * 4 + (shape(SMALL, D, jnp.float32),),
        in_specs=vmem(3),
        out_specs=tuple(vmem(5)),
        compiler_params=limits(28),
        cost_estimate=COST,
        name="prep",
    )(mine, other, notes)


def early_kernel(rows_hbm, near_ref, out_ref, rows_ref, done):
    load = pltpu.make_async_copy(rows_hbm.at[0], rows_ref, done)
    load.start()
    load.wait()
    out_ref[...] = take(rows_ref[...], near_ref[...])


def early(rows, near):
    return pl.pallas_call(
        early_kernel,
        out_shape=shape(PAIR, near.shape[1], jnp.float32),
        in_specs=anywhere(1) + vmem(1),
        out_specs=vmem(1)[0],
        scratch_shapes=[pltpu.VMEM((PAIR, HALF), jnp.bfloat16), pltpu.SemaphoreType.DMA],
        compiler_params=limits(12),
        cost_estimate=COST,
        name="early",
    )(rows, near)


def conv_kernel(sub, rows_hbm, part_hbm, far_hbm, small_ref, own_ref, other_ref, gated, taps, rows_ref, part_ref, far_ref, done):
    width = own_ref.shape[1]
    tiles = width // LANE
    loads = [
        pltpu.make_async_copy(rows_hbm.at[1], rows_ref, done.at[0]),
        pltpu.make_async_copy(far_hbm, far_ref, done.at[1]),
        pltpu.make_async_copy(part_hbm, part_ref, done.at[2]),
    ]
    for load in loads:
        load.start()
    half = lax.axis_index("core")
    for tile in range(tiles):
        gated[tile, 0:GAP, :] = jnp.zeros((GAP, LANE), jnp.float32)
        gated[tile, GAP + PAIR : 2 * GAP + PAIR, :] = jnp.zeros((GAP, LANE), jnp.float32)
        taps[tile] = small_ref[0:KERNEL, lanes(half * (BLOCKS // 2) + sub + tile)]
    for load in loads:
        load.wait()
    both = part_ref[...] + take(rows_ref[...], far_ref[...])
    mixed = both[:, 0:width] * jax.nn.sigmoid(both[:, width:])
    for tile in range(tiles):
        gated[tile, GAP : GAP + PAIR, :] = mixed[:, tile * LANE : (tile + 1) * LANE]

    def slide(out_ref, base):
        def one(step, carry):
            for tile in range(tiles):
                total = jnp.zeros((TILE, LANE), jnp.float32)
                for tap in range(KERNEL):
                    window = gated[tile, pl.ds(base + step * TILE + tap, TILE), :]
                    total = total + window * taps[tile, tap : tap + 1, :]
                at = pl.ds(pl.multiple_of(step * TILE, TILE), TILE)
                out_ref[at, tile * LANE : (tile + 1) * LANE] = total.astype(jnp.bfloat16)
            return carry

        lax.fori_loop(0, PAD // TILE, one, 0)

    slide(own_ref, 0)
    slide(other_ref, PAD)


def conv(sub, rows, part, far, small):
    width = far.shape[1] // 2
    out = shape(PAD, width)
    return pl.pallas_call(
        functools.partial(conv_kernel, sub),
        out_shape=(out, out),
        in_specs=anywhere(3) + vmem(1),
        out_specs=tuple(vmem(2)),
        scratch_shapes=[
            pltpu.VMEM((width // LANE, PAIR + 2 * GAP, LANE), jnp.float32),
            pltpu.VMEM((width // LANE, KERNEL, LANE), jnp.float32),
            pltpu.VMEM((PAIR, HALF), jnp.bfloat16),
            pltpu.VMEM(part.shape, part.dtype),
            pltpu.VMEM(far.shape, far.dtype),
            pltpu.SemaphoreType.DMA((3,)),
        ],
        compiler_params=limits(16),
        cost_estimate=COST,
        name="conv",
    )(rows, part, far, small)


def finish_kernel(
    m0, m1, m2, m3, o0, o1, o2, o3, small_ref, pick_ref, base_hbm,
    e8, er, d8, dr, f8, fr, g8, gr, out_hbm, first, second, weights, base, result, done, sent,
):
    sources = (e8, er, d8, dr, f8, fr, g8, gr)
    loads = [
        pltpu.make_async_copy(
            source, weights.at[index // 2, pl.ds(index % 2 * HALF, HALF), :], done.at[index]
        )
        for index, source in enumerate(sources)
    ]
    loads.append(pltpu.make_async_copy(base_hbm, base, done.at[len(sources)]))
    for load in loads:
        load.start()
    half = lax.axis_index("core")
    pieces = []
    for side, group in ((half, (m0, m1, m2, m3)), (1 - half, (o0, o1, o2, o3))):
        block = side * (BLOCKS // 2)
        for ref in group:
            for tile in range(ref.shape[1] // LANE):
                pieces.append((block, ref[:, tile * LANE : (tile + 1) * LANE].astype(jnp.float32)))
                block = block + 1
    mean = jnp.sum(sum(values for _, values in pieces), axis=-1, keepdims=True) / D
    total = jnp.zeros((PAD, LANE), jnp.float32)
    for _, values in pieces:
        center = values - mean
        total = total + center * center
    scale = lax.rsqrt(jnp.sum(total, axis=-1, keepdims=True) / D + epsilon)
    for place in range(0, BLOCKS, 2):
        parts = []
        for block, values in pieces[place : place + 2]:
            gain = small_ref[KERNEL + 1 : KERNEL + 2, lanes(block)]
            post = (values - mean) * scale * gain
            parts.append((post * jax.nn.sigmoid(post)).astype(jnp.bfloat16))
        kept = take(pick_ref[...], beside(*parts)).astype(jnp.bfloat16)
        for tile, (block, _) in enumerate(pieces[place : place + 2]):
            part = kept[:, tile * LANE : (tile + 1) * LANE]
            first[:, lanes(spot(OUT1, block))] = part
            second[:, lanes(spot(OUT2, block))] = part
    width = HALF // 2
    loads[len(sources)].wait()
    stores = []
    for turn_index, (side, active, edge) in enumerate(
        ((half, first, 0), (half, second, width), (1 - half, first, 0), (1 - half, second, width))
    ):
        at = pl.ds(pl.multiple_of(side * HALF + edge, width), width)
        loads[2 * turn_index].wait()
        loads[2 * turn_index + 1].wait()
        mixed = take(active[...], weights[turn_index]) + base[:, at].astype(jnp.float32)
        result[turn_index] = mixed.astype(jnp.bfloat16)
        stores.append(pltpu.make_async_copy(result.at[turn_index], out_hbm.at[:, at], sent.at[turn_index]))
        stores[-1].start()
    for store in stores:
        store.wait()


def finish(mine, others, small, pick, base, weights):
    return pl.pallas_call(
        finish_kernel,
        out_shape=shape(RCV_DEV, D),
        in_specs=vmem(10) + anywhere(9),
        out_specs=anywhere(1)[0],
        scratch_shapes=[pltpu.VMEM((RCV_DEV, D), jnp.bfloat16)] * 2
        + [
            pltpu.VMEM((4, D, HALF // 2), jnp.bfloat16),
            pltpu.VMEM((RCV_DEV, D), jnp.bfloat16),
            pltpu.VMEM((4, RCV_DEV, HALF // 2), jnp.bfloat16),
            pltpu.SemaphoreType.DMA((9,)),
            pltpu.SemaphoreType.DMA((4,)),
        ],
        compiler_params=limits(28),
        cost_estimate=COST,
        name="finish",
    )(*mine, *others, small, pick, base, *weights)


def hyper_shards(
    frames, lengths, destination, offsets, norm_gain, weight_in, depth_kernel, post_gain, weight_out
):
    low = lax.axis_index("core") == 0
    per = weight_in.shape[0]

    rows = frames[0]
    notes = jnp.concatenate(
        [depth_kernel.T, norm_gain[None], post_gain[None], jnp.zeros((SMALL - KERNEL - 2, per), jnp.bfloat16)], 0
    )
    blank = jnp.zeros_like(notes)
    notes = jnp.where(low, beside(notes, blank), beside(blank, notes))
    up, down, notes = cut(lengths, destination, offsets, rows, notes)
    left = beside(weight_in[:, 0:HALF], weight_in[:, D : D + HALF], weight_out[:, 0:HALF])
    right = beside(weight_in[:, HALF:D], weight_in[:, D + HALF :], weight_out[:, HALF:])
    kept, given = jnp.where(low, left, right), jnp.where(low, right, left)
    got = hop(given, "c")
    chip = jnp.where(low, stack(kept, got), stack(got, kept))
    chip, up, down = tie(chip, up, down)

    notes = notes + hop(notes, "c")

    def span(which):
        if which >= 4:
            return [chip[:, 2 * HALF + (which - 4) * 2 * PART : 2 * HALF + (which - 3) * 2 * PART]]
        return [chip[:, gate + which * PART : gate + (which + 1) * PART] for gate in (0, HALF)]

    def streams(*which):
        return beside(*[piece for one in which for piece in span(one)])

    def wide(notes, name):
        return beside(notes, hop(notes, name))

    size = 2 * PART

    prev, next_ = turn(up, 1), turn(down, -1)
    one, two = streams(0, 5, 2), streams(3, 4, 1)
    one_far, two_far = hop(one, "z1"), hop(two, "z2")
    one, two, notes = tie(stack(one, one_far), stack(two, two_far), wide(notes, NOTES[0]))

    in1_out2, in3, in4_out1, in2 = one[:, 0 : 2 * size], one[:, 2 * size :], two[:, 0 : 2 * size], two[:, 2 * size :]
    far = [hop(in3, "z2"), hop(in4_out1, "x"), hop(in2, "z1")]
    in1_out2, notes, prev, next_ = tie(in1_out2, notes, prev, next_)
    far = [hop(in1_out2, "y")] + far
    in1_out2, in3, in4_out1, in2, notes = tie(
        stack(in1_out2, far[0]), stack(in3, far[1]), stack(in4_out1, far[2]), stack(in2, far[3]), wide(wide(notes, NOTES[1]), NOTES[2])
    )
    spread, base, pick = place(lengths, destination, offsets, rows, prev, next_, notes)

    in1, in4 = in1_out2[:, 0:size], in4_out1[:, 0:size]
    in3_out2, in2_out1 = beside(in3, in1_out2[:, size:]), beside(in2, in4_out1[:, size:])
    far = hop(in1, "z2"), hop(in3_out2, "x"), hop(in2_out1, "y"), hop(in4, "z1")
    in1, in3_out2, in2_out1, in4, notes, spread, base, pick = tie(
        stack(in1, far[0]), stack(in3_out2, far[1]), stack(in2_out1, far[2]), stack(in4, far[3]), wide(notes, NOTES[3]),
        spread, base, pick,
    )

    in2, out1, in3, out2 = in2_out1[:, 0:size], in2_out1[:, size:], in3_out2[:, 0:size], in3_out2[:, size:]
    out1_far, out2_far = hop(out1, "z1"), hop(out2, "z2")
    in1_far, in3_far = hop(in1, "x"), hop(in3, "y")
    n1, n2, n3, n4, small = prep(spread, hop(spread, "c"), notes)
    part1, part2, part3, part4 = early(n1, in1), early(n2, in2), early(n3, in3), early(n4, in4)
    in2, in4, small, part1, part2, part3, part4 = tie(in2, in4, small, part1, part2, part3, part4)
    in2_far, in4_far = hop(in2, "x"), hop(in4, "y")

    def run(normed, which, part, far):
        mine, given_part = conv(which * PART // LANE, normed, part, far, small)
        return mine, hop(given_part, "c")

    m0, o0 = run(n1, 0, part1, in1_far)
    m2, o2 = run(n3, 2, part3, in3_far)
    out1, out2, out1_far, out2_far, in2_far, in4_far, m0, o0, m2, o2 = tie(
        out1, out2, out1_far, out2_far, in2_far, in4_far, m0, o0, m2, o2
    )
    weights = [out1, out1_far, out2, out2_far]
    weights = weights + [hop(array, "c") for array in weights]
    m1, o1 = run(n2, 1, part2, in2_far)
    m3, o3 = run(n4, 3, part4, in4_far)
    mixed = finish((m0, m1, m2, m3), (o0, o1, o2, o3), small, pick, base, weights)
    return mixed[None]


def solution(mesh):
    if dict(mesh.shape) == {"dp": 8, "group": 4}:
        grid = jax.sharding.Mesh(mesh.devices.reshape(4, 2, 2, 2), ("z", "y", "x", "core"))
        dp, group, body = ("z", "y"), ("x", "core"), hyper_shards
    else:
        grid, dp, group, body = mesh, ("dp",), ("group",), shards
    every = dp + group
    placed = (
        P(group, dp, None),
        P(group, dp),
        P(group, dp),
        P(group, dp),
        P(every),
        P(every, None),
        P(every, None),
        P(every),
        P(every, None),
    )
    return jax.shard_map(
        body, mesh=grid, in_specs=placed, out_specs=P(group, dp, None), check_vma=False
    )
```

```python
import functools

import jax
import jax.numpy as jnp
from jax import lax
from jax.experimental import pallas as pl
from jax.experimental.pallas import tpu as pltpu
from jax.sharding import PartitionSpec as P

D = 2048
KERNEL = 32
MAXLEN = 192
RCV_DEV = 384


epsilon = 1e-05


def shifted(array, axis, by):
    peers = lax.axis_size(axis)
    return lax.ppermute(array, axis, [(i, (i + by) % peers) for i in range(peers)])


def layer_norm(values, scale_gain):
    center = values - jnp.mean(values, axis=-1, keepdims=True)
    spread = jnp.mean(center * center, axis=-1, keepdims=True)
    return center * lax.rsqrt(spread + epsilon) * scale_gain.astype(jnp.float32)


def depth_pass(gated_rows, segment, depth_kernel):
    row_count = gated_rows.shape[0]
    margin = KERNEL // 2
    padded = jnp.pad(gated_rows, ((margin, margin), (0, 0)))
    labels = jnp.pad(segment, (margin, margin), constant_values=-1)
    kernel_rows = depth_kernel.astype(jnp.float32)
    depthwise = jnp.zeros_like(gated_rows)
    for column in range(KERNEL):
        inside = (labels[column : column + row_count] == segment)[:, None]
        depthwise = (
            depthwise
            + jnp.where(inside, padded[column : column + row_count], 0.0) * kernel_rows[:, column]
        )
    return depthwise


def conv_module(inputs, segment, params):
    norm_gain, weight_in, depth_kernel, post_gain, weight_out = params
    widths = inputs.shape[1]
    source = inputs.astype(jnp.float32)
    normed = layer_norm(source, norm_gain).astype(jnp.bfloat16)
    projected = jnp.dot(normed, weight_in, preferred_element_type=jnp.float32)
    gated_rows = projected[:, :widths] * jax.nn.sigmoid(projected[:, widths:])
    depthwise = depth_pass(gated_rows, segment, depth_kernel)
    normed_post = layer_norm(depthwise, post_gain)
    active = (normed_post * jax.nn.sigmoid(normed_post)).astype(jnp.bfloat16)
    return (source + jnp.dot(active, weight_out, preferred_element_type=jnp.float32)).astype(
        jnp.bfloat16
    )


def relocate(own_part, next_part, prev_part):
    from_prev = shifted((next_part[0], next_part[1]), "dp", 1)
    from_next = shifted((prev_part[0], prev_part[1]), "dp", -1)
    received = jnp.zeros((RCV_DEV + MAXLEN, D), jnp.bfloat16)
    segment = jnp.zeros((RCV_DEV,), jnp.int32)
    position = jnp.arange(RCV_DEV, dtype=jnp.int32)
    arrivals = (own_part, from_prev, from_next)
    for label_id in range(3):
        frame_rows, meta_data = arrivals[label_id]
        current = lax.dynamic_slice_in_dim(received, meta_data[1], MAXLEN, 0)
        received = lax.dynamic_update_slice_in_dim(received, current + frame_rows, meta_data[1], 0)
        inside = (position >= meta_data[1]) & (position < meta_data[1] + meta_data[0])
        segment = jnp.where(inside, label_id + 1, segment)
    return (received[:RCV_DEV], segment)


def shards(
    frames, lengths, destination, offsets, norm_gain, weight_in, depth_kernel, post_gain, weight_out
):
    dp_count = lax.axis_size("dp")
    params = (
        lax.all_gather(norm_gain, ("dp", "group"), axis=0, tiled=True),
        lax.all_gather(weight_in, ("dp", "group"), axis=0, tiled=True),
        lax.all_gather(depth_kernel, ("dp", "group"), axis=0, tiled=True),
        lax.all_gather(post_gain, ("dp", "group"), axis=0, tiled=True),
        lax.all_gather(weight_out, ("dp", "group"), axis=0, tiled=True),
    )
    my_index = lax.axis_index("dp")
    local_frames = frames[0]
    lengths_here = lengths[0]
    dest_here = destination[0]
    offsets_here = offsets[0]
    starts = jnp.cumsum(lengths_here) - lengths_here
    relative = (dest_here - my_index) % dp_count
    slot_ids = jnp.arange(3, dtype=jnp.int32)

    def pick_entry(values, which):
        return jnp.sum(jnp.where(slot_ids == which, values, 0))

    def slot_of(code):
        return jnp.sum(jnp.where(relative == code, slot_ids, 0))

    chosen = (slot_of(0), slot_of(1), slot_of(dp_count - 1))

    def cut_utterance(source_rows, which):
        start_row = pick_entry(starts, which)
        live_count = pick_entry(lengths_here, which)
        frame_rows = lax.dynamic_slice_in_dim(source_rows, start_row, MAXLEN, 0)
        keep_rows = jnp.arange(MAXLEN, dtype=jnp.int32) < live_count
        kept = jnp.where(keep_rows[:, None], frame_rows, jnp.zeros_like(frame_rows))
        return (kept, jnp.stack([live_count, pick_entry(offsets_here, which)]))

    received, segment = relocate(
        cut_utterance(local_frames, chosen[0]),
        cut_utterance(local_frames, chosen[1]),
        cut_utterance(local_frames, chosen[2]),
    )
    mixed = conv_module(received, segment, params)
    return mixed[None]


SWAP = ((0, 1), (1, 0))
HOPS = {
    "c": ("core", SWAP),
    "x": ("x", SWAP),
    "y": ("y", SWAP),
    "z1": ("z", tuple((i, i ^ 1) for i in range(4))),
    "z2": ("z", tuple((i, i ^ 2) for i in range(4))),
}
GAP = KERNEL // 2
PAD = RCV_DEV + 4 * GAP
PAIR = 2 * PAD
LANE = 128
BLOCKS = D // LANE
HALF = D // 2
PART = 256
IN1, IN2 = ("z1", "y", "z2", "x"), ("z2", "z1", "y", "x")
IN3, IN4 = ("z1", "z2", "x", "y"), ("z2", "x", "z1", "y")
OUT1, OUT2 = ("z2", "x", "y", "z1"), ("z1", "y", "x", "z2")
NOTES = ("z1", "z2", "y", "x")
SMALL = 48
TILE = 64


def hop(array, name):
    axis, pairs = HOPS[name]
    return lax.ppermute(array, axis, pairs)


def turn(array, by):
    return lax.ppermute(array, ("z", "y"), [(i, (i + by) % 8) for i in range(8)])


def stack(first, second):
    return jnp.concatenate([first, second], 0)


def beside(*parts):
    return jnp.concatenate(parts, 1)


def tie(*arrays):
    return list(lax.optimization_barrier(arrays))


def coordinates():
    return [lax.axis_index(name) for name in ("z", "y", "x", "core")]


def spot(order, block):
    z, y, x, _ = coordinates()
    bit = {"z2": (block >> 3) ^ (z >> 1), "z1": ((block >> 2) & 1) ^ (z & 1), "y": ((block >> 1) & 1) ^ y, "x": (block & 1) ^ x}
    return sum(bit[name] << place for place, name in enumerate(order))


def lanes(index):
    return pl.ds(pl.multiple_of(index * LANE, LANE), LANE)


COST = pl.CostEstimate(flops=2**20, bytes_accessed=2**16, transcendentals=0)


def local(lens, dest, offs, code):
    z, y, _, _ = coordinates()
    count, offset, start, before = 0, 0, 0, 0
    for slot in range(3):
        match = (dest[0, slot] - (z * 2 + y) + 8) % 8 == code
        count = jnp.where(match, lens[0, slot], count)
        offset = jnp.where(match, offs[0, slot], offset)
        start = jnp.where(match, before, start)
        before = before + lens[0, slot]
    return count, offset, start


def hot(condition):
    return jnp.where(condition, 1.0, 0.0).astype(jnp.bfloat16)


def take(picker, rows):
    return jnp.dot(picker, rows, preferred_element_type=jnp.float32)


def grid_of(rows, columns):
    shape = (rows, columns)
    return lax.broadcasted_iota(jnp.int32, shape, 0), lax.broadcasted_iota(jnp.int32, shape, 1)


def cut_kernel(lens, dest, offs, rows_ref, notes_ref, up_ref, down_ref, out_ref):
    row, lane = grid_of(SMALL, LANE)
    slot = lane - lax.axis_index("core") * (LANE // 2)
    notes = notes_ref[...].astype(jnp.float32)
    for which in range(3):
        facts = (lens[0, which], dest[0, which], offs[0, which] // 2, offs[0, which] % 2)
        for place, fact in enumerate(facts):
            here = (slot == which) & (row == KERNEL + 2 + place)
            notes = jnp.where(here, fact.astype(jnp.float32), notes)
    out_ref[...] = notes.astype(jnp.bfloat16)
    for code, sent_ref in ((1, up_ref), (7, down_ref)):
        count, _, start = local(lens, dest, offs, code)
        step, slot = grid_of(MAXLEN, rows_ref.shape[0])
        picker = hot((slot == start + step) & (step < count))
        sent_ref[...] = take(picker, rows_ref[...]).astype(jnp.bfloat16)


def smem(count):
    return [pl.BlockSpec(memory_space=pltpu.SMEM)] * count


def vmem(count):
    return [pl.BlockSpec(memory_space=pltpu.VMEM)] * count


def anywhere(count):
    return [pl.BlockSpec(memory_space=pl.ANY)] * count


def shape(rows, columns, dtype=jnp.bfloat16):
    return jax.ShapeDtypeStruct((rows, columns), dtype)


def limits(mebibytes):
    return pltpu.CompilerParams(vmem_limit_bytes=mebibytes * 2**20)


def cut(lens, dest, offs, rows, notes):
    sent = shape(MAXLEN, D)
    return pl.pallas_call(
        cut_kernel,
        out_shape=(sent, sent, shape(SMALL, LANE)),
        in_specs=smem(3) + vmem(2),
        out_specs=tuple(vmem(3)),
        compiler_params=limits(16),
        cost_estimate=COST,
        name="cut",
    )(lens, dest, offs, rows, notes)


def place_kernel(lens, dest, offs, rows_ref, prev_ref, next_ref, notes_ref, spread_ref, base_ref, pick_ref):
    count, offset, start = local(lens, dest, offs, 0)
    z, y, x, core = coordinates()
    here = z * 2 + y
    ones = jnp.ones((1, 1), jnp.int32)

    def noted(place):
        block = (place >> 1) * 4 + (place & 1) * 2 + x
        note = notes_ref[32:SMALL, lanes(spot(NOTES[0:3], block))].astype(jnp.float32)
        _, lane = grid_of(1, LANE)
        slot = lane - core * (LANE // 2)
        ours = (slot >= 0) & (slot < 3) & (note[3:4].astype(jnp.int32) == here)

        def chosen(row):
            found = jnp.sum(jnp.where(ours, note[row : row + 1], 0.0), axis=-1, keepdims=True)
            return found.astype(jnp.int32)

        return chosen(2), chosen(4) * 2 + chosen(5)

    parts = [(count * ones, offset * ones), noted((here + 7) & 7), noted((here + 1) & 7)]

    def placer(which, width, first):
        mine = parts[which]
        rank = sum((other[1] < mine[1]).astype(jnp.int32) for other in parts)
        step, slot = grid_of(PAD, width)
        source = slot - first
        inside = (source >= 0) & (source < mine[0])
        return hot((step == GAP + mine[1] + GAP * rank + source) & inside)

    from_own = placer(0, rows_ref.shape[0], start)
    from_prev = placer(1, MAXLEN, 0)
    from_next = placer(2, MAXLEN, 0)
    found = take(from_own, rows_ref[...]) + take(from_prev, prev_ref[...]) + take(from_next, next_ref[...])
    spread_ref[...] = found.astype(jnp.bfloat16)
    flat, step = grid_of(RCV_DEV, PAD)
    rank = sum((part[1] <= flat).astype(jnp.int32) for part in parts)
    pick = hot(step == flat + GAP * rank)
    pick_ref[...] = pick
    base_ref[...] = take(pick, spread_ref[...]).astype(jnp.bfloat16)


def place(lens, dest, offs, rows, prev, next_, notes):
    return pl.pallas_call(
        place_kernel,
        out_shape=(shape(PAD, D), shape(RCV_DEV, D), shape(RCV_DEV, PAD)),
        in_specs=smem(3) + vmem(4),
        out_specs=tuple(vmem(3)),
        compiler_params=limits(24),
        cost_estimate=COST,
        name="place",
    )(lens, dest, offs, rows, prev, next_, notes)


def prep_kernel(mine_ref, other_ref, notes_ref, out1, out2, out3, out4, small_ref):
    for block in range(BLOCKS):
        tile = notes_ref[:, lanes(spot(NOTES, block))]
        small_ref[:, block * LANE : (block + 1) * LANE] = tile.astype(jnp.float32)
    for base, rows_ref in ((0, mine_ref), (PAD, other_ref)):

        def one(step, carry):
            values = rows_ref[pl.ds(pl.multiple_of(step * TILE, TILE), TILE), :].astype(jnp.float32)
            center = values - jnp.mean(values, axis=-1, keepdims=True)
            spread = jnp.mean(center * center, axis=-1, keepdims=True)
            scaled = center * lax.rsqrt(spread + epsilon) * small_ref[KERNEL : KERNEL + 1, :]
            scaled = scaled.astype(jnp.bfloat16)
            at = pl.ds(pl.multiple_of(base + step * TILE, TILE), TILE)
            for block in range(BLOCKS):
                part = scaled[:, block * LANE : (block + 1) * LANE]
                for order, out_ref in ((IN1, out1), (IN2, out2), (IN3, out3), (IN4, out4)):
                    place = spot(order, block)
                    out_ref[place >> 3, at, lanes(place & 7)] = part
            return carry

        lax.fori_loop(0, PAD // TILE, one, 0)


def prep(mine, other, notes):
    return pl.pallas_call(
        prep_kernel,
        out_shape=(jax.ShapeDtypeStruct((2, PAIR, HALF), jnp.bfloat16),) * 4 + (shape(SMALL, D, jnp.float32),),
        in_specs=vmem(3),
        out_specs=tuple(vmem(5)),
        compiler_params=limits(28),
        cost_estimate=COST,
        name="prep",
    )(mine, other, notes)


def early_kernel(rows_ref, near_ref, out_ref):
    out_ref[...] = take(rows_ref[0], near_ref[...])


def early(rows, near):
    return pl.pallas_call(
        early_kernel,
        out_shape=shape(PAIR, near.shape[1], jnp.float32),
        in_specs=vmem(2),
        out_specs=vmem(1)[0],
        compiler_params=limits(12),
        cost_estimate=COST,
        name="early",
    )(rows, near)


def conv_kernel(sub, rows_ref, part_ref, far_ref, small_ref, own_ref, other_ref, gated, taps):
    width = own_ref.shape[1]
    tiles = width // LANE
    half = lax.axis_index("core")
    for tile in range(tiles):
        gated[tile, 0:GAP, :] = jnp.zeros((GAP, LANE), jnp.float32)
        gated[tile, GAP + PAIR : 2 * GAP + PAIR, :] = jnp.zeros((GAP, LANE), jnp.float32)
        taps[tile] = small_ref[0:KERNEL, lanes(half * (BLOCKS // 2) + sub + tile)]
    both = part_ref[...] + take(rows_ref[1], far_ref[...])
    mixed = both[:, 0:width] * jax.nn.sigmoid(both[:, width:])
    for tile in range(tiles):
        gated[tile, GAP : GAP + PAIR, :] = mixed[:, tile * LANE : (tile + 1) * LANE]

    def slide(out_ref, base):
        def one(step, carry):
            for tile in range(tiles):
                total = jnp.zeros((TILE, LANE), jnp.float32)
                for tap in range(KERNEL):
                    window = gated[tile, pl.ds(base + step * TILE + tap, TILE), :]
                    total = total + window * taps[tile, tap : tap + 1, :]
                at = pl.ds(pl.multiple_of(step * TILE, TILE), TILE)
                out_ref[at, tile * LANE : (tile + 1) * LANE] = total.astype(jnp.bfloat16)
            return carry

        lax.fori_loop(0, PAD // TILE, one, 0)

    slide(own_ref, 0)
    slide(other_ref, PAD)


def conv(sub, rows, part, far, small):
    width = far.shape[1] // 2
    out = shape(PAD, width)
    return pl.pallas_call(
        functools.partial(conv_kernel, sub),
        out_shape=(out, out),
        in_specs=vmem(4),
        out_specs=tuple(vmem(2)),
        scratch_shapes=[
            pltpu.VMEM((width // LANE, PAIR + 2 * GAP, LANE), jnp.float32),
            pltpu.VMEM((width // LANE, KERNEL, LANE), jnp.float32),
        ],
        compiler_params=limits(16),
        cost_estimate=COST,
        name="conv",
    )(rows, part, far, small)


def finish_kernel(
    m0, m1, m2, m3, o0, o1, o2, o3, small_ref, pick_ref, base,
    e8, er, d8, dr, f8, fr, g8, gr, out_hbm, first, second, result, sent,
):
    sources = (e8, er, d8, dr, f8, fr, g8, gr)
    half = lax.axis_index("core")
    pieces = []
    for side, group in ((half, (m0, m1, m2, m3)), (1 - half, (o0, o1, o2, o3))):
        block = side * (BLOCKS // 2)
        for ref in group:
            for tile in range(ref.shape[1] // LANE):
                pieces.append((block, ref[:, tile * LANE : (tile + 1) * LANE].astype(jnp.float32)))
                block = block + 1
    mean = jnp.sum(sum(values for _, values in pieces), axis=-1, keepdims=True) / D
    total = jnp.zeros((PAD, LANE), jnp.float32)
    for _, values in pieces:
        center = values - mean
        total = total + center * center
    scale = lax.rsqrt(jnp.sum(total, axis=-1, keepdims=True) / D + epsilon)
    for place in range(0, BLOCKS, 2):
        parts = []
        for block, values in pieces[place : place + 2]:
            gain = small_ref[KERNEL + 1 : KERNEL + 2, lanes(block)]
            post = (values - mean) * scale * gain
            parts.append((post * jax.nn.sigmoid(post)).astype(jnp.bfloat16))
        kept = take(pick_ref[...], beside(*parts)).astype(jnp.bfloat16)
        for tile, (block, _) in enumerate(pieces[place : place + 2]):
            part = kept[:, tile * LANE : (tile + 1) * LANE]
            first[:, lanes(spot(OUT1, block))] = part
            second[:, lanes(spot(OUT2, block))] = part
    width = HALF // 2
    stores = []
    for turn_index, (side, active, edge) in enumerate(
        ((half, first, 0), (half, second, width), (1 - half, first, 0), (1 - half, second, width))
    ):
        at = pl.ds(pl.multiple_of(side * HALF + edge, width), width)
        near, far = sources[2 * turn_index], sources[2 * turn_index + 1]
        mixed = take(active[:, 0:HALF], near[...]) + take(active[:, HALF:D], far[...]) + base[:, at].astype(jnp.float32)
        result[turn_index] = mixed.astype(jnp.bfloat16)
        stores.append(pltpu.make_async_copy(result.at[turn_index], out_hbm.at[:, at], sent.at[turn_index]))
        stores[-1].start()
    for store in stores:
        store.wait()


def finish(mine, others, small, pick, base, weights):
    return pl.pallas_call(
        finish_kernel,
        out_shape=shape(RCV_DEV, D),
        in_specs=vmem(19),
        out_specs=anywhere(1)[0],
        scratch_shapes=[pltpu.VMEM((RCV_DEV, D), jnp.bfloat16)] * 2
        + [
            pltpu.VMEM((4, RCV_DEV, HALF // 2), jnp.bfloat16),
            pltpu.SemaphoreType.DMA((4,)),
        ],
        compiler_params=limits(28),
        cost_estimate=COST,
        name="finish",
    )(*mine, *others, small, pick, base, *weights)


def hyper_shards(
    frames, lengths, destination, offsets, norm_gain, weight_in, depth_kernel, post_gain, weight_out
):
    low = lax.axis_index("core") == 0
    per = weight_in.shape[0]

    rows = frames[0]
    notes = jnp.concatenate(
        [depth_kernel.T, norm_gain[None], post_gain[None], jnp.zeros((SMALL - KERNEL - 2, per), jnp.bfloat16)], 0
    )
    blank = jnp.zeros_like(notes)
    notes = jnp.where(low, beside(notes, blank), beside(blank, notes))
    up, down, notes = cut(lengths, destination, offsets, rows, notes)
    left = beside(weight_in[:, 0:HALF], weight_in[:, D : D + HALF], weight_out[:, 0:HALF])
    right = beside(weight_in[:, HALF:D], weight_in[:, D + HALF :], weight_out[:, HALF:])
    kept, given = jnp.where(low, left, right), jnp.where(low, right, left)
    got = hop(given, "c")
    chip = jnp.where(low, stack(kept, got), stack(got, kept))
    chip, up, down = tie(chip, up, down)

    notes = notes + hop(notes, "c")

    def span(which):
        if which >= 4:
            return [chip[:, 2 * HALF + (which - 4) * 2 * PART : 2 * HALF + (which - 3) * 2 * PART]]
        return [chip[:, gate + which * PART : gate + (which + 1) * PART] for gate in (0, HALF)]

    def streams(*which):
        return beside(*[piece for one in which for piece in span(one)])

    def wide(notes, name):
        return beside(notes, hop(notes, name))

    size = 2 * PART

    prev, next_ = turn(up, 1), turn(down, -1)
    one, two = streams(0, 5, 2), streams(3, 4, 1)
    one_far, two_far = hop(one, "z1"), hop(two, "z2")
    one, two, notes = tie(stack(one, one_far), stack(two, two_far), wide(notes, NOTES[0]))

    in1_out2, in3, in4_out1, in2 = one[:, 0 : 2 * size], one[:, 2 * size :], two[:, 0 : 2 * size], two[:, 2 * size :]
    far = [hop(in3, "z2"), hop(in4_out1, "x"), hop(in2, "z1")]
    in1_out2, notes, prev, next_ = tie(in1_out2, notes, prev, next_)
    far = [hop(in1_out2, "y")] + far
    in1_out2, in3, in4_out1, in2, notes = tie(
        stack(in1_out2, far[0]), stack(in3, far[1]), stack(in4_out1, far[2]), stack(in2, far[3]), wide(wide(notes, NOTES[1]), NOTES[2])
    )
    spread, base, pick = place(lengths, destination, offsets, rows, prev, next_, notes)

    in1, in4 = in1_out2[:, 0:size], in4_out1[:, 0:size]
    in3_out2, in2_out1 = beside(in3, in1_out2[:, size:]), beside(in2, in4_out1[:, size:])
    far = hop(in1, "z2"), hop(in3_out2, "x"), hop(in2_out1, "y"), hop(in4, "z1")
    in1, in3_out2, in2_out1, in4, notes, spread, base, pick = tie(
        stack(in1, far[0]), stack(in3_out2, far[1]), stack(in2_out1, far[2]), stack(in4, far[3]), wide(notes, NOTES[3]),
        spread, base, pick,
    )

    in2, out1, in3, out2 = in2_out1[:, 0:size], in2_out1[:, size:], in3_out2[:, 0:size], in3_out2[:, size:]
    out1_far, out2_far = hop(out1, "z1"), hop(out2, "z2")
    in1_far, in3_far = hop(in1, "x"), hop(in3, "y")
    n1, n2, n3, n4, small = prep(spread, hop(spread, "c"), notes)
    part1, part2, part3, part4 = early(n1, in1), early(n2, in2), early(n3, in3), early(n4, in4)
    in2, in4, small, part1, part2, part3, part4 = tie(in2, in4, small, part1, part2, part3, part4)
    in2_far, in4_far = hop(in2, "x"), hop(in4, "y")

    def run(normed, which, part, far):
        mine, given_part = conv(which * PART // LANE, normed, part, far, small)
        return mine, hop(given_part, "c")

    m0, o0 = run(n1, 0, part1, in1_far)
    m2, o2 = run(n3, 2, part3, in3_far)
    out1, out2, out1_far, out2_far, in2_far, in4_far, m0, o0, m2, o2 = tie(
        out1, out2, out1_far, out2_far, in2_far, in4_far, m0, o0, m2, o2
    )
    weights = [out1, out1_far, out2, out2_far]
    weights = weights + [hop(array, "c") for array in weights]
    m1, o1 = run(n2, 1, part2, in2_far)
    m3, o3 = run(n4, 3, part4, in4_far)
    mixed = finish((m0, m1, m2, m3), (o0, o1, o2, o3), small, pick, base, weights)
    return mixed[None]


def solution(mesh):
    if dict(mesh.shape) == {"dp": 8, "group": 4}:
        grid = jax.sharding.Mesh(mesh.devices.reshape(4, 2, 2, 2), ("z", "y", "x", "core"))
        dp, group, body = ("z", "y"), ("x", "core"), hyper_shards
    else:
        grid, dp, group, body = mesh, ("dp",), ("group",), shards
    every = dp + group
    placed = (
        P(group, dp, None),
        P(group, dp),
        P(group, dp),
        P(group, dp),
        P(every),
        P(every, None),
        P(every, None),
        P(every),
        P(every, None),
    )
    return jax.shard_map(
        body, mesh=grid, in_specs=placed, out_specs=P(group, dp, None), check_vma=False
    )
```

```python
import functools

import jax
import jax.numpy as jnp
from jax import lax
from jax.experimental import pallas as pl
from jax.experimental.pallas import tpu as pltpu
from jax.sharding import PartitionSpec as P

D = 2048
KERNEL = 32
MAXLEN = 192
RCV_DEV = 384


epsilon = 1e-05


def shifted(array, axis, by):
    peers = lax.axis_size(axis)
    return lax.ppermute(array, axis, [(i, (i + by) % peers) for i in range(peers)])


def layer_norm(values, scale_gain):
    center = values - jnp.mean(values, axis=-1, keepdims=True)
    spread = jnp.mean(center * center, axis=-1, keepdims=True)
    return center * lax.rsqrt(spread + epsilon) * scale_gain.astype(jnp.float32)


def depth_pass(gated_rows, segment, depth_kernel):
    row_count = gated_rows.shape[0]
    margin = KERNEL // 2
    padded = jnp.pad(gated_rows, ((margin, margin), (0, 0)))
    labels = jnp.pad(segment, (margin, margin), constant_values=-1)
    kernel_rows = depth_kernel.astype(jnp.float32)
    depthwise = jnp.zeros_like(gated_rows)
    for column in range(KERNEL):
        inside = (labels[column : column + row_count] == segment)[:, None]
        depthwise = (
            depthwise
            + jnp.where(inside, padded[column : column + row_count], 0.0) * kernel_rows[:, column]
        )
    return depthwise


def conv_module(inputs, segment, params):
    norm_gain, weight_in, depth_kernel, post_gain, weight_out = params
    widths = inputs.shape[1]
    source = inputs.astype(jnp.float32)
    normed = layer_norm(source, norm_gain).astype(jnp.bfloat16)
    projected = jnp.dot(normed, weight_in, preferred_element_type=jnp.float32)
    gated_rows = projected[:, :widths] * jax.nn.sigmoid(projected[:, widths:])
    depthwise = depth_pass(gated_rows, segment, depth_kernel)
    normed_post = layer_norm(depthwise, post_gain)
    active = (normed_post * jax.nn.sigmoid(normed_post)).astype(jnp.bfloat16)
    return (source + jnp.dot(active, weight_out, preferred_element_type=jnp.float32)).astype(
        jnp.bfloat16
    )


def relocate(own_part, next_part, prev_part):
    from_prev = shifted((next_part[0], next_part[1]), "dp", 1)
    from_next = shifted((prev_part[0], prev_part[1]), "dp", -1)
    received = jnp.zeros((RCV_DEV + MAXLEN, D), jnp.bfloat16)
    segment = jnp.zeros((RCV_DEV,), jnp.int32)
    position = jnp.arange(RCV_DEV, dtype=jnp.int32)
    arrivals = (own_part, from_prev, from_next)
    for label_id in range(3):
        frame_rows, meta_data = arrivals[label_id]
        current = lax.dynamic_slice_in_dim(received, meta_data[1], MAXLEN, 0)
        received = lax.dynamic_update_slice_in_dim(received, current + frame_rows, meta_data[1], 0)
        inside = (position >= meta_data[1]) & (position < meta_data[1] + meta_data[0])
        segment = jnp.where(inside, label_id + 1, segment)
    return (received[:RCV_DEV], segment)


def shards(
    frames, lengths, destination, offsets, norm_gain, weight_in, depth_kernel, post_gain, weight_out
):
    dp_count = lax.axis_size("dp")
    params = (
        lax.all_gather(norm_gain, ("dp", "group"), axis=0, tiled=True),
        lax.all_gather(weight_in, ("dp", "group"), axis=0, tiled=True),
        lax.all_gather(depth_kernel, ("dp", "group"), axis=0, tiled=True),
        lax.all_gather(post_gain, ("dp", "group"), axis=0, tiled=True),
        lax.all_gather(weight_out, ("dp", "group"), axis=0, tiled=True),
    )
    my_index = lax.axis_index("dp")
    local_frames = frames[0]
    lengths_here = lengths[0]
    dest_here = destination[0]
    offsets_here = offsets[0]
    starts = jnp.cumsum(lengths_here) - lengths_here
    relative = (dest_here - my_index) % dp_count
    slot_ids = jnp.arange(3, dtype=jnp.int32)

    def pick_entry(values, which):
        return jnp.sum(jnp.where(slot_ids == which, values, 0))

    def slot_of(code):
        return jnp.sum(jnp.where(relative == code, slot_ids, 0))

    chosen = (slot_of(0), slot_of(1), slot_of(dp_count - 1))

    def cut_utterance(source_rows, which):
        start_row = pick_entry(starts, which)
        live_count = pick_entry(lengths_here, which)
        frame_rows = lax.dynamic_slice_in_dim(source_rows, start_row, MAXLEN, 0)
        keep_rows = jnp.arange(MAXLEN, dtype=jnp.int32) < live_count
        kept = jnp.where(keep_rows[:, None], frame_rows, jnp.zeros_like(frame_rows))
        return (kept, jnp.stack([live_count, pick_entry(offsets_here, which)]))

    received, segment = relocate(
        cut_utterance(local_frames, chosen[0]),
        cut_utterance(local_frames, chosen[1]),
        cut_utterance(local_frames, chosen[2]),
    )
    mixed = conv_module(received, segment, params)
    return mixed[None]


SWAP = ((0, 1), (1, 0))
HOPS = {
    "c": ("core", SWAP),
    "x": ("x", SWAP),
    "y": ("y", SWAP),
    "z1": ("z", tuple((i, i ^ 1) for i in range(4))),
    "z2": ("z", tuple((i, i ^ 2) for i in range(4))),
}
GAP = KERNEL // 2
PAD = RCV_DEV + 4 * GAP
PAIR = 2 * PAD
LANE = 128
BLOCKS = D // LANE
HALF = D // 2
PART = 256
IN1, IN2 = ("z1", "y", "z2", "x"), ("z2", "z1", "y", "x")
IN3, IN4 = ("z1", "z2", "x", "y"), ("z2", "x", "z1", "y")
OUT1, OUT2 = ("z2", "x", "y", "z1"), ("z1", "y", "x", "z2")
NOTES = ("z1", "z2", "y", "x")
SMALL = 48
TILE = 64
SLIDE = 224


def hop(array, name):
    axis, pairs = HOPS[name]
    return lax.ppermute(array, axis, pairs)


def turn(array, by):
    return lax.ppermute(array, ("z", "y"), [(i, (i + by) % 8) for i in range(8)])


def stack(first, second):
    return jnp.concatenate([first, second], 0)


def beside(*parts):
    return jnp.concatenate(parts, 1)


def tie(*arrays):
    return list(lax.optimization_barrier(arrays))


def coordinates():
    return [lax.axis_index(name) for name in ("z", "y", "x", "core")]


def spot(order, block):
    z, y, x, _ = coordinates()
    bit = {"z2": (block >> 3) ^ (z >> 1), "z1": ((block >> 2) & 1) ^ (z & 1), "y": ((block >> 1) & 1) ^ y, "x": (block & 1) ^ x}
    return sum(bit[name] << place for place, name in enumerate(order))


def lanes(index):
    return pl.ds(pl.multiple_of(index * LANE, LANE), LANE)


COST = pl.CostEstimate(flops=2**20, bytes_accessed=2**16, transcendentals=0)


def local(lens, dest, offs, code):
    z, y, _, _ = coordinates()
    count, offset, start, before = 0, 0, 0, 0
    for slot in range(3):
        match = (dest[0, slot] - (z * 2 + y) + 8) % 8 == code
        count = jnp.where(match, lens[0, slot], count)
        offset = jnp.where(match, offs[0, slot], offset)
        start = jnp.where(match, before, start)
        before = before + lens[0, slot]
    return count, offset, start


def hot(condition):
    return jnp.where(condition, 1.0, 0.0).astype(jnp.bfloat16)


def take(picker, rows):
    return jnp.dot(picker, rows, preferred_element_type=jnp.float32)


def grid_of(rows, columns):
    shape = (rows, columns)
    return lax.broadcasted_iota(jnp.int32, shape, 0), lax.broadcasted_iota(jnp.int32, shape, 1)


def cut_kernel(lens, dest, offs, rows_ref, notes_ref, up_ref, down_ref, out_ref):
    row, lane = grid_of(SMALL, LANE)
    slot = lane - lax.axis_index("core") * (LANE // 2)
    notes = notes_ref[...].astype(jnp.float32)
    for which in range(3):
        facts = (lens[0, which], dest[0, which], offs[0, which] // 2, offs[0, which] % 2)
        for place, fact in enumerate(facts):
            here = (slot == which) & (row == KERNEL + 2 + place)
            notes = jnp.where(here, fact.astype(jnp.float32), notes)
    out_ref[...] = notes.astype(jnp.bfloat16)
    for code, sent_ref in ((1, up_ref), (7, down_ref)):
        count, _, start = local(lens, dest, offs, code)
        step, slot = grid_of(MAXLEN, rows_ref.shape[0])
        picker = hot((slot == start + step) & (step < count))
        sent_ref[...] = take(picker, rows_ref[...]).astype(jnp.bfloat16)


def smem(count):
    return [pl.BlockSpec(memory_space=pltpu.SMEM)] * count


def vmem(count):
    return [pl.BlockSpec(memory_space=pltpu.VMEM)] * count


def anywhere(count):
    return [pl.BlockSpec(memory_space=pl.ANY)] * count


def shape(rows, columns, dtype=jnp.bfloat16):
    return jax.ShapeDtypeStruct((rows, columns), dtype)


def limits(mebibytes):
    return pltpu.CompilerParams(vmem_limit_bytes=mebibytes * 2**20)


def cut(lens, dest, offs, rows, notes):
    sent = shape(MAXLEN, D)
    return pl.pallas_call(
        cut_kernel,
        out_shape=(sent, sent, shape(SMALL, LANE)),
        in_specs=smem(3) + vmem(2),
        out_specs=tuple(vmem(3)),
        compiler_params=limits(16),
        cost_estimate=COST,
        name="cut",
    )(lens, dest, offs, rows, notes)


def place_kernel(lens, dest, offs, rows_ref, prev_ref, next_ref, notes_ref, spread_ref, base_ref, pick_ref):
    count, offset, start = local(lens, dest, offs, 0)
    z, y, x, core = coordinates()
    here = z * 2 + y
    ones = jnp.ones((1, 1), jnp.int32)

    def noted(place):
        block = (place >> 1) * 4 + (place & 1) * 2 + x
        note = notes_ref[32:SMALL, lanes(spot(NOTES[0:3], block))].astype(jnp.float32)
        _, lane = grid_of(1, LANE)
        slot = lane - core * (LANE // 2)
        ours = (slot >= 0) & (slot < 3) & (note[3:4].astype(jnp.int32) == here)

        def chosen(row):
            found = jnp.sum(jnp.where(ours, note[row : row + 1], 0.0), axis=-1, keepdims=True)
            return found.astype(jnp.int32)

        return chosen(2), chosen(4) * 2 + chosen(5)

    parts = [(count * ones, offset * ones), noted((here + 7) & 7), noted((here + 1) & 7)]

    def placer(which, width, first):
        mine = parts[which]
        rank = sum((other[1] < mine[1]).astype(jnp.int32) for other in parts)
        step, slot = grid_of(PAD, width)
        source = slot - first
        inside = (source >= 0) & (source < mine[0])
        return hot((step == GAP + mine[1] + GAP * rank + source) & inside)

    from_own = placer(0, rows_ref.shape[0], start)
    from_prev = placer(1, MAXLEN, 0)
    from_next = placer(2, MAXLEN, 0)
    found = take(from_own, rows_ref[...]) + take(from_prev, prev_ref[...]) + take(from_next, next_ref[...])
    spread_ref[...] = found.astype(jnp.bfloat16)
    flat, step = grid_of(RCV_DEV, PAD)
    rank = sum((part[1] <= flat).astype(jnp.int32) for part in parts)
    pick = hot(step == flat + GAP * rank)
    pick_ref[...] = pick
    base_ref[...] = take(pick, spread_ref[...]).astype(jnp.bfloat16)


def place(lens, dest, offs, rows, prev, next_, notes):
    return pl.pallas_call(
        place_kernel,
        out_shape=(shape(PAD, D), shape(RCV_DEV, D), shape(RCV_DEV, PAD)),
        in_specs=smem(3) + vmem(4),
        out_specs=tuple(vmem(3)),
        compiler_params=limits(24),
        cost_estimate=COST,
        name="place",
    )(lens, dest, offs, rows, prev, next_, notes)


def prep_kernel(mine_ref, other_ref, notes_ref, out1, out2, out3, out4, small_ref):
    for block in range(BLOCKS):
        tile = notes_ref[:, lanes(spot(NOTES, block))]
        small_ref[:, block * LANE : (block + 1) * LANE] = tile.astype(jnp.float32)
    for base, rows_ref in ((0, mine_ref), (PAD, other_ref)):

        def one(step, carry):
            values = rows_ref[pl.ds(pl.multiple_of(step * TILE, TILE), TILE), :].astype(jnp.float32)
            center = values - jnp.mean(values, axis=-1, keepdims=True)
            spread = jnp.mean(center * center, axis=-1, keepdims=True)
            scaled = center * lax.rsqrt(spread + epsilon) * small_ref[KERNEL : KERNEL + 1, :]
            scaled = scaled.astype(jnp.bfloat16)
            at = pl.ds(pl.multiple_of(base + step * TILE, TILE), TILE)
            for block in range(BLOCKS):
                part = scaled[:, block * LANE : (block + 1) * LANE]
                for order, out_ref in ((IN1, out1), (IN2, out2), (IN3, out3), (IN4, out4)):
                    place = spot(order, block)
                    out_ref[place >> 3, at, lanes(place & 7)] = part
            return carry

        lax.fori_loop(0, PAD // TILE, one, 0)


def prep(mine, other, notes):
    return pl.pallas_call(
        prep_kernel,
        out_shape=(jax.ShapeDtypeStruct((2, PAIR, HALF), jnp.bfloat16),) * 4 + (shape(SMALL, D, jnp.float32),),
        in_specs=vmem(3),
        out_specs=tuple(vmem(5)),
        compiler_params=limits(28),
        cost_estimate=COST,
        name="prep",
    )(mine, other, notes)


def early_kernel(rows_ref, near_ref, out_ref):
    out_ref[...] = take(rows_ref[0], near_ref[...])


def early(rows, near):
    return pl.pallas_call(
        early_kernel,
        out_shape=shape(PAIR, near.shape[1], jnp.float32),
        in_specs=vmem(2),
        out_specs=vmem(1)[0],
        compiler_params=limits(12),
        cost_estimate=COST,
        name="early",
    )(rows, near)


def conv_kernel(sub, rows_ref, part_ref, far_ref, small_ref, own_ref, other_ref, gated, taps):
    width = own_ref.shape[1]
    tiles = width // LANE
    half = lax.axis_index("core")
    for tile in range(tiles):
        gated[tile, 0:GAP, :] = jnp.zeros((GAP, LANE), jnp.float32)
        gated[tile, GAP + PAIR : 2 * GAP + PAIR, :] = jnp.zeros((GAP, LANE), jnp.float32)
        taps[tile] = small_ref[0:KERNEL, lanes(half * (BLOCKS // 2) + sub + tile)]
    both = part_ref[...] + take(rows_ref[1], far_ref[...])
    mixed = both[:, 0:width] * jax.nn.sigmoid(both[:, width:])
    for tile in range(tiles):
        gated[tile, GAP : GAP + PAIR, :] = mixed[:, tile * LANE : (tile + 1) * LANE]

    def slide(out_ref, base):
        def one(step, carry):
            for tile in range(tiles):
                total = jnp.zeros((SLIDE, LANE), jnp.float32)
                for tap in range(KERNEL):
                    window = gated[tile, pl.ds(base + step * SLIDE + tap, SLIDE), :]
                    total = total + window * taps[tile, tap : tap + 1, :]
                at = pl.ds(pl.multiple_of(step * SLIDE, SLIDE), SLIDE)
                out_ref[at, tile * LANE : (tile + 1) * LANE] = total.astype(jnp.bfloat16)
            return carry

        lax.fori_loop(0, PAD // SLIDE, one, 0)

    slide(own_ref, 0)
    slide(other_ref, PAD)


def conv(sub, rows, part, far, small):
    width = far.shape[1] // 2
    out = shape(PAD, width)
    return pl.pallas_call(
        functools.partial(conv_kernel, sub),
        out_shape=(out, out),
        in_specs=vmem(4),
        out_specs=tuple(vmem(2)),
        scratch_shapes=[
            pltpu.VMEM((width // LANE, PAIR + 2 * GAP, LANE), jnp.float32),
            pltpu.VMEM((width // LANE, KERNEL, LANE), jnp.float32),
        ],
        compiler_params=limits(16),
        cost_estimate=COST,
        name="conv",
    )(rows, part, far, small)


def finish_kernel(
    m0, m1, m2, m3, o0, o1, o2, o3, small_ref, pick_ref, base,
    e8, er, d8, dr, f8, fr, g8, gr, out_hbm, first, second, result, sent,
):
    sources = (e8, er, d8, dr, f8, fr, g8, gr)
    half = lax.axis_index("core")
    pieces = []
    for side, group in ((half, (m0, m1, m2, m3)), (1 - half, (o0, o1, o2, o3))):
        block = side * (BLOCKS // 2)
        for ref in group:
            for tile in range(ref.shape[1] // LANE):
                pieces.append((block, ref[:, tile * LANE : (tile + 1) * LANE].astype(jnp.float32)))
                block = block + 1
    mean = jnp.sum(sum(values for _, values in pieces), axis=-1, keepdims=True) / D
    total = jnp.zeros((PAD, LANE), jnp.float32)
    for _, values in pieces:
        center = values - mean
        total = total + center * center
    scale = lax.rsqrt(jnp.sum(total, axis=-1, keepdims=True) / D + epsilon)
    for place in range(0, BLOCKS, 2):
        parts = []
        for block, values in pieces[place : place + 2]:
            gain = small_ref[KERNEL + 1 : KERNEL + 2, lanes(block)]
            post = (values - mean) * scale * gain
            parts.append((post * jax.nn.sigmoid(post)).astype(jnp.bfloat16))
        kept = take(pick_ref[...], beside(*parts)).astype(jnp.bfloat16)
        for tile, (block, _) in enumerate(pieces[place : place + 2]):
            part = kept[:, tile * LANE : (tile + 1) * LANE]
            first[:, lanes(spot(OUT1, block))] = part
            second[:, lanes(spot(OUT2, block))] = part
    width = HALF // 2
    stores = []
    for turn_index, (side, active, edge) in enumerate(
        ((half, first, 0), (half, second, width), (1 - half, first, 0), (1 - half, second, width))
    ):
        at = pl.ds(pl.multiple_of(side * HALF + edge, width), width)
        near, far = sources[2 * turn_index], sources[2 * turn_index + 1]
        mixed = take(active[:, 0:HALF], near[...]) + take(active[:, HALF:D], far[...]) + base[:, at].astype(jnp.float32)
        result[turn_index] = mixed.astype(jnp.bfloat16)
        stores.append(pltpu.make_async_copy(result.at[turn_index], out_hbm.at[:, at], sent.at[turn_index]))
        stores[-1].start()
    for store in stores:
        store.wait()


def finish(mine, others, small, pick, base, weights):
    return pl.pallas_call(
        finish_kernel,
        out_shape=shape(RCV_DEV, D),
        in_specs=vmem(19),
        out_specs=anywhere(1)[0],
        scratch_shapes=[pltpu.VMEM((RCV_DEV, D), jnp.bfloat16)] * 2
        + [
            pltpu.VMEM((4, RCV_DEV, HALF // 2), jnp.bfloat16),
            pltpu.SemaphoreType.DMA((4,)),
        ],
        compiler_params=limits(28),
        cost_estimate=COST,
        name="finish",
    )(*mine, *others, small, pick, base, *weights)


def hyper_shards(
    frames, lengths, destination, offsets, norm_gain, weight_in, depth_kernel, post_gain, weight_out
):
    low = lax.axis_index("core") == 0
    per = weight_in.shape[0]

    rows = frames[0]
    notes = jnp.concatenate(
        [depth_kernel.T, norm_gain[None], post_gain[None], jnp.zeros((SMALL - KERNEL - 2, per), jnp.bfloat16)], 0
    )
    blank = jnp.zeros_like(notes)
    notes = jnp.where(low, beside(notes, blank), beside(blank, notes))
    up, down, notes = cut(lengths, destination, offsets, rows, notes)
    left = beside(weight_in[:, 0:HALF], weight_in[:, D : D + HALF], weight_out[:, 0:HALF])
    right = beside(weight_in[:, HALF:D], weight_in[:, D + HALF :], weight_out[:, HALF:])
    kept, given = jnp.where(low, left, right), jnp.where(low, right, left)
    got = hop(given, "c")
    chip = jnp.where(low, stack(kept, got), stack(got, kept))
    chip, up, down = tie(chip, up, down)

    notes = notes + hop(notes, "c")

    def span(which):
        if which >= 4:
            return [chip[:, 2 * HALF + (which - 4) * 2 * PART : 2 * HALF + (which - 3) * 2 * PART]]
        return [chip[:, gate + which * PART : gate + (which + 1) * PART] for gate in (0, HALF)]

    def streams(*which):
        return beside(*[piece for one in which for piece in span(one)])

    def wide(notes, name):
        return beside(notes, hop(notes, name))

    size = 2 * PART

    prev, next_ = turn(up, 1), turn(down, -1)
    one, two = streams(0, 5, 2), streams(3, 4, 1)
    one_far, two_far = hop(one, "z1"), hop(two, "z2")
    one, two, notes = tie(stack(one, one_far), stack(two, two_far), wide(notes, NOTES[0]))

    in1_out2, in3, in4_out1, in2 = one[:, 0 : 2 * size], one[:, 2 * size :], two[:, 0 : 2 * size], two[:, 2 * size :]
    far = [hop(in3, "z2"), hop(in4_out1, "x"), hop(in2, "z1")]
    in1_out2, notes, prev, next_ = tie(in1_out2, notes, prev, next_)
    far = [hop(in1_out2, "y")] + far
    in1_out2, in3, in4_out1, in2, notes = tie(
        stack(in1_out2, far[0]), stack(in3, far[1]), stack(in4_out1, far[2]), stack(in2, far[3]), wide(wide(notes, NOTES[1]), NOTES[2])
    )
    spread, base, pick = place(lengths, destination, offsets, rows, prev, next_, notes)

    in1, in4 = in1_out2[:, 0:size], in4_out1[:, 0:size]
    in3_out2, in2_out1 = beside(in3, in1_out2[:, size:]), beside(in2, in4_out1[:, size:])
    far = hop(in1, "z2"), hop(in3_out2, "x"), hop(in2_out1, "y"), hop(in4, "z1")
    in1, in3_out2, in2_out1, in4, notes, spread, base, pick = tie(
        stack(in1, far[0]), stack(in3_out2, far[1]), stack(in2_out1, far[2]), stack(in4, far[3]), wide(notes, NOTES[3]),
        spread, base, pick,
    )

    in2, out1, in3, out2 = in2_out1[:, 0:size], in2_out1[:, size:], in3_out2[:, 0:size], in3_out2[:, size:]
    out1_far, out2_far = hop(out1, "z1"), hop(out2, "z2")
    in1_far, in3_far = hop(in1, "x"), hop(in3, "y")
    n1, n2, n3, n4, small = prep(spread, hop(spread, "c"), notes)
    part1, part2, part3, part4 = early(n1, in1), early(n2, in2), early(n3, in3), early(n4, in4)
    in2, in4, small, part1, part2, part3, part4 = tie(in2, in4, small, part1, part2, part3, part4)
    in2_far, in4_far = hop(in2, "x"), hop(in4, "y")

    def run(normed, which, part, far):
        mine, given_part = conv(which * PART // LANE, normed, part, far, small)
        return mine, hop(given_part, "c")

    m0, o0 = run(n1, 0, part1, in1_far)
    m2, o2 = run(n3, 2, part3, in3_far)
    out1, out2, out1_far, out2_far, in2_far, in4_far, m0, o0, m2, o2 = tie(
        out1, out2, out1_far, out2_far, in2_far, in4_far, m0, o0, m2, o2
    )
    weights = [out1, out1_far, out2, out2_far]
    weights = weights + [hop(array, "c") for array in weights]
    m1, o1 = run(n2, 1, part2, in2_far)
    m3, o3 = run(n4, 3, part4, in4_far)
    mixed = finish((m0, m1, m2, m3), (o0, o1, o2, o3), small, pick, base, weights)
    return mixed[None]


def solution(mesh):
    if dict(mesh.shape) == {"dp": 8, "group": 4}:
        grid = jax.sharding.Mesh(mesh.devices.reshape(4, 2, 2, 2), ("z", "y", "x", "core"))
        dp, group, body = ("z", "y"), ("x", "core"), hyper_shards
    else:
        grid, dp, group, body = mesh, ("dp",), ("group",), shards
    every = dp + group
    placed = (
        P(group, dp, None),
        P(group, dp),
        P(group, dp),
        P(group, dp),
        P(every),
        P(every, None),
        P(every, None),
        P(every),
        P(every, None),
    )
    return jax.shard_map(
        body, mesh=grid, in_specs=placed, out_specs=P(group, dp, None), check_vma=False
    )
```

```python
import functools

import jax
import jax.numpy as jnp
from jax import lax
from jax.experimental import pallas as pl
from jax.experimental.pallas import tpu as pltpu
from jax.sharding import PartitionSpec as P

D = 2048
KERNEL = 32
MAXLEN = 192
RCV_DEV = 384


epsilon = 1e-05


def shifted(array, axis, by):
    peers = lax.axis_size(axis)
    return lax.ppermute(array, axis, [(i, (i + by) % peers) for i in range(peers)])


def layer_norm(values, scale_gain):
    center = values - jnp.mean(values, axis=-1, keepdims=True)
    spread = jnp.mean(center * center, axis=-1, keepdims=True)
    return center * lax.rsqrt(spread + epsilon) * scale_gain.astype(jnp.float32)


def depth_pass(gated_rows, segment, depth_kernel):
    row_count = gated_rows.shape[0]
    margin = KERNEL // 2
    padded = jnp.pad(gated_rows, ((margin, margin), (0, 0)))
    labels = jnp.pad(segment, (margin, margin), constant_values=-1)
    kernel_rows = depth_kernel.astype(jnp.float32)
    depthwise = jnp.zeros_like(gated_rows)
    for column in range(KERNEL):
        inside = (labels[column : column + row_count] == segment)[:, None]
        depthwise = (
            depthwise
            + jnp.where(inside, padded[column : column + row_count], 0.0) * kernel_rows[:, column]
        )
    return depthwise


def conv_module(inputs, segment, params):
    norm_gain, weight_in, depth_kernel, post_gain, weight_out = params
    widths = inputs.shape[1]
    source = inputs.astype(jnp.float32)
    normed = layer_norm(source, norm_gain).astype(jnp.bfloat16)
    projected = jnp.dot(normed, weight_in, preferred_element_type=jnp.float32)
    gated_rows = projected[:, :widths] * jax.nn.sigmoid(projected[:, widths:])
    depthwise = depth_pass(gated_rows, segment, depth_kernel)
    normed_post = layer_norm(depthwise, post_gain)
    active = (normed_post * jax.nn.sigmoid(normed_post)).astype(jnp.bfloat16)
    return (source + jnp.dot(active, weight_out, preferred_element_type=jnp.float32)).astype(
        jnp.bfloat16
    )


def relocate(own_part, next_part, prev_part):
    from_prev = shifted((next_part[0], next_part[1]), "dp", 1)
    from_next = shifted((prev_part[0], prev_part[1]), "dp", -1)
    received = jnp.zeros((RCV_DEV + MAXLEN, D), jnp.bfloat16)
    segment = jnp.zeros((RCV_DEV,), jnp.int32)
    position = jnp.arange(RCV_DEV, dtype=jnp.int32)
    arrivals = (own_part, from_prev, from_next)
    for label_id in range(3):
        frame_rows, meta_data = arrivals[label_id]
        current = lax.dynamic_slice_in_dim(received, meta_data[1], MAXLEN, 0)
        received = lax.dynamic_update_slice_in_dim(received, current + frame_rows, meta_data[1], 0)
        inside = (position >= meta_data[1]) & (position < meta_data[1] + meta_data[0])
        segment = jnp.where(inside, label_id + 1, segment)
    return (received[:RCV_DEV], segment)


def shards(
    frames, lengths, destination, offsets, norm_gain, weight_in, depth_kernel, post_gain, weight_out
):
    dp_count = lax.axis_size("dp")
    params = (
        lax.all_gather(norm_gain, ("dp", "group"), axis=0, tiled=True),
        lax.all_gather(weight_in, ("dp", "group"), axis=0, tiled=True),
        lax.all_gather(depth_kernel, ("dp", "group"), axis=0, tiled=True),
        lax.all_gather(post_gain, ("dp", "group"), axis=0, tiled=True),
        lax.all_gather(weight_out, ("dp", "group"), axis=0, tiled=True),
    )
    my_index = lax.axis_index("dp")
    local_frames = frames[0]
    lengths_here = lengths[0]
    dest_here = destination[0]
    offsets_here = offsets[0]
    starts = jnp.cumsum(lengths_here) - lengths_here
    relative = (dest_here - my_index) % dp_count
    slot_ids = jnp.arange(3, dtype=jnp.int32)

    def pick_entry(values, which):
        return jnp.sum(jnp.where(slot_ids == which, values, 0))

    def slot_of(code):
        return jnp.sum(jnp.where(relative == code, slot_ids, 0))

    chosen = (slot_of(0), slot_of(1), slot_of(dp_count - 1))

    def cut_utterance(source_rows, which):
        start_row = pick_entry(starts, which)
        live_count = pick_entry(lengths_here, which)
        frame_rows = lax.dynamic_slice_in_dim(source_rows, start_row, MAXLEN, 0)
        keep_rows = jnp.arange(MAXLEN, dtype=jnp.int32) < live_count
        kept = jnp.where(keep_rows[:, None], frame_rows, jnp.zeros_like(frame_rows))
        return (kept, jnp.stack([live_count, pick_entry(offsets_here, which)]))

    received, segment = relocate(
        cut_utterance(local_frames, chosen[0]),
        cut_utterance(local_frames, chosen[1]),
        cut_utterance(local_frames, chosen[2]),
    )
    mixed = conv_module(received, segment, params)
    return mixed[None]


SWAP = ((0, 1), (1, 0))
HOPS = {
    "c": ("core", SWAP),
    "x": ("x", SWAP),
    "y": ("y", SWAP),
    "z1": ("z", tuple((i, i ^ 1) for i in range(4))),
    "z2": ("z", tuple((i, i ^ 2) for i in range(4))),
}
GAP = KERNEL // 2
PAD = RCV_DEV + 4 * GAP
PAIR = 2 * PAD
LANE = 128
BLOCKS = D // LANE
HALF = D // 2
PART = 256
IN1, IN2 = ("z1", "y", "z2", "x"), ("z2", "z1", "y", "x")
IN3, IN4 = ("z1", "z2", "x", "y"), ("z2", "x", "z1", "y")
OUT1, OUT2 = ("z2", "x", "y", "z1"), ("z1", "y", "x", "z2")
NOTES = ("z1", "z2", "y", "x")
SMALL = 48
TILE = 64
SLIDE = 224


def hop(array, name):
    axis, pairs = HOPS[name]
    return lax.ppermute(array, axis, pairs)


def turn(array, by):
    return lax.ppermute(array, ("z", "y"), [(i, (i + by) % 8) for i in range(8)])


def stack(first, second):
    return jnp.concatenate([first, second], 0)


def beside(*parts):
    return jnp.concatenate(parts, 1)


def tie(*arrays):
    return list(lax.optimization_barrier(arrays))


def coordinates():
    return [lax.axis_index(name) for name in ("z", "y", "x", "core")]


def spot(order, block):
    z, y, x, _ = coordinates()
    bit = {"z2": (block >> 3) ^ (z >> 1), "z1": ((block >> 2) & 1) ^ (z & 1), "y": ((block >> 1) & 1) ^ y, "x": (block & 1) ^ x}
    return sum(bit[name] << place for place, name in enumerate(order))


def lanes(index):
    return pl.ds(pl.multiple_of(index * LANE, LANE), LANE)


COST = pl.CostEstimate(flops=2**20, bytes_accessed=2**16, transcendentals=0)


def local(lens, dest, offs, code):
    z, y, _, _ = coordinates()
    count, offset, start, before = 0, 0, 0, 0
    for slot in range(3):
        match = (dest[0, slot] - (z * 2 + y) + 8) % 8 == code
        count = jnp.where(match, lens[0, slot], count)
        offset = jnp.where(match, offs[0, slot], offset)
        start = jnp.where(match, before, start)
        before = before + lens[0, slot]
    return count, offset, start


def hot(condition):
    return jnp.where(condition, 1.0, 0.0).astype(jnp.bfloat16)


def take(picker, rows):
    return jnp.dot(picker, rows, preferred_element_type=jnp.float32)


def grid_of(rows, columns):
    shape = (rows, columns)
    return lax.broadcasted_iota(jnp.int32, shape, 0), lax.broadcasted_iota(jnp.int32, shape, 1)


def cut_kernel(lens, dest, offs, rows_ref, notes_ref, up_ref, down_ref, out_ref):
    row, lane = grid_of(SMALL, LANE)
    slot = lane - lax.axis_index("core") * (LANE // 2)
    notes = notes_ref[...].astype(jnp.float32)
    for which in range(3):
        facts = (lens[0, which], dest[0, which], offs[0, which] // 2, offs[0, which] % 2)
        for place, fact in enumerate(facts):
            here = (slot == which) & (row == KERNEL + 2 + place)
            notes = jnp.where(here, fact.astype(jnp.float32), notes)
    out_ref[...] = notes.astype(jnp.bfloat16)
    for code, sent_ref in ((1, up_ref), (7, down_ref)):
        count, _, start = local(lens, dest, offs, code)
        step, slot = grid_of(MAXLEN, rows_ref.shape[0])
        picker = hot((slot == start + step) & (step < count))
        sent_ref[...] = take(picker, rows_ref[...]).astype(jnp.bfloat16)


def smem(count):
    return [pl.BlockSpec(memory_space=pltpu.SMEM)] * count


def vmem(count):
    return [pl.BlockSpec(memory_space=pltpu.VMEM)] * count


def anywhere(count):
    return [pl.BlockSpec(memory_space=pl.ANY)] * count


def shape(rows, columns, dtype=jnp.bfloat16):
    return jax.ShapeDtypeStruct((rows, columns), dtype)


def limits(mebibytes):
    return pltpu.CompilerParams(vmem_limit_bytes=mebibytes * 2**20)


def cut(lens, dest, offs, rows, notes):
    sent = shape(MAXLEN, D)
    return pl.pallas_call(
        cut_kernel,
        out_shape=(sent, sent, shape(SMALL, LANE)),
        in_specs=smem(3) + vmem(2),
        out_specs=tuple(vmem(3)),
        compiler_params=limits(16),
        cost_estimate=COST,
        name="cut",
    )(lens, dest, offs, rows, notes)


def place_kernel(lens, dest, offs, rows_ref, prev_ref, next_ref, notes_ref, spread_ref, base_ref, pick_ref):
    count, offset, start = local(lens, dest, offs, 0)
    z, y, x, core = coordinates()
    here = z * 2 + y
    ones = jnp.ones((1, 1), jnp.int32)

    def noted(place):
        block = (place >> 1) * 4 + (place & 1) * 2 + x
        note = notes_ref[32:SMALL, lanes(spot(NOTES[0:3], block))].astype(jnp.float32)
        _, lane = grid_of(1, LANE)
        slot = lane - core * (LANE // 2)
        ours = (slot >= 0) & (slot < 3) & (note[3:4].astype(jnp.int32) == here)

        def chosen(row):
            found = jnp.sum(jnp.where(ours, note[row : row + 1], 0.0), axis=-1, keepdims=True)
            return found.astype(jnp.int32)

        return chosen(2), chosen(4) * 2 + chosen(5)

    parts = [(count * ones, offset * ones), noted((here + 7) & 7), noted((here + 1) & 7)]

    def placer(which, width, first):
        mine = parts[which]
        rank = sum((other[1] < mine[1]).astype(jnp.int32) for other in parts)
        step, slot = grid_of(PAD, width)
        source = slot - first
        inside = (source >= 0) & (source < mine[0])
        return hot((step == GAP + mine[1] + GAP * rank + source) & inside)

    from_own = placer(0, rows_ref.shape[0], start)
    from_prev = placer(1, MAXLEN, 0)
    from_next = placer(2, MAXLEN, 0)
    found = take(from_own, rows_ref[...]) + take(from_prev, prev_ref[...]) + take(from_next, next_ref[...])
    spread_ref[...] = found.astype(jnp.bfloat16)
    flat, step = grid_of(RCV_DEV, PAD)
    rank = sum((part[1] <= flat).astype(jnp.int32) for part in parts)
    pick = hot(step == flat + GAP * rank)
    pick_ref[...] = pick
    base_ref[...] = take(pick, spread_ref[...]).astype(jnp.bfloat16)


def place(lens, dest, offs, rows, prev, next_, notes):
    return pl.pallas_call(
        place_kernel,
        out_shape=(shape(PAD, D), shape(RCV_DEV, D), shape(RCV_DEV, PAD)),
        in_specs=smem(3) + vmem(4),
        out_specs=tuple(vmem(3)),
        compiler_params=limits(24),
        cost_estimate=COST,
        name="place",
    )(lens, dest, offs, rows, prev, next_, notes)


def prep_kernel(mine_ref, other_ref, notes_ref, out1, out2, out3, out4, small_ref):
    for block in range(BLOCKS):
        tile = notes_ref[:, lanes(spot(NOTES, block))]
        small_ref[:, block * LANE : (block + 1) * LANE] = tile.astype(jnp.float32)
    for base, rows_ref in ((0, mine_ref), (PAD, other_ref)):

        def one(step, carry):
            values = rows_ref[pl.ds(pl.multiple_of(step * TILE, TILE), TILE), :].astype(jnp.float32)
            center = values - jnp.mean(values, axis=-1, keepdims=True)
            spread = jnp.mean(center * center, axis=-1, keepdims=True)
            scaled = center * lax.rsqrt(spread + epsilon) * small_ref[KERNEL : KERNEL + 1, :]
            scaled = scaled.astype(jnp.bfloat16)
            at = pl.ds(pl.multiple_of(base + step * TILE, TILE), TILE)
            for block in range(BLOCKS):
                part = scaled[:, block * LANE : (block + 1) * LANE]
                for order, out_ref in ((IN1, out1), (IN2, out2), (IN3, out3), (IN4, out4)):
                    place = spot(order, block)
                    out_ref[place >> 3, at, lanes(place & 7)] = part
            return carry

        lax.fori_loop(0, PAD // TILE, one, 0)


def prep(mine, other, notes):
    return pl.pallas_call(
        prep_kernel,
        out_shape=(jax.ShapeDtypeStruct((2, PAIR, HALF), jnp.bfloat16),) * 4 + (shape(SMALL, D, jnp.float32),),
        in_specs=vmem(3),
        out_specs=tuple(vmem(5)),
        compiler_params=limits(28),
        cost_estimate=COST,
        name="prep",
    )(mine, other, notes)


def early_kernel(rows_ref, near_ref, out_ref):
    out_ref[...] = take(rows_ref[0], near_ref[...])


def early(rows, near):
    return pl.pallas_call(
        early_kernel,
        out_shape=shape(PAIR, near.shape[1], jnp.float32),
        in_specs=vmem(2),
        out_specs=vmem(1)[0],
        compiler_params=limits(12),
        cost_estimate=COST,
        name="early",
    )(rows, near)


def conv_kernel(sub, rows_ref, part_ref, far_ref, small_ref, own_ref, other_ref, gated, taps):
    width = own_ref.shape[1]
    tiles = width // LANE
    half = lax.axis_index("core")
    for tile in range(tiles):
        gated[tile, 0:GAP, :] = jnp.zeros((GAP, LANE), jnp.float32)
        gated[tile, GAP + PAIR : 2 * GAP + PAIR, :] = jnp.zeros((GAP, LANE), jnp.float32)
        taps[tile] = small_ref[0:KERNEL, lanes(half * (BLOCKS // 2) + sub + tile)]
    both = part_ref[...] + take(rows_ref[1], far_ref[...])
    mixed = both[:, 0:width] * jax.nn.sigmoid(both[:, width:])
    for tile in range(tiles):
        gated[tile, GAP : GAP + PAIR, :] = mixed[:, tile * LANE : (tile + 1) * LANE]

    def slide(out_ref, base):
        def one(step, carry):
            for tile in range(tiles):
                total = jnp.zeros((SLIDE, LANE), jnp.float32)
                for tap in range(KERNEL):
                    window = gated[tile, pl.ds(base + step * SLIDE + tap, SLIDE), :]
                    total = total + window * taps[tile, tap : tap + 1, :]
                at = pl.ds(pl.multiple_of(step * SLIDE, SLIDE), SLIDE)
                out_ref[at, tile * LANE : (tile + 1) * LANE] = total.astype(jnp.bfloat16)
            return carry

        lax.fori_loop(0, PAD // SLIDE, one, 0)

    slide(own_ref, 0)
    slide(other_ref, PAD)


def conv(sub, rows, part, far, small):
    width = far.shape[1] // 2
    out = shape(PAD, width)
    return pl.pallas_call(
        functools.partial(conv_kernel, sub),
        out_shape=(out, out),
        in_specs=vmem(4),
        out_specs=tuple(vmem(2)),
        scratch_shapes=[
            pltpu.VMEM((width // LANE, PAIR + 2 * GAP, LANE), jnp.float32),
            pltpu.VMEM((width // LANE, KERNEL, LANE), jnp.float32),
        ],
        compiler_params=limits(16),
        cost_estimate=COST,
        name="conv",
    )(rows, part, far, small)


def finish_kernel(
    m0, m1, m2, m3, o0, o1, o2, o3, small_ref, pick_ref, base,
    e8, er, d8, dr, f8, fr, g8, gr, out_hbm, first, second, result, sent,
):
    sources = (e8, er, d8, dr, f8, fr, g8, gr)
    half = lax.axis_index("core")
    pieces = []
    for side, group in ((half, (m0, m1, m2, m3)), (1 - half, (o0, o1, o2, o3))):
        block = side * (BLOCKS // 2)
        for ref in group:
            for tile in range(ref.shape[1] // LANE):
                pieces.append((block, ref[:, tile * LANE : (tile + 1) * LANE].astype(jnp.float32)))
                block = block + 1
    mean = jnp.sum(sum(values for _, values in pieces), axis=-1, keepdims=True) / D
    total = jnp.zeros((PAD, LANE), jnp.float32)
    for _, values in pieces:
        center = values - mean
        total = total + center * center
    scale = lax.rsqrt(jnp.sum(total, axis=-1, keepdims=True) / D + epsilon)
    for place in range(0, BLOCKS, 2):
        parts = []
        for block, values in pieces[place : place + 2]:
            gain = small_ref[KERNEL + 1 : KERNEL + 2, lanes(block)]
            post = (values - mean) * scale * gain
            parts.append((post * jax.nn.sigmoid(post)).astype(jnp.bfloat16))
        kept = take(pick_ref[...], beside(*parts)).astype(jnp.bfloat16)
        for tile, (block, _) in enumerate(pieces[place : place + 2]):
            part = kept[:, tile * LANE : (tile + 1) * LANE]
            first[:, lanes(spot(OUT1, block))] = part
            second[:, lanes(spot(OUT2, block))] = part
    width = HALF // 2
    stores = []
    for turn_index, (side, active, edge) in enumerate(
        ((half, first, 0), (half, second, width), (1 - half, first, 0), (1 - half, second, width))
    ):
        at = pl.ds(pl.multiple_of(side * HALF + edge, width), width)
        near, far = sources[2 * turn_index], sources[2 * turn_index + 1]
        mixed = take(active[:, 0:HALF], near[...]) + take(active[:, HALF:D], far[...]) + base[:, at].astype(jnp.float32)
        result[turn_index] = mixed.astype(jnp.bfloat16)
        stores.append(pltpu.make_async_copy(result.at[turn_index], out_hbm.at[:, at], sent.at[turn_index]))
        stores[-1].start()
    for store in stores:
        store.wait()


def finish(mine, others, small, pick, base, weights):
    return pl.pallas_call(
        finish_kernel,
        out_shape=shape(RCV_DEV, D),
        in_specs=vmem(19),
        out_specs=anywhere(1)[0],
        scratch_shapes=[pltpu.VMEM((RCV_DEV, D), jnp.bfloat16)] * 2
        + [
            pltpu.VMEM((4, RCV_DEV, HALF // 2), jnp.bfloat16),
            pltpu.SemaphoreType.DMA((4,)),
        ],
        compiler_params=limits(28),
        cost_estimate=COST,
        name="finish",
    )(*mine, *others, small, pick, base, *weights)


def hyper_shards(
    frames, lengths, destination, offsets, norm_gain, weight_in, depth_kernel, post_gain, weight_out
):
    low = lax.axis_index("core") == 0
    per = weight_in.shape[0]

    rows = frames[0]
    notes = jnp.concatenate(
        [depth_kernel.T, norm_gain[None], post_gain[None], jnp.zeros((SMALL - KERNEL - 2, per), jnp.bfloat16)], 0
    )
    blank = jnp.zeros_like(notes)
    notes = jnp.where(low, beside(notes, blank), beside(blank, notes))
    up, down, notes = cut(lengths, destination, offsets, rows, notes)
    left = beside(weight_in[:, 0:HALF], weight_in[:, D : D + HALF], weight_out[:, 0:HALF])
    right = beside(weight_in[:, HALF:D], weight_in[:, D + HALF :], weight_out[:, HALF:])
    kept, given = jnp.where(low, left, right), jnp.where(low, right, left)
    got = hop(given, "c")
    chip = jnp.where(low, stack(kept, got), stack(got, kept))
    chip, up, down = tie(chip, up, down)

    notes = notes + hop(notes, "c")

    def span(which):
        if which >= 4:
            return [chip[:, 2 * HALF + (which - 4) * 2 * PART : 2 * HALF + (which - 3) * 2 * PART]]
        return [chip[:, gate + which * PART : gate + (which + 1) * PART] for gate in (0, HALF)]

    def streams(*which):
        return beside(*[piece for one in which for piece in span(one)])

    def wide(notes, name):
        return beside(notes, hop(notes, name))

    size = 2 * PART

    prev, next_ = turn(up, 1), turn(down, -1)
    one, two = streams(0, 5, 2), streams(3, 4, 1)
    one_far, two_far = hop(one, "z1"), hop(two, "z2")
    one, two, notes = tie(stack(one, one_far), stack(two, two_far), wide(notes, NOTES[0]))

    in1_out2, in3, in4_out1, in2 = one[:, 0 : 2 * size], one[:, 2 * size :], two[:, 0 : 2 * size], two[:, 2 * size :]
    far = [hop(in3, "z2"), hop(in4_out1, "x"), hop(in2, "z1")]
    in1_out2, notes, prev, next_ = tie(in1_out2, notes, prev, next_)
    far = [hop(in1_out2, "y")] + far
    in1_out2, in3, in4_out1, in2, notes = tie(
        stack(in1_out2, far[0]), stack(in3, far[1]), stack(in4_out1, far[2]), stack(in2, far[3]), wide(wide(notes, NOTES[1]), NOTES[2])
    )
    spread, base, pick = place(lengths, destination, offsets, rows, prev, next_, notes)

    in1, in4 = in1_out2[:, 0:size], in4_out1[:, 0:size]
    in3_out2, in2_out1 = beside(in3, in1_out2[:, size:]), beside(in2, in4_out1[:, size:])
    far = hop(in1, "z2"), hop(in3_out2, "x"), hop(in2_out1, "y"), hop(in4, "z1")
    in1, in3_out2, in2_out1, in4, notes, spread, base, pick = tie(
        stack(in1, far[0]), stack(in3_out2, far[1]), stack(in2_out1, far[2]), stack(in4, far[3]), wide(notes, NOTES[3]),
        spread, base, pick,
    )

    in2, out1, in3, out2 = in2_out1[:, 0:size], in2_out1[:, size:], in3_out2[:, 0:size], in3_out2[:, size:]
    out1_far, out2_far = hop(out1, "z1"), hop(out2, "z2")
    in1_far, in3_far = hop(in1, "x"), hop(in3, "y")
    n1, n2, n3, n4, small = prep(spread, hop(spread, "c"), notes)
    part1, part2, part3, part4 = early(n1, in1), early(n2, in2), early(n3, in3), early(n4, in4)
    in2, in4, small, part1, part2, part3, part4, out1, out2 = tie(
        in2, in4, small, part1, part2, part3, part4, out1, out2
    )
    out1_other, out2_other = hop(out1, "c"), hop(out2, "c")
    in2_far, in4_far = hop(in2, "x"), hop(in4, "y")

    def run(normed, which, part, far):
        mine, given_part = conv(which * PART // LANE, normed, part, far, small)
        return mine, hop(given_part, "c")

    m0, o0 = run(n1, 0, part1, in1_far)
    m2, o2 = run(n3, 2, part3, in3_far)
    out1_other, out2_other, out1_far, out2_far, in2_far, in4_far, m0, o0, m2, o2 = tie(
        out1_other, out2_other, out1_far, out2_far, in2_far, in4_far, m0, o0, m2, o2
    )
    weights = [out1, out1_far, out2, out2_far, out1_other, hop(out1_far, "c"), out2_other, hop(out2_far, "c")]
    m1, o1 = run(n2, 1, part2, in2_far)
    m3, o3 = run(n4, 3, part4, in4_far)
    mixed = finish((m0, m1, m2, m3), (o0, o1, o2, o3), small, pick, base, weights)
    return mixed[None]


def solution(mesh):
    if dict(mesh.shape) == {"dp": 8, "group": 4}:
        grid = jax.sharding.Mesh(mesh.devices.reshape(4, 2, 2, 2), ("z", "y", "x", "core"))
        dp, group, body = ("z", "y"), ("x", "core"), hyper_shards
    else:
        grid, dp, group, body = mesh, ("dp",), ("group",), shards
    every = dp + group
    placed = (
        P(group, dp, None),
        P(group, dp),
        P(group, dp),
        P(group, dp),
        P(every),
        P(every, None),
        P(every, None),
        P(every),
        P(every, None),
    )
    return jax.shard_map(
        body, mesh=grid, in_specs=placed, out_specs=P(group, dp, None), check_vma=False
    )
```
